512 devices in a mesh: row: 8 (over y, core), col: 16 (over z_lo, x), layer: 4 (over z_hi).
Axes of the slice: x: 4, y: 4, z: 16 (z_hi: 4, z_lo: 4; z = z_hi * 4 + z_lo), core: 2. Of those that a mesh axis runs over, the one named last changes fastest.
Arguments:
- panel: bfloat16 [8192, 4, 4096], P('row', 'layer', 'col'), may hold values from -6 to 6
- in_pattern: int32 [64, 4, 32], P('row', 'layer', 'col'), may hold values 0 or 1
- slab: bfloat16 [4, 32, 128, 8192], P('layer', 'row', None, 'col'), may hold values from -0.046875 to 0.046875
- owner: int32 [4, 32], P('layer'), may hold values from 0 to 31, each once within a row
- out_pattern: int32 [64, 64], P(('row', 'layer'), 'col'), may hold values 0 or 1
Outputs:
- product: bfloat16 [8192, 8192], P(('row', 'layer'), 'col')
The draws below stay inside these ranges and needn't reach their ends.
Inputs may be any that keep to these rules, and one draw needn't show every extreme that they name: `owner`: each row lists every number of 0 to 31 once.
All inputs are finite; a program needn't handle non-finite values. No bound on the sum of `in_pattern` or of `out_pattern` on one device may be relied on, other than what follows from the above.
Results may differ from the reference program's by a relative error of at most 0.001.
Values may be sent and summed in bfloat16 or wider, within the bound.
No kernel may reach another device: no remote copies, remote signals or barrier semaphores. Data moves between devices by JAX's collectives and lax.ppermute only.
A program may use at most 64 MiB of HBM per device.

```python
import jax
import jax.numpy as jnp

BS = 128
MB = 64
KL = 32
NB = 64
N_LAYER = 4


def with_ends(drawn, stream_key, least, largest):
    index_at = [jax.random.randint(jax.random.fold_in(stream_key, axis), (), 0, length) for axis, length in enumerate(drawn.shape)]
    main_axis = drawn.shape.index(max(drawn.shape))
    neighbour = index_at[:main_axis] + [(index_at[main_axis] + 1) % drawn.shape[main_axis]] + index_at[main_axis + 1:]
    return drawn.at[tuple(index_at)].set(least).at[tuple(neighbour)].set(largest)


def levels(rng, shape, pieces, low, largest):
    loudness, own = 1.0, jax.random.fold_in(rng, 6)
    for dim, blocks in pieces:
        draws = jnp.exp(jax.random.uniform(jax.random.fold_in(own, dim), (blocks,), jnp.float32, low / len(pieces), largest / len(pieces)))
        loudness = loudness * jnp.repeat(draws, shape[dim] // blocks).reshape([-1 if axis == dim else 1 for axis in range(len(shape))])
    return loudness


def normal_values(rng, shape, scale, reach, cuts=(), kind=jnp.bfloat16):
    level = levels(rng, shape, cuts, -0.22, 0.18) if cuts else 1.0
    array = jax.random.normal(rng, shape, jnp.float32) * scale * level
    return jnp.minimum(jnp.maximum(array, -reach), reach).astype(kind)


def setup_inputs(seed: int = 0) -> dict:
    streams_of = jax.random.split(jax.random.key(seed), 6)
    return {
        "panel": normal_values(streams_of[0], (MB * BS, N_LAYER, KL * BS), 1.0, 6.0, ((0, 8), (1, 4), (2, 16))),
        "in_pattern": with_ends((jax.random.randint(streams_of[1], (MB, N_LAYER, KL), 0, 3) < 2).astype(jnp.int32), jax.random.fold_in(streams_of[1], 1), 0, 1),
        "slab": normal_values(streams_of[2], (N_LAYER, KL, BS, NB * BS), (N_LAYER * KL * BS) ** -0.5, 0.046875, ((0, 4), (1, 8), (3, 16))),
        "owner": jax.vmap(lambda own: jax.random.permutation(own, KL))(jax.random.split(streams_of[3], N_LAYER)).reshape((N_LAYER, KL)).astype(jnp.int32),
        "out_pattern": with_ends((jax.random.randint(streams_of[4], (MB, NB), 0, 4) < 3).astype(jnp.int32), jax.random.fold_in(streams_of[4], 1), 0, 1),
    }


def reference(panel, in_pattern, slab, owner, out_pattern):
    shaped = panel.reshape(MB, BS, N_LAYER, KL, BS)
    keeper = in_pattern.astype(jnp.bfloat16)[:, None, :, :, None]
    masked = (shaped * keeper).reshape(MB * BS, N_LAYER, KL * BS)
    running = jnp.zeros((MB * BS, NB * BS), jnp.float32)
    for layer_index in range(N_LAYER):
        picked = jnp.take(slab[layer_index], owner[layer_index].astype(jnp.int32), axis=0)
        picked = picked.reshape(KL * BS, NB * BS)
        running = running + jnp.dot(masked[:, layer_index, :], picked, preferred_element_type=jnp.float32)
    blocked = running.reshape(MB, BS, NB, BS) * out_pattern.astype(jnp.float32)[:, None, :, None]
    return blocked.reshape(MB * BS, NB * BS).astype(jnp.bfloat16)
```

```python
import itertools

import jax
import jax.numpy as jnp
from jax import lax
from jax.experimental import pallas as pl
from jax.experimental.pallas import tpu as pltpu
from jax.sharding import PartitionSpec as P

AXES = ("row", "col", "layer")
BS = 128
LEVELS = 32700.0
TINY = 1e-33
STEPS = 8.0
PAD = 16


def moves(f):
    pairs = []
    for y, c, zl, x, zh in itertools.product(range(4), range(2), range(4), range(4), range(4)):
        y2, c2, zl2, x2 = f(y, c, zl, x)
        pairs.append((((y * 2 + c) * 16 + zl * 4 + x) * 4 + zh, ((y2 * 2 + c2) * 16 + zl2 * 4 + x2) * 4 + zh))
    return pairs


def send(v, f):
    return lax.ppermute(v, AXES, moves(f))


def mask_kernel(pat_ref, x_ref, o_ref):
    for b in range(x_ref.shape[0] // BS):
        for j in range(x_ref.shape[1] // BS):
            keep = pat_ref[b, j].astype(jnp.float32).astype(jnp.bfloat16)
            at = (pl.ds(b * BS, BS), pl.ds(j * BS, BS))
            o_ref[at] = x_ref[at] * keep


def mask(panel, pattern):
    return pl.pallas_call(
        mask_kernel,
        out_shape=jax.ShapeDtypeStruct(panel.shape, panel.dtype),
        in_specs=[pl.BlockSpec(memory_space=pltpu.SMEM), pl.BlockSpec(memory_space=pltpu.VMEM)],
        out_specs=pl.BlockSpec(memory_space=pltpu.VMEM),
        name="mask",
    )(pattern, panel)


def mm_kernel(owner_ref, pos_ref, a_ref, mine_ref, other_ref, o_ref, a_s, b_s, acc, sem_a, sem_b):
    rows = a_s.shape[0]
    pieces = a_ref.shape[0]
    kw = a_ref.shape[2]
    y, c = pos_ref[0], pos_ref[1]

    def copy_a(s):
        return pltpu.make_async_copy(a_ref.at[s], a_s.at[:, pl.ds(s * kw, kw)], sem_a.at[s])

    def dst_b(j):
        return b_s.at[pl.ds(j * BS, BS), :]

    for s in range(pieces):
        copy_a(s).start()
        for j in (2 * s, 2 * s + 1):
            n = owner_ref[j]
            row, i = n // 4, n % 4
            rel = (row // 2 + 4 - y) % 4
            same = (row % 2) == c

            @pl.when(same)
            def _():
                pltpu.make_async_copy(mine_ref.at[rel, i], dst_b(j), sem_b.at[j]).start()

            @pl.when(jnp.logical_not(same))
            def _():
                pltpu.make_async_copy(other_ref.at[rel, i], dst_b(j), sem_b.at[j]).start()

    tile = 256
    for k in range(pieces // 2):
        for s in (2 * k, 2 * k + 1):
            copy_a(s).wait()
            for j in (2 * s, 2 * s + 1):
                pltpu.make_async_copy(mine_ref.at[0, 0], dst_b(j), sem_b.at[j]).wait()

        @pl.loop(0, rows // tile)
        def _(t):
            at = pl.ds(pl.multiple_of(t * tile, tile), tile)
            part = jnp.dot(a_s[at, pl.ds(k * 2 * kw, 2 * kw)], b_s[pl.ds(k * 2 * kw, 2 * kw), :], preferred_element_type=jnp.float32)
            if k == 0:
                acc[at, :] = part
            else:
                acc[at, :] += part

    chunk = rows // 4
    for l in range(4):
        x = acc[pl.ds(l * chunk, chunk), :]
        top = jnp.max(jnp.abs(x), axis=0, keepdims=True)
        code = jnp.ceil(jnp.log2(jnp.maximum(top, TINY)) * STEPS)
        q = jnp.round(x * (jnp.exp2(code * (-1.0 / STEPS)) * LEVELS)).astype(jnp.int32)
        o_ref[l, pl.ds(0, chunk), :] = q.astype(jnp.int16)
        o_ref[l, pl.ds(chunk, PAD), :] = jnp.broadcast_to(code.astype(jnp.int32), (PAD, x.shape[1])).astype(jnp.int16)


def matmul(owner, pos, a, mine, other):
    pieces, rows, kw = a.shape
    cols = mine.shape[3]
    return pl.pallas_call(
        mm_kernel,
        out_shape=jax.ShapeDtypeStruct((4, rows // 4 + PAD, cols), jnp.int16),
        in_specs=[pl.BlockSpec(memory_space=pltpu.SMEM)] * 2 + [pl.BlockSpec(memory_space=pl.ANY)] * 3,
        out_specs=pl.BlockSpec(memory_space=pltpu.VMEM),
        scratch_shapes=[
            pltpu.VMEM((rows, pieces * kw), jnp.bfloat16),
            pltpu.VMEM((pieces * kw, cols), jnp.bfloat16),
            pltpu.VMEM((rows, cols), jnp.float32),
            pltpu.SemaphoreType.DMA((pieces,)),
            pltpu.SemaphoreType.DMA((2 * pieces,)),
        ],
        compiler_params=pltpu.CompilerParams(vmem_limit_bytes=40 << 20),
        cost_estimate=pl.CostEstimate(flops=2 * rows * cols * pieces * kw, bytes_accessed=14 << 20, transcendentals=0),
        name="matmul",
    )(owner, pos, a, mine, other)


def total_kernel(pat_ref, q_ref, o_ref):
    rows, cols = o_ref.shape
    total = jnp.zeros((rows, cols), jnp.float32)
    for l in range(4):
        code = q_ref[l, pl.ds(rows, PAD), :].astype(jnp.int32)[0:1, :].astype(jnp.float32)
        total = total + q_ref[l, pl.ds(0, rows), :].astype(jnp.int32).astype(jnp.float32) * (jnp.exp2(code * (1.0 / STEPS)) * (1.0 / LEVELS))
    for b in range(rows // BS):
        for n in range(cols // BS):
            keep = pat_ref[b, n].astype(jnp.float32)
            o_ref[pl.ds(b * BS, BS), pl.ds(n * BS, BS)] = (total[b * BS:(b + 1) * BS, n * BS:(n + 1) * BS] * keep).astype(jnp.bfloat16)


def total(pattern, q):
    _, rows, cols = q.shape
    return pl.pallas_call(
        total_kernel,
        out_shape=jax.ShapeDtypeStruct((rows - PAD, cols), jnp.bfloat16),
        in_specs=[pl.BlockSpec(memory_space=pltpu.SMEM), pl.BlockSpec(memory_space=pltpu.VMEM)],
        out_specs=pl.BlockSpec(memory_space=pltpu.VMEM),
        compiler_params=pltpu.CompilerParams(vmem_limit_bytes=16 << 20),
        name="total",
    )(pattern, q)


def shards(panel, in_pattern, slab, owner, out_pattern):
    row = lax.axis_index("row")
    pos = jnp.stack([row // 2, row % 2])
    own = slab[0]
    with jax.named_scope("slab_ring"):
        below = send(own, lambda y, c, zl, x: ((y + 1) % 4, c, zl, x))
        above = send(own, lambda y, c, zl, x: ((y + 3) % 4, c, zl, x))
        far = send(own, lambda y, c, zl, x: ((y + 2) % 4, c, zl, x))
        mine = jnp.stack([own, above, far, below])
        other = send(mine, lambda y, c, zl, x: (y, 1 - c, zl, x))
    masked = mask(panel[:, 0, :], in_pattern[:, 0, :])
    gathered = lax.all_gather(masked, "col", axis=0, tiled=False)
    q = matmul(owner[0], pos, gathered, mine, other)
    q = lax.all_to_all(q, "layer", 0, 0, tiled=True)
    return total(out_pattern, q)


def solution(mesh):
    in_specs = (
        P("row", "layer", "col"),
        P("row", "layer", "col"),
        P("layer", "row", None, "col"),
        P("layer", None),
        P(("row", "layer"), "col"),
    )
    out_specs = P(("row", "layer"), "col")
    return jax.shard_map(shards, mesh=mesh, in_specs=in_specs, out_specs=out_specs, check_vma=False)
```

```python
import itertools

import jax
import jax.numpy as jnp
from jax import lax
from jax.experimental import pallas as pl
from jax.experimental.pallas import tpu as pltpu
from jax.sharding import PartitionSpec as P

AXES = ("row", "col", "layer")
BS = 128
LEVELS = 32700.0
TINY = 1e-33
STEPS = 8.0
PAD = 16


def moves(f):
    pairs = []
    for y, c, zl, x, zh in itertools.product(range(4), range(2), range(4), range(4), range(4)):
        y2, c2, zl2, x2 = f(y, c, zl, x)
        pairs.append((((y * 2 + c) * 16 + zl * 4 + x) * 4 + zh, ((y2 * 2 + c2) * 16 + zl2 * 4 + x2) * 4 + zh))
    return pairs


def send(v, f):
    return lax.ppermute(v, AXES, moves(f))


def mask_kernel(pos_ref, pat_ref, x_ref, first_ref, second_ref):
    q = pos_ref[3]
    for h, o_ref in ((q, first_ref), (1 - q, second_ref)):
        for b in range(o_ref.shape[0] // BS):
            for j in range(x_ref.shape[1] // BS):
                block = 2 * b + h
                keep = pat_ref[block, j].astype(jnp.float32).astype(jnp.bfloat16)
                cols = pl.ds(j * BS, BS)
                o_ref[pl.ds(b * BS, BS), cols] = x_ref[pl.ds(pl.multiple_of(block * BS, BS), BS), cols] * keep


def mask(pos, panel, pattern):
    rows, width = panel.shape
    return pl.pallas_call(
        mask_kernel,
        out_shape=[jax.ShapeDtypeStruct((rows // 2, width), panel.dtype)] * 2,
        in_specs=[pl.BlockSpec(memory_space=pltpu.SMEM)] * 2 + [pl.BlockSpec(memory_space=pltpu.VMEM)],
        out_specs=[pl.BlockSpec(memory_space=pltpu.VMEM)] * 2,
        name="mask",
    )(pos, pattern, panel)


def mm_kernel(pos_ref, owner_ref, *refs):
    a_refs, mine, other = refs[:8], refs[8:12], refs[12:16]
    o_ref, place, a_s, b_s, acc, sem_a, sem_b = refs[16:]
    rows = a_s.shape[0]
    y, c, p, x = pos_ref[0], pos_ref[1], pos_ref[2], pos_ref[4]
    kw = 2 * BS

    def col(piece, i):
        batch, rel = piece // 4, piece % 4
        half = (p + batch) % 2
        return (2 * half + (c + i) % 2) * 4 + (x + rel) % 4

    def copy_a(piece, i):
        s = 2 * piece + i
        return pltpu.make_async_copy(a_refs[piece].at[i], a_s.at[:, pl.ds(s * kw, kw)], sem_a.at[s])

    for piece in range(8):
        for i in range(2):
            copy_a(piece, i).start()
            for u in range(2):
                place[owner_ref[2 * col(piece, i) + u]] = 2 * (2 * piece + i) + u

    def copy_b(ref, i, at):
        return pltpu.make_async_copy(ref.at[:, i], b_s.at[:, pl.ds(pl.multiple_of(at * BS, BS), BS), :], sem_b.at[at])

    for rel in range(4):
        for k, group in enumerate((mine, other)):
            for i in range(4):
                block = (((y + rel) % 4) * 2 + (c + k) % 2) * 4 + i
                copy_b(group[rel], i, place[block]).start()

    tile = 256
    for k in range(8):
        for i in range(2):
            copy_a(k, i).wait()
            for u in range(2):
                copy_b(mine[0], 0, 4 * k + 2 * i + u).wait()

        @pl.loop(0, rows // tile)
        def _(t):
            at = pl.ds(pl.multiple_of(t * tile, tile), tile)
            for g in range(2):
                part = jnp.dot(a_s[at, pl.ds(k * 2 * kw, 2 * kw)], b_s[g, pl.ds(k * 2 * kw, 2 * kw), :], preferred_element_type=jnp.float32)
                if k == 0:
                    acc[g, at, :] = part
                else:
                    acc[g, at, :] += part

    for l in range(4):
        codes = []
        for t in range(8):
            v = acc[t // 4, pl.ds(l * BS, BS), pl.ds((t % 4) * BS, BS)]
            top = jnp.max(jnp.abs(v), axis=0, keepdims=True)
            code = jnp.ceil(jnp.log2(jnp.maximum(top, TINY)) * STEPS)
            codes.append(code)
            v = jnp.round(v * (jnp.exp2(code * (-1.0 / STEPS)) * LEVELS)).astype(jnp.int32)
            o_ref[l, pl.ds(t * BS, BS), :] = v.astype(jnp.int16)
        codes = jnp.concatenate(codes + codes, axis=0)
        o_ref[l, pl.ds(8 * BS, PAD), :] = codes.astype(jnp.int32).astype(jnp.int16)


def matmul(pos, owner, a, mine, other):
    _, rows, kw = a[0].shape
    cols = mine[0].shape[3]
    depth = 16 * kw
    return pl.pallas_call(
        mm_kernel,
        out_shape=jax.ShapeDtypeStruct((4, 8 * BS + PAD, BS), jnp.int16),
        in_specs=[pl.BlockSpec(memory_space=pltpu.SMEM)] * 2 + [pl.BlockSpec(memory_space=pl.ANY)] * 16,
        out_specs=pl.BlockSpec(memory_space=pltpu.VMEM),
        scratch_shapes=[
            pltpu.SMEM((32,), jnp.int32),
            pltpu.VMEM((rows, depth), jnp.bfloat16),
            pltpu.VMEM((2, depth, cols), jnp.bfloat16),
            pltpu.VMEM((2, rows, cols), jnp.float32),
            pltpu.SemaphoreType.DMA((16,)),
            pltpu.SemaphoreType.DMA((32,)),
        ],
        compiler_params=pltpu.CompilerParams(vmem_limit_bytes=32 << 20),
        cost_estimate=pl.CostEstimate(flops=4 * rows * cols * depth, bytes_accessed=14 << 20, transcendentals=0),
        name="matmul",
    )(pos, owner, *a, *mine, *other)


def total_kernel(pos_ref, v_ref, first_ref, second_ref):
    other = (pos_ref[1] + pos_ref[3]) % 2
    for g, o_ref in ((other, first_ref), (1 - other, second_ref)):
        for n in range(4):
            t = g * 4 + n
            at = pl.ds(pl.multiple_of(t * BS, BS), BS)
            total = jnp.zeros((BS, BS), jnp.float32)
            for l in range(4):
                codes = v_ref[l, pl.ds(8 * BS, PAD), :].astype(jnp.int32).astype(jnp.float32)
                code = jnp.where(g == 0, codes[n:n + 1, :], codes[4 + n:5 + n, :])
                total = total + v_ref[l, at, :].astype(jnp.int32).astype(jnp.float32) * (jnp.exp2(code * (1.0 / STEPS)) * (1.0 / LEVELS))
            o_ref[:, pl.ds(n * BS, BS)] = total.astype(jnp.bfloat16)


def total(pos, v):
    return pl.pallas_call(
        total_kernel,
        out_shape=[jax.ShapeDtypeStruct((BS, 4 * BS), jnp.bfloat16)] * 2,
        in_specs=[pl.BlockSpec(memory_space=pltpu.SMEM), pl.BlockSpec(memory_space=pltpu.VMEM)],
        out_specs=[pl.BlockSpec(memory_space=pltpu.VMEM)] * 2,
        name="total",
    )(pos, v)


def place_kernel(pos_ref, pat_ref, first_ref, second_ref, o_ref):
    q = pos_ref[3]
    for b, ref in ((q, first_ref), (1 - q, second_ref)):
        for n in range(4):
            keep = pat_ref[b, n].astype(jnp.float32).astype(jnp.bfloat16)
            cols = pl.ds(n * BS, BS)
            o_ref[pl.ds(pl.multiple_of(b * BS, BS), BS), cols] = ref[:, cols] * keep


def place(pos, pattern, first, second):
    return pl.pallas_call(
        place_kernel,
        out_shape=jax.ShapeDtypeStruct((2 * BS, 4 * BS), jnp.bfloat16),
        in_specs=[pl.BlockSpec(memory_space=pltpu.SMEM)] * 2 + [pl.BlockSpec(memory_space=pltpu.VMEM)] * 2,
        out_specs=pl.BlockSpec(memory_space=pltpu.VMEM),
        name="place",
    )(pos, pattern, first, second)


def shards(panel, in_pattern, slab, owner, out_pattern):
    row, col = lax.axis_index("row"), lax.axis_index("col")
    zl = col // 4
    pos = jnp.stack([row // 2, row % 2, zl // 2, zl % 2, col % 4])
    first, second = mask(pos, panel[:, 0, :], in_pattern[:, 0, :])
    with jax.named_scope("panel_pair"):
        first = send(first, lambda y, c, zl, x: (y, zl % 2, zl - zl % 2 + c, x))
        second = send(second, lambda y, c, zl, x: (y, 1 - zl % 2, zl - zl % 2 + c, x))
        near = jnp.stack([first, second])
    with jax.named_scope("slab_pair"):
        own = slab[0]
        pair = send(own, lambda y, c, zl, x: (y, c, zl ^ 1, x))
        own = jnp.stack([own, pair])
    with jax.named_scope("panel_far"):
        beyond = send(near, lambda y, c, zl, x: (y, c, zl ^ 2, x))

    def ring_x(v):
        return [v] + [send(v, lambda y, c, zl, x, d=d: (y, c, zl, (x - d) % 4)) for d in (1, 2, 3)]

    with jax.named_scope("panel_near_ring"):
        a = ring_x(near)
    with jax.named_scope("slab_ring"):
        mine = [own] + [send(own, lambda y, c, zl, x, d=d: ((y - d) % 4, c, zl, x)) for d in (1, 2, 3)]
        other = [send(v, lambda y, c, zl, x: (y, 1 - c, zl, x)) for v in mine]
    with jax.named_scope("panel_far_ring"):
        a = a + ring_x(beyond)
    v = matmul(pos, owner[0], a, mine, other)
    v = lax.all_to_all(v, "layer", 0, 0, tiled=True)
    first, second = total(pos, v)
    with jax.named_scope("product_pair"):
        first = send(first, lambda y, c, zl, x: (y, zl % 2, zl - zl % 2 + c, x))
        second = send(second, lambda y, c, zl, x: (y, zl % 2, zl - zl % 2 + 1 - c, x))
    return place(pos, out_pattern, first, second)


def solution(mesh):
    in_specs = (
        P("row", "layer", "col"),
        P("row", "layer", "col"),
        P("layer", "row", None, "col"),
        P("layer", None),
        P(("row", "layer"), "col"),
    )
    out_specs = P(("row", "layer"), "col")
    return jax.shard_map(shards, mesh=mesh, in_specs=in_specs, out_specs=out_specs, check_vma=False)
```

```python
import itertools

import jax
import jax.numpy as jnp
from jax import lax
from jax.experimental import pallas as pl
from jax.experimental.pallas import tpu as pltpu
from jax.sharding import PartitionSpec as P

AXES = ("row", "col", "layer")
BS = 128
LEVELS = 32700.0
TINY = 1e-33
STEPS = 8.0
PAD = 16


def moves(f):
    pairs = []
    for y, c, zl, x, zh in itertools.product(range(4), range(2), range(4), range(4), range(4)):
        y2, c2, zl2, x2, zh2 = f(y, c, zl, x, zh)
        pairs.append((((y * 2 + c) * 16 + zl * 4 + x) * 4 + zh, ((y2 * 2 + c2) * 16 + zl2 * 4 + x2) * 4 + zh2))
    return pairs


def send(v, f):
    return lax.ppermute(v, AXES, moves(f))


def to_x(v, d):
    return send(v, lambda y, c, zl, x, zh: (y, c, zl, (x + d) % 4, zh))


def to_y(v, d):
    return send(v, lambda y, c, zl, x, zh: ((y + d) % 4, c, zl, x, zh))


def to_layer(v, d):
    return send(v, lambda y, c, zl, x, zh: (y, c, zl, x, (zh + d) % 4))


def to_core(v):
    return send(v, lambda y, c, zl, x, zh: (y, 1 - c, zl, x, zh))


def mask_kernel(pos_ref, pat_ref, x_ref, first_ref, second_ref):
    q = pos_ref[3]
    for h, o_ref in ((q, first_ref), (1 - q, second_ref)):
        for b in range(o_ref.shape[0] // BS):
            for j in range(x_ref.shape[1] // BS):
                block = 2 * b + h
                keep = pat_ref[j, block].astype(jnp.float32).astype(jnp.bfloat16)
                cols = pl.ds(j * BS, BS)
                o_ref[pl.ds(b * BS, BS), cols] = x_ref[pl.ds(pl.multiple_of(block * BS, BS), BS), cols] * keep


def mask(pos, panel, pattern):
    rows, width = panel.shape
    return pl.pallas_call(
        mask_kernel,
        out_shape=[jax.ShapeDtypeStruct((rows // 2, width), panel.dtype)] * 2,
        in_specs=[pl.BlockSpec(memory_space=pltpu.SMEM)] * 2 + [pl.BlockSpec(memory_space=pltpu.VMEM)],
        out_specs=[pl.BlockSpec(memory_space=pltpu.VMEM)] * 2,
        name="mask",
    )(pos, pattern, panel)


PANEL = (
    ((0, 0, 0), (0, 0, 1)),
    ((0, 3, 0), (0, 3, 1)),
    ((0, 1, 0), (0, 1, 1)),
    ((1, 0, 0), (1, 0, 1)),
    ((0, 2, 0), (1, 3, 0), (1, 3, 1)),
    ((0, 2, 1), (1, 1, 0), (1, 1, 1)),
    ((1, 2, 0),),
    ((1, 2, 1),),
)
R0 = tuple((0, g, i) for g in range(2) for i in range(4))
R1P = tuple((3, 0, i) for i in range(4))
R1M = tuple((1, 0, i) for i in range(4))
R2P = ((2, 0, 0), (2, 0, 1)) + tuple((3, 1, i) for i in range(4))
R2M = ((2, 0, 2), (2, 0, 3)) + tuple((1, 1, i) for i in range(4))
R3P = ((2, 1, 0), (2, 1, 1))
R3M = ((2, 1, 2), (2, 1, 3))
SLAB = (
    (0, R0[:4]),
    (0, R0[4:]),
    (0, R1P),
    (0, R1M),
    (0, R2P),
    (0, R2M),
    (0, R3P),
    (0, R3M),
    (1, R0),
    (1, R1P + R1M + R2P + R2M),
    (1, R3P + R3M),
)
NA, NB = len(PANEL), len(SLAB)


def quantize(v):
    top = jnp.max(jnp.abs(v), axis=0, keepdims=True)
    code = jnp.ceil(jnp.log2(jnp.maximum(top, TINY)) * STEPS)
    v = jnp.round(v * (jnp.exp2(code * (-1.0 / STEPS)) * LEVELS)).astype(jnp.int32)
    return v.astype(jnp.int16), code


def mm_kernel(pos_ref, owner_ref, *refs):
    a_refs, b_refs = refs[:NA], refs[NA:NA + NB]
    own_ref, *o_refs = refs[NA + NB:NA + NB + 4]
    place, a_s, b_s, acc, sem_a, sem_b = refs[NA + NB + 4:]
    rows = a_s.shape[0]
    y, c, p, x, layer = pos_ref[0], pos_ref[1], pos_ref[2], pos_ref[4], pos_ref[5]
    kw = 2 * BS
    pieces = [(n, at) + piece for n, group in enumerate(PANEL) for at, piece in enumerate(group)]

    def copy_a(s):
        n, at = pieces[s][:2]
        return pltpu.make_async_copy(a_refs[n].at[at], a_s.at[:, pl.ds(s * kw, kw)], sem_a.at[s])

    for s, (_, _, batch, rel, i) in enumerate(pieces):
        copy_a(s).start()
        col = (2 * ((p + batch) % 2) + (c + i) % 2) * 4 + (x + rel) % 4
        for u in range(2):
            place[owner_ref[2 * col + u]] = 2 * s + u

    def copy_b(ref, i, g, at):
        return pltpu.make_async_copy(ref.at[i], b_s.at[g, pl.ds(pl.multiple_of(at * BS, BS), BS), :], sem_b.at[g, at])

    for ref, (k, blocks) in zip(b_refs, SLAB):
        for n, (rel, g, i) in enumerate(blocks):
            block = (((y + rel) % 4) * 2 + (c + k) % 2) * 4 + i
            copy_b(ref, n, g, place[block]).start()

    tile = 256
    for k in range(8):
        for s in (2 * k, 2 * k + 1):
            copy_a(s).wait()
            for at in (2 * s, 2 * s + 1):
                for g in range(2):
                    copy_b(b_refs[0], 0, g, at).wait()

        @pl.loop(0, rows // tile)
        def _(t):
            at = pl.ds(pl.multiple_of(t * tile, tile), tile)
            for g in range(2):
                part = jnp.dot(a_s[at, pl.ds(k * 2 * kw, 2 * kw)], b_s[g, pl.ds(k * 2 * kw, 2 * kw), :], preferred_element_type=jnp.float32)
                if k == 0:
                    acc[g, at, :] = part
                else:
                    acc[g, at, :] += part

    def chunk(rel, t):
        at = pl.ds(pl.multiple_of(((layer + rel) % 4) * BS, BS), BS)
        return acc[t // 4, at, pl.ds((t % 4) * BS, BS)]

    for rel, o_ref in zip((1, 2, 3), o_refs):
        codes = []
        for t in range(8):
            v, code = quantize(chunk(rel, t))
            o_ref[pl.ds(t * BS, BS), :] = v
            codes.append(code)
        codes = jnp.concatenate(codes + codes, axis=0)
        o_ref[pl.ds(8 * BS, PAD), :] = codes.astype(jnp.int32).astype(jnp.int16)
    for t in range(8):
        own_ref[pl.ds(t * BS, BS), :] = chunk(0, t)


def matmul(pos, owner, a, b):
    _, rows, kw = a[0].shape
    cols = b[0].shape[2]
    depth = 16 * kw
    return pl.pallas_call(
        mm_kernel,
        out_shape=[jax.ShapeDtypeStruct((8 * BS, BS), jnp.float32)] + [jax.ShapeDtypeStruct((8 * BS + PAD, BS), jnp.int16)] * 3,
        in_specs=[pl.BlockSpec(memory_space=pltpu.SMEM)] * 2 + [pl.BlockSpec(memory_space=pl.ANY)] * (NA + NB),
        out_specs=[pl.BlockSpec(memory_space=pltpu.VMEM)] * 4,
        scratch_shapes=[
            pltpu.SMEM((32,), jnp.int32),
            pltpu.VMEM((rows, depth), jnp.bfloat16),
            pltpu.VMEM((2, depth, cols), jnp.bfloat16),
            pltpu.VMEM((2, rows, cols), jnp.float32),
            pltpu.SemaphoreType.DMA((16,)),
            pltpu.SemaphoreType.DMA((2, 32)),
        ],
        compiler_params=pltpu.CompilerParams(vmem_limit_bytes=32 << 20),
        cost_estimate=pl.CostEstimate(flops=4 * rows * cols * depth, bytes_accessed=14 << 20, transcendentals=0),
        name="matmul",
    )(pos, owner, *a, *b)


def total_kernel(pos_ref, own_ref, *refs):
    v_refs, o_refs = refs[:3], refs[3:]
    other = (pos_ref[1] + pos_ref[3]) % 2
    for g, o_ref in zip((other, 1 - other), o_refs):
        for n in range(4):
            at = pl.ds(pl.multiple_of((g * 4 + n) * BS, BS), BS)
            total = own_ref[at, :]
            for v_ref in v_refs:
                codes = v_ref[pl.ds(8 * BS, PAD), :].astype(jnp.int32).astype(jnp.float32)
                code = jnp.where(g == 0, codes[n:n + 1, :], codes[4 + n:5 + n, :])
                total = total + v_ref[at, :].astype(jnp.int32).astype(jnp.float32) * (jnp.exp2(code * (1.0 / STEPS)) * (1.0 / LEVELS))
            o_ref[:, pl.ds(n * BS, BS)] = total.astype(jnp.bfloat16)


def total(pos, own, v):
    return pl.pallas_call(
        total_kernel,
        out_shape=[jax.ShapeDtypeStruct((BS, 4 * BS), jnp.bfloat16)] * 2,
        in_specs=[pl.BlockSpec(memory_space=pltpu.SMEM)] + [pl.BlockSpec(memory_space=pltpu.VMEM)] * 4,
        out_specs=[pl.BlockSpec(memory_space=pltpu.VMEM)] * 2,
        name="total",
    )(pos, own, *v)


def place_kernel(pos_ref, pat_ref, first_ref, second_ref, o_ref):
    q = pos_ref[3]
    for b, ref in ((q, first_ref), (1 - q, second_ref)):
        for n in range(4):
            keep = pat_ref[b, n].astype(jnp.float32).astype(jnp.bfloat16)
            cols = pl.ds(n * BS, BS)
            o_ref[pl.ds(pl.multiple_of(b * BS, BS), BS), cols] = ref[:, cols] * keep


def place(pos, pattern, first, second):
    return pl.pallas_call(
        place_kernel,
        out_shape=jax.ShapeDtypeStruct((2 * BS, 4 * BS), jnp.bfloat16),
        in_specs=[pl.BlockSpec(memory_space=pltpu.SMEM)] * 2 + [pl.BlockSpec(memory_space=pltpu.VMEM)] * 2,
        out_specs=pl.BlockSpec(memory_space=pltpu.VMEM),
        name="place",
    )(pos, pattern, first, second)


def shards(panel, in_pattern, slab, owner, out_pattern):
    row, col = lax.axis_index("row"), lax.axis_index("col")
    zl = col // 4
    pos = jnp.stack([row // 2, row % 2, zl // 2, zl % 2, col % 4, lax.axis_index("layer")])
    cat = lambda *v: jnp.concatenate(v, axis=0)
    own = slab[0]
    first, second = mask(pos, panel[:, 0, :], in_pattern[:, 0, :].T)
    with jax.named_scope("round0"):
        first = send(first, lambda y, c, zl, x, zh: (y, zl % 2, zl - zl % 2 + c, x, zh))
        second = send(second, lambda y, c, zl, x, zh: (y, 1 - zl % 2, zl - zl % 2 + c, x, zh))
        pair = send(own, lambda y, c, zl, x, zh: (y, c, zl ^ 1, x, zh))
        b1p, b1m = to_y(own, 1), to_y(own, -1)
        first, second, pair, b1p, b1m = lax.optimization_barrier((first, second, pair, b1p, b1m))
        near = jnp.stack([first, second])
    with jax.named_scope("round1"):
        far = send(near, lambda y, c, zl, x, zh: (y, c, zl ^ 2, x, zh))
        a1p, a1m = to_x(near, 1), to_x(near, -1)
        b2p, b2m = to_y(cat(b1p[:2], pair), 1), to_y(cat(b1m[2:], pair), -1)
        far, a1p, a1m, b2p, b2m = lax.optimization_barrier((far, a1p, a1m, b2p, b2m))
    with jax.named_scope("round2"):
        a2p, a2m = to_x(cat(a1p[:1], far), 1), to_x(cat(a1m[1:], far), -1)
        b3p, b3m = to_y(b2p[2:4], 1), to_y(b2m[4:], -1)
        c12 = to_core(cat(b1p, b1m, b2p, b2m))
        a2p, a2m, b3p, b3m, c12 = lax.optimization_barrier((a2p, a2m, b3p, b3m, c12))
    with jax.named_scope("round3"):
        a3p, a3m = to_x(a2p[1:2], 1), to_x(a2m[2:], -1)
        c3, c0 = to_core(cat(b3p, b3m)), to_core(cat(own, pair))
    own_part, *parts = matmul(
        pos, owner[0], (near, a1p, a1m, far, a2p, a2m, a3p, a3m), (own, pair, b1p, b1m, b2p, b2m, b3p, b3m, c0, c12, c3)
    )
    with jax.named_scope("layer_sums"):
        far_part = to_layer(parts[1], 2)
        parts = [to_layer(parts[0], 1), far_part, to_layer(parts[2], 3)]
    first, second = total(pos, own_part, parts)
    with jax.named_scope("product_pair"):
        first = send(first, lambda y, c, zl, x, zh: (y, zl % 2, zl - zl % 2 + c, x, zh))
        second = send(second, lambda y, c, zl, x, zh: (y, zl % 2, zl - zl % 2 + 1 - c, x, zh))
    return place(pos, out_pattern, first, second)


def solution(mesh):
    in_specs = (
        P("row", "layer", "col"),
        P("row", "layer", "col"),
        P("layer", "row", None, "col"),
        P("layer", None),
        P(("row", "layer"), "col"),
    )
    out_specs = P(("row", "layer"), "col")
    return jax.shard_map(shards, mesh=mesh, in_specs=in_specs, out_specs=out_specs, check_vma=False)
```

```python
import itertools

import jax
import jax.numpy as jnp
from jax import lax
from jax.experimental import pallas as pl
from jax.experimental.pallas import tpu as pltpu
from jax.sharding import PartitionSpec as P

AXES = ("row", "col", "layer")
BS = 128
LEVELS = 32700.0
TINY = 1e-33
STEPS = 8.0
PAD = 16


def moves(f):
    pairs = []
    for y, c, zl, x, zh in itertools.product(range(4), range(2), range(4), range(4), range(4)):
        y2, c2, zl2, x2, zh2 = f(y, c, zl, x, zh)
        pairs.append((((y * 2 + c) * 16 + zl * 4 + x) * 4 + zh, ((y2 * 2 + c2) * 16 + zl2 * 4 + x2) * 4 + zh2))
    return pairs


def send(v, f):
    return lax.ppermute(v, AXES, moves(f))


def to_x(v, d):
    return send(v, lambda y, c, zl, x, zh: (y, c, zl, (x + d) % 4, zh))


def to_y(v, d):
    return send(v, lambda y, c, zl, x, zh: ((y + d) % 4, c, zl, x, zh))


def to_layer(v, d):
    return send(v, lambda y, c, zl, x, zh: (y, c, zl, x, (zh + d) % 4))


def to_core(v):
    return send(v, lambda y, c, zl, x, zh: (y, 1 - c, zl, x, zh))


def mask_kernel(pos_ref, pat_ref, x_ref, first_ref, second_ref):
    q = pos_ref[3]
    for h, o_ref in ((q, first_ref), (1 - q, second_ref)):
        for b in range(o_ref.shape[0] // BS):
            for j in range(x_ref.shape[1] // BS):
                block = 2 * b + h
                keep = pat_ref[j, block].astype(jnp.float32).astype(jnp.bfloat16)
                cols = pl.ds(j * BS, BS)
                o_ref[pl.ds(b * BS, BS), cols] = x_ref[pl.ds(pl.multiple_of(block * BS, BS), BS), cols] * keep


def mask(pos, panel, pattern):
    rows, width = panel.shape
    return pl.pallas_call(
        mask_kernel,
        out_shape=[jax.ShapeDtypeStruct((rows // 2, width), panel.dtype)] * 2,
        in_specs=[pl.BlockSpec(memory_space=pltpu.SMEM)] * 2 + [pl.BlockSpec(memory_space=pltpu.VMEM)],
        out_specs=[pl.BlockSpec(memory_space=pltpu.VMEM)] * 2,
        name="mask",
    )(pos, pattern, panel)


PANEL = (
    ((0, 0, 0), (0, 0, 1)),
    ((0, 3, 0), (0, 3, 1)),
    ((0, 1, 0), (0, 1, 1)),
    ((1, 0, 0), (1, 0, 1)),
    ((0, 2, 0), (1, 3, 0), (1, 3, 1)),
    ((0, 2, 1), (1, 1, 0), (1, 1, 1)),
    ((1, 2, 0),),
    ((1, 2, 1),),
)
SLAB = (
    (0, 0, 4, 0, 0, 0, 0),
    (1, 0, 4, 1, 0, 0, 0),
    (2, 0, 4, 0, 0, 3, 0),
    (3, 0, 4, 0, 0, 1, 0),
    (4, 0, 2, 0, 0, 2, 0),
    (4, 2, 4, 1, 0, 3, 0),
    (5, 0, 2, 0, 0, 2, 2),
    (5, 2, 4, 1, 0, 1, 0),
    (6, 0, 2, 1, 0, 2, 0),
    (7, 0, 2, 1, 0, 2, 2),
    (8, 0, 4, 0, 1, 0, 0),
    (8, 4, 4, 1, 1, 0, 0),
    (9, 0, 4, 0, 1, 3, 0),
    (9, 4, 4, 0, 1, 1, 0),
    (9, 8, 2, 0, 1, 2, 0),
    (9, 10, 4, 1, 1, 3, 0),
    (9, 14, 2, 0, 1, 2, 2),
    (9, 16, 4, 1, 1, 1, 0),
    (10, 0, 2, 1, 1, 2, 0),
    (10, 2, 2, 1, 1, 2, 2),
)
NA, NB = 8, 11


def quantize(tiles, o_ref):
    codes = []
    for t, v in enumerate(tiles):
        top = jnp.max(jnp.abs(v), axis=0, keepdims=True)
        code = jnp.ceil(jnp.log2(jnp.maximum(top, TINY)) * STEPS)
        v = jnp.round(v * (jnp.exp2(code * (-1.0 / STEPS)) * LEVELS)).astype(jnp.int32)
        o_ref[pl.ds(t * BS, BS), :] = v.astype(jnp.int16)
        codes.append(code)
    codes = jnp.concatenate(codes * (PAD // len(codes)), axis=0)
    o_ref[pl.ds(len(tiles) * BS, PAD), :] = codes.astype(jnp.int32).astype(jnp.int16)


def scales(v_ref, tiles):
    codes = v_ref[pl.ds(tiles * BS, PAD), :].astype(jnp.int32).astype(jnp.float32)
    return jnp.exp2(codes * (1.0 / STEPS)) * (1.0 / LEVELS)


def values(v_ref, at):
    return v_ref[at, :].astype(jnp.int32).astype(jnp.float32)


def product(chunks, pos_ref, owner_ref, a_refs, b_refs, a_s):
    y, c, p, x, layer = pos_ref[0], pos_ref[1], pos_ref[2], pos_ref[4], pos_ref[5]
    for ref, group in zip(a_refs, PANEL):
        for n, (batch, rel, i) in enumerate(group):
            col = (2 * ((p + batch) % 2) + (c + i) % 2) * 4 + (x + rel) % 4
            for u in range(2):
                block = owner_ref[2 * col + u]
                row = block // 4
                at = ((row + c) % 2) * 16 + ((row // 2 + 4 - y) % 4) * 4 + block % 4
                at = pl.ds(pl.multiple_of(at * BS, BS), BS)
                for k, chunk in enumerate(chunks):
                    rows = pl.ds(pl.multiple_of(((layer + chunk) % 4) * BS, BS), BS)
                    a_s[pl.ds(k * BS, BS), at] = ref[n, rows, pl.ds(u * BS, BS)]
    for g in range(2):
        total = None
        for array, first, blocks, half, core, rel, i in SLAB:
            if half != g:
                continue
            at = pl.ds((core * 16 + rel * 4 + i) * BS, blocks * BS)
            b = b_refs[array][pl.ds(first, blocks)].reshape(blocks * BS, 4 * BS)
            part = jnp.dot(a_s[:, at], b, preferred_element_type=jnp.float32)
            total = part if total is None else total + part
        yield g, total


def far_kernel(pos_ref, owner_ref, *refs):
    a_refs, b_refs, (o0_ref, o1_ref, a_s) = refs[:NA], refs[NA:NA + NB], refs[NA + NB:]
    for g, total in product((2,), pos_ref, owner_ref, a_refs, b_refs, a_s):
        quantize([total[:, n * BS:(n + 1) * BS] for n in range(4)], (o0_ref, o1_ref)[g])


def rest_kernel(pos_ref, owner_ref, *refs):
    a_refs, b_refs, (*o_refs, a_s) = refs[:NA], refs[NA:NA + NB], refs[NA + NB:]
    for g, total in product((0, 1, 3), pos_ref, owner_ref, a_refs, b_refs, a_s):
        for k, o_ref in enumerate(o_refs):
            o_ref[g] = total[k * BS:(k + 1) * BS]


def matmul(kernel, name, chunks, out_shape, pos, owner, a, b):
    depth = 32 * BS
    return pl.pallas_call(
        kernel,
        out_shape=out_shape,
        in_specs=[pl.BlockSpec(memory_space=pltpu.SMEM)] * 2 + [pl.BlockSpec(memory_space=pltpu.VMEM)] * (NA + NB),
        out_specs=[pl.BlockSpec(memory_space=pltpu.VMEM)] * len(out_shape),
        scratch_shapes=[pltpu.VMEM((chunks * BS, depth), jnp.bfloat16)],
        compiler_params=pltpu.CompilerParams(vmem_limit_bytes=32 << 20),
        cost_estimate=pl.CostEstimate(flops=2 * chunks * BS * 8 * BS * depth, bytes_accessed=1 << 20, transcendentals=0),
        name=name,
    )(pos, owner, *a, *b)


def add_kernel(own1_ref, own3_ref, got1_ref, got3_ref, o1_ref, o3_ref):
    for half, own_ref, got_ref, o_ref in ((0, own1_ref, got1_ref, o1_ref), (1, own3_ref, got3_ref, o3_ref)):
        scale = scales(got_ref, 4)
        tiles = []
        for t in range(8):
            v = own_ref[t // 4, :, pl.ds((t % 4) * BS, BS)]
            if t // 4 == half:
                n = t % 4
                v = v + values(got_ref, pl.ds(n * BS, BS)) * scale[n:n + 1, :]
            tiles.append(v)
        quantize(tiles, o_ref)


def add(own1, own3, got1, got3):
    return pl.pallas_call(
        add_kernel,
        out_shape=[jax.ShapeDtypeStruct((8 * BS + PAD, BS), jnp.int16)] * 2,
        in_specs=[pl.BlockSpec(memory_space=pltpu.VMEM)] * 4,
        out_specs=[pl.BlockSpec(memory_space=pltpu.VMEM)] * 2,
        name="add",
    )(own1, own3, got1, got3)


def total_kernel(pos_ref, own_ref, *refs):
    v_refs, o_refs = refs[:2], refs[2:]
    other = (pos_ref[1] + pos_ref[3]) % 2
    found = [scales(v_ref, 8) for v_ref in v_refs]
    for g, o_ref in zip((other, 1 - other), o_refs):
        for n in range(4):
            at = pl.ds(pl.multiple_of((g * 4 + n) * BS, BS), BS)
            total = own_ref[g, :, pl.ds(n * BS, BS)]
            for v_ref, scale in zip(v_refs, found):
                total = total + values(v_ref, at) * jnp.where(g == 0, scale[n:n + 1, :], scale[4 + n:5 + n, :])
            o_ref[:, pl.ds(n * BS, BS)] = total.astype(jnp.bfloat16)


def total(pos, own, v):
    return pl.pallas_call(
        total_kernel,
        out_shape=[jax.ShapeDtypeStruct((BS, 4 * BS), jnp.bfloat16)] * 2,
        in_specs=[pl.BlockSpec(memory_space=pltpu.SMEM)] + [pl.BlockSpec(memory_space=pltpu.VMEM)] * 3,
        out_specs=[pl.BlockSpec(memory_space=pltpu.VMEM)] * 2,
        name="total",
    )(pos, own, *v)


def place_kernel(pos_ref, pat_ref, first_ref, second_ref, o_ref):
    q = pos_ref[3]
    for b, ref in ((q, first_ref), (1 - q, second_ref)):
        for n in range(4):
            keep = pat_ref[b, n].astype(jnp.float32).astype(jnp.bfloat16)
            cols = pl.ds(n * BS, BS)
            o_ref[pl.ds(pl.multiple_of(b * BS, BS), BS), cols] = ref[:, cols] * keep


def place(pos, pattern, first, second):
    return pl.pallas_call(
        place_kernel,
        out_shape=jax.ShapeDtypeStruct((2 * BS, 4 * BS), jnp.bfloat16),
        in_specs=[pl.BlockSpec(memory_space=pltpu.SMEM)] * 2 + [pl.BlockSpec(memory_space=pltpu.VMEM)] * 2,
        out_specs=pl.BlockSpec(memory_space=pltpu.VMEM),
        name="place",
    )(pos, pattern, first, second)


def shards(panel, in_pattern, slab, owner, out_pattern):
    row, col = lax.axis_index("row"), lax.axis_index("col")
    zl = col // 4
    pos = jnp.stack([row // 2, row % 2, zl // 2, zl % 2, col % 4, lax.axis_index("layer")])
    cat = lambda *v: jnp.concatenate(v, axis=0)
    own = slab[0]
    first, second = mask(pos, panel[:, 0, :], in_pattern[:, 0, :].T)
    with jax.named_scope("round0"):
        first = send(first, lambda y, c, zl, x, zh: (y, zl % 2, zl - zl % 2 + c, x, zh))
        second = send(second, lambda y, c, zl, x, zh: (y, 1 - zl % 2, zl - zl % 2 + c, x, zh))
        pair = send(own, lambda y, c, zl, x, zh: (y, c, zl ^ 1, x, zh))
        b1p, b1m = to_y(own, 1), to_y(own, -1)
        first, second, pair, b1p, b1m = lax.optimization_barrier((first, second, pair, b1p, b1m))
        near = jnp.stack([first, second])
    with jax.named_scope("round1"):
        far = send(near, lambda y, c, zl, x, zh: (y, c, zl ^ 2, x, zh))
        a1p, a1m = to_x(near, 1), to_x(near, -1)
        b2p, b2m = to_y(cat(b1p[:2], pair), 1), to_y(cat(b1m[2:], pair), -1)
        far, a1p, a1m, b2p, b2m = lax.optimization_barrier((far, a1p, a1m, b2p, b2m))
    with jax.named_scope("round2"):
        a2p, a2m = to_x(cat(a1p[:1], far), 1), to_x(cat(a1m[1:], far), -1)
        b3p, b3m = to_y(b2p[2:4], 1), to_y(b2m[4:], -1)
        c12 = to_core(cat(b1p, b1m, b2p, b2m))
        a2p, a2m, b3p, b3m, c12, late = lax.optimization_barrier((a2p, a2m, b3p, b3m, c12, pair))
    with jax.named_scope("round3"):
        a3p, a3m = to_x(a2p[1:2], 1), to_x(a2m[2:], -1)
        c3, c0 = to_core(cat(b3p, b3m)), to_core(cat(own, late))
    a = (near, a1p, a1m, far, a2p, a2m, a3p, a3m)
    b = (own, pair, b1p, b1m, b2p, b2m, b3p, b3m, c0, c12, c3)
    half_shape = [jax.ShapeDtypeStruct((4 * BS + PAD, BS), jnp.int16)] * 2
    whole_shape = [jax.ShapeDtypeStruct((2, BS, 4 * BS), jnp.float32)] * 3
    far1, far3 = matmul(far_kernel, "matmul_far", 1, half_shape, pos, owner[0], a, b)
    with jax.named_scope("layer_halves"):
        got1, got3 = to_layer(far1, 1), to_layer(far3, -1)
    own_part, part1, part3 = matmul(rest_kernel, "matmul_rest", 3, whole_shape, pos, owner[0], a, b)
    part1, part3 = add(part1, part3, got1, got3)
    with jax.named_scope("layer_sums"):
        got1, got3 = to_layer(part1, 1), to_layer(part3, -1)
    first, second = total(pos, own_part, (got1, got3))
    with jax.named_scope("product_pair"):
        first = send(first, lambda y, c, zl, x, zh: (y, zl % 2, zl - zl % 2 + c, x, zh))
        second = send(second, lambda y, c, zl, x, zh: (y, zl % 2, zl - zl % 2 + 1 - c, x, zh))
    return place(pos, out_pattern, first, second)


def solution(mesh):
    in_specs = (
        P("row", "layer", "col"),
        P("row", "layer", "col"),
        P("layer", "row", None, "col"),
        P("layer", None),
        P(("row", "layer"), "col"),
    )
    out_specs = P(("row", "layer"), "col")
    return jax.shard_map(shards, mesh=mesh, in_specs=in_specs, out_specs=out_specs, check_vma=False)
```

```python
import itertools

import jax
import jax.numpy as jnp
from jax import lax
from jax.experimental import pallas as pl
from jax.experimental.pallas import tpu as pltpu
from jax.sharding import PartitionSpec as P

AXES = ("row", "col", "layer")
BS = 128
LEVELS = 32700.0
TINY = 1e-33
STEPS = 8.0
PAD = 16


def moves(f):
    pairs = []
    for y, c, zl, x, zh in itertools.product(range(4), range(2), range(4), range(4), range(4)):
        y2, c2, zl2, x2, zh2 = f(y, c, zl, x, zh)
        pairs.append((((y * 2 + c) * 16 + zl * 4 + x) * 4 + zh, ((y2 * 2 + c2) * 16 + zl2 * 4 + x2) * 4 + zh2))
    return pairs


def send(v, f):
    return lax.ppermute(v, AXES, moves(f))


def to_x(v, d):
    return send(v, lambda y, c, zl, x, zh: (y, c, zl, (x + d) % 4, zh))


def to_layer(v, d):
    return send(v, lambda y, c, zl, x, zh: (y, c, zl, x, (zh + d) % 4))


def mask_kernel(pos_ref, pat_ref, x_ref, first_ref, second_ref):
    q = pos_ref[3]
    for h, o_ref in ((q, first_ref), (1 - q, second_ref)):
        for b in range(o_ref.shape[0] // BS):
            for j in range(x_ref.shape[1] // BS):
                block = 2 * b + h
                keep = pat_ref[j, block].astype(jnp.float32).astype(jnp.bfloat16)
                cols = pl.ds(j * BS, BS)
                o_ref[pl.ds(b * BS, BS), cols] = x_ref[pl.ds(pl.multiple_of(block * BS, BS), BS), cols] * keep


def mask(pos, panel, pattern):
    rows, width = panel.shape
    return pl.pallas_call(
        mask_kernel,
        out_shape=[jax.ShapeDtypeStruct((rows // 2, width), panel.dtype)] * 2,
        in_specs=[pl.BlockSpec(memory_space=pltpu.SMEM)] * 2 + [pl.BlockSpec(memory_space=pltpu.VMEM)],
        out_specs=[pl.BlockSpec(memory_space=pltpu.VMEM)] * 2,
        name="mask",
    )(pos, pattern, panel)


PANEL = ((0, 0), (0, 3), (0, 1), (0, 2), (1, 0), (1, 3), (1, 1), (1, 2))
NA = len(PANEL)


def quantize(tiles, o_ref):
    codes = []
    for t, v in enumerate(tiles):
        top = jnp.max(jnp.abs(v), axis=0, keepdims=True)
        code = jnp.ceil(jnp.log2(jnp.maximum(top, TINY)) * STEPS)
        v = jnp.round(v * (jnp.exp2(code * (-1.0 / STEPS)) * LEVELS)).astype(jnp.int32)
        o_ref[pl.ds(t * BS, BS), :] = v.astype(jnp.int16)
        codes.append(code)
    codes = jnp.concatenate(codes * (PAD // len(codes)), axis=0)
    o_ref[pl.ds(len(tiles) * BS, PAD), :] = codes.astype(jnp.int32).astype(jnp.int16)


def scales(v_ref, tiles):
    codes = v_ref[pl.ds(tiles * BS, PAD), :].astype(jnp.int32).astype(jnp.float32)
    return jnp.exp2(codes * (1.0 / STEPS)) * (1.0 / LEVELS)


def values(v_ref, at):
    return v_ref[at, :].astype(jnp.int32).astype(jnp.float32)


def product(chunks, pos_ref, owner_ref, a_refs, b_ref, a_s):
    c, p, x, layer = pos_ref[1], pos_ref[2], pos_ref[4], pos_ref[5]
    for ref, (batch, rel) in zip(a_refs, PANEL):
        for i in range(2):
            col = (2 * ((p + batch) % 2) + (c + i) % 2) * 4 + (x + rel) % 4
            for u in range(2):
                at = pl.ds(pl.multiple_of(owner_ref[2 * col + u] * BS, BS), BS)
                for k, chunk in enumerate(chunks):
                    rows = pl.ds(pl.multiple_of(((layer + chunk) % 4) * BS, BS), BS)
                    a_s[pl.ds(k * BS, BS), at] = ref[i, rows, pl.ds(u * BS, BS)]
    for g in range(2):
        total = None
        for row in range(8):
            b = b_ref[row, pl.ds(4 * g, 4)].reshape(4 * BS, 4 * BS)
            part = jnp.dot(a_s[:, pl.ds(row * 4 * BS, 4 * BS)], b, preferred_element_type=jnp.float32)
            total = part if total is None else total + part
        yield g, total


def far_kernel(pos_ref, owner_ref, *refs):
    a_refs, (b_ref, o0_ref, o1_ref, a_s) = refs[:NA], refs[NA:]
    for g, total in product((2,), pos_ref, owner_ref, a_refs, b_ref, a_s):
        quantize([total[:, n * BS:(n + 1) * BS] for n in range(4)], (o0_ref, o1_ref)[g])


def rest_kernel(pos_ref, owner_ref, *refs):
    a_refs, (b_ref, *o_refs, a_s) = refs[:NA], refs[NA:]
    for g, total in product((0, 1, 3), pos_ref, owner_ref, a_refs, b_ref, a_s):
        for k, o_ref in enumerate(o_refs):
            o_ref[g] = total[k * BS:(k + 1) * BS]


def matmul(kernel, name, chunks, out_shape, pos, owner, a, b):
    depth = 32 * BS
    return pl.pallas_call(
        kernel,
        out_shape=out_shape,
        in_specs=[pl.BlockSpec(memory_space=pltpu.SMEM)] * 2 + [pl.BlockSpec(memory_space=pltpu.VMEM)] * (NA + 1),
        out_specs=[pl.BlockSpec(memory_space=pltpu.VMEM)] * len(out_shape),
        scratch_shapes=[pltpu.VMEM((chunks * BS, depth), jnp.bfloat16)],
        compiler_params=pltpu.CompilerParams(vmem_limit_bytes=32 << 20),
        cost_estimate=pl.CostEstimate(flops=2 * chunks * BS * 8 * BS * depth, bytes_accessed=1 << 20, transcendentals=0),
        name=name,
    )(pos, owner, *a, b)


def add_kernel(own1_ref, own3_ref, got1_ref, got3_ref, o1_ref, o3_ref):
    for half, own_ref, got_ref, o_ref in ((0, own1_ref, got1_ref, o1_ref), (1, own3_ref, got3_ref, o3_ref)):
        scale = scales(got_ref, 4)
        tiles = []
        for t in range(8):
            v = own_ref[t // 4, :, pl.ds((t % 4) * BS, BS)]
            if t // 4 == half:
                n = t % 4
                v = v + values(got_ref, pl.ds(n * BS, BS)) * scale[n:n + 1, :]
            tiles.append(v)
        quantize(tiles, o_ref)


def add(own1, own3, got1, got3):
    return pl.pallas_call(
        add_kernel,
        out_shape=[jax.ShapeDtypeStruct((8 * BS + PAD, BS), jnp.int16)] * 2,
        in_specs=[pl.BlockSpec(memory_space=pltpu.VMEM)] * 4,
        out_specs=[pl.BlockSpec(memory_space=pltpu.VMEM)] * 2,
        name="add",
    )(own1, own3, got1, got3)


def total_kernel(pos_ref, own_ref, *refs):
    v_refs, o_refs = refs[:2], refs[2:]
    other = (pos_ref[1] + pos_ref[3]) % 2
    found = [scales(v_ref, 8) for v_ref in v_refs]
    for g, o_ref in zip((other, 1 - other), o_refs):
        for n in range(4):
            at = pl.ds(pl.multiple_of((g * 4 + n) * BS, BS), BS)
            total = own_ref[g, :, pl.ds(n * BS, BS)]
            for v_ref, scale in zip(v_refs, found):
                total = total + values(v_ref, at) * jnp.where(g == 0, scale[n:n + 1, :], scale[4 + n:5 + n, :])
            o_ref[:, pl.ds(n * BS, BS)] = total.astype(jnp.bfloat16)


def total(pos, own, v):
    return pl.pallas_call(
        total_kernel,
        out_shape=[jax.ShapeDtypeStruct((BS, 4 * BS), jnp.bfloat16)] * 2,
        in_specs=[pl.BlockSpec(memory_space=pltpu.SMEM)] + [pl.BlockSpec(memory_space=pltpu.VMEM)] * 3,
        out_specs=[pl.BlockSpec(memory_space=pltpu.VMEM)] * 2,
        name="total",
    )(pos, own, *v)


def place_kernel(pos_ref, pat_ref, first_ref, second_ref, o_ref):
    q = pos_ref[3]
    for b, ref in ((q, first_ref), (1 - q, second_ref)):
        for n in range(4):
            keep = pat_ref[b, n].astype(jnp.float32).astype(jnp.bfloat16)
            cols = pl.ds(n * BS, BS)
            o_ref[pl.ds(pl.multiple_of(b * BS, BS), BS), cols] = ref[:, cols] * keep


def place(pos, pattern, first, second):
    return pl.pallas_call(
        place_kernel,
        out_shape=jax.ShapeDtypeStruct((2 * BS, 4 * BS), jnp.bfloat16),
        in_specs=[pl.BlockSpec(memory_space=pltpu.SMEM)] * 2 + [pl.BlockSpec(memory_space=pltpu.VMEM)] * 2,
        out_specs=pl.BlockSpec(memory_space=pltpu.VMEM),
        name="place",
    )(pos, pattern, first, second)


def shards(panel, in_pattern, slab, owner, out_pattern):
    row, col = lax.axis_index("row"), lax.axis_index("col")
    zl = col // 4
    pos = jnp.stack([row // 2, row % 2, zl // 2, zl % 2, col % 4, lax.axis_index("layer")])
    first, second = mask(pos, panel[:, 0, :], in_pattern[:, 0, :].T)
    own = slab[0]
    with jax.named_scope("slab_pair"):
        pair = send(own, lambda y, c, zl, x, zh: (y, c, zl ^ 1, x, zh))
    with jax.named_scope("panel_pair"):
        first = send(first, lambda y, c, zl, x, zh: (y, zl % 2, zl - zl % 2 + c, x, zh))
        second = send(second, lambda y, c, zl, x, zh: (y, 1 - zl % 2, zl - zl % 2 + c, x, zh))
        pair, first, second = lax.optimization_barrier((pair, first, second))
        near = jnp.stack([first, second])
    with jax.named_scope("slab_rows"):
        b = lax.all_gather(jnp.concatenate([own, pair]), "row", axis=0)
    with jax.named_scope("panel_far"):
        far = send(near, lambda y, c, zl, x, zh: (y, c, zl ^ 2, x, zh))
    with jax.named_scope("panel_near_x"):
        near_x = [to_x(near, d) for d in (1, 3, 2)]
    with jax.named_scope("panel_far_x"):
        far_x = [to_x(far, d) for d in (1, 3, 2)]
    a = (near, *near_x, far, *far_x)
    half_shape = [jax.ShapeDtypeStruct((4 * BS + PAD, BS), jnp.int16)] * 2
    whole_shape = [jax.ShapeDtypeStruct((2, BS, 4 * BS), jnp.float32)] * 3
    far1, far3 = matmul(far_kernel, "matmul_far", 1, half_shape, pos, owner[0], a, b)
    with jax.named_scope("layer_halves"):
        got1, got3 = to_layer(far1, 1), to_layer(far3, -1)
    own_part, part1, part3 = matmul(rest_kernel, "matmul_rest", 3, whole_shape, pos, owner[0], a, b)
    part1, part3 = add(part1, part3, got1, got3)
    with jax.named_scope("layer_sums"):
        got1, got3 = to_layer(part1, 1), to_layer(part3, -1)
    first, second = total(pos, own_part, (got1, got3))
    with jax.named_scope("product_pair"):
        first = send(first, lambda y, c, zl, x, zh: (y, zl % 2, zl - zl % 2 + c, x, zh))
        second = send(second, lambda y, c, zl, x, zh: (y, zl % 2, zl - zl % 2 + 1 - c, x, zh))
    return place(pos, out_pattern, first, second)


def solution(mesh):
    in_specs = (
        P("row", "layer", "col"),
        P("row", "layer", "col"),
        P("layer", "row", None, "col"),
        P("layer", None),
        P(("row", "layer"), "col"),
    )
    out_specs = P(("row", "layer"), "col")
    return jax.shard_map(shards, mesh=mesh, in_specs=in_specs, out_specs=out_specs, check_vma=False)
```

```python
import itertools

import jax
import jax.numpy as jnp
from jax import lax
from jax.experimental import pallas as pl
from jax.experimental.pallas import tpu as pltpu
from jax.sharding import PartitionSpec as P

AXES = ("row", "col", "layer")
BS = 128
LEVELS = 32700.0
TINY = 1e-33
STEPS = 8.0
PAD = 16


def moves(f):
    pairs = []
    for y, c, zl, x, zh in itertools.product(range(4), range(2), range(4), range(4), range(4)):
        y2, c2, zl2, x2, zh2 = f(y, c, zl, x, zh)
        pairs.append((((y * 2 + c) * 16 + zl * 4 + x) * 4 + zh, ((y2 * 2 + c2) * 16 + zl2 * 4 + x2) * 4 + zh2))
    return pairs


def send(v, f):
    return lax.ppermute(v, AXES, moves(f))


def to_x(v, d):
    return send(v, lambda y, c, zl, x, zh: (y, c, zl, (x + d) % 4, zh))


def to_y(v, d):
    return send(v, lambda y, c, zl, x, zh: ((y + d) % 4, c, zl, x, zh))


def to_layer(v, d):
    return send(v, lambda y, c, zl, x, zh: (y, c, zl, x, (zh + d) % 4))


def to_core(v):
    return send(v, lambda y, c, zl, x, zh: (y, 1 - c, zl, x, zh))


def mask_kernel(pos_ref, pat_ref, x_ref, first_ref, second_ref):
    q = pos_ref[3]
    for h, o_ref in ((q, first_ref), (1 - q, second_ref)):
        for b in range(o_ref.shape[0] // BS):
            for j in range(x_ref.shape[1] // BS):
                block = 2 * b + h
                keep = pat_ref[j, block].astype(jnp.float32).astype(jnp.bfloat16)
                cols = pl.ds(j * BS, BS)
                o_ref[pl.ds(b * BS, BS), cols] = x_ref[pl.ds(pl.multiple_of(block * BS, BS), BS), cols] * keep


def mask(pos, panel, pattern):
    rows, width = panel.shape
    return pl.pallas_call(
        mask_kernel,
        out_shape=[jax.ShapeDtypeStruct((rows // 2, width), panel.dtype)] * 2,
        in_specs=[pl.BlockSpec(memory_space=pltpu.SMEM)] * 2 + [pl.BlockSpec(memory_space=pltpu.VMEM)],
        out_specs=[pl.BlockSpec(memory_space=pltpu.VMEM)] * 2,
        name="mask",
    )(pos, pattern, panel)


PANEL = (
    ((0, 0, 0), (0, 0, 1)),
    ((0, 3, 0), (0, 3, 1)),
    ((0, 1, 0), (0, 1, 1)),
    ((1, 0, 0), (1, 0, 1)),
    ((0, 2, 0), (1, 3, 0), (1, 3, 1)),
    ((0, 2, 1), (1, 1, 0), (1, 1, 1)),
    ((1, 2, 0), (1, 2, 1)),
)
SLAB = (
    (0, 0, 4, 0, 0, 0, 0),
    (1, 0, 4, 1, 0, 0, 0),
    (2, 0, 4, 0, 0, 3, 0),
    (3, 0, 4, 0, 0, 1, 0),
    (4, 0, 2, 0, 0, 2, 0),
    (4, 2, 4, 1, 0, 3, 0),
    (5, 0, 2, 0, 0, 2, 2),
    (5, 2, 4, 1, 0, 1, 0),
    (6, 0, 4, 1, 0, 2, 0),
    (7, 0, 4, 0, 1, 0, 0),
    (7, 4, 4, 1, 1, 0, 0),
    (7, 8, 4, 0, 1, 3, 0),
    (7, 12, 4, 0, 1, 1, 0),
    (7, 16, 2, 0, 1, 2, 0),
    (7, 18, 4, 1, 1, 3, 0),
    (7, 22, 2, 0, 1, 2, 2),
    (7, 24, 4, 1, 1, 1, 0),
    (8, 0, 4, 1, 1, 2, 0),
)
NA, NB = 7, 9


def quantize(tiles, o_ref):
    codes = []
    for t, v in enumerate(tiles):
        top = jnp.max(jnp.abs(v), axis=0, keepdims=True)
        code = jnp.ceil(jnp.log2(jnp.maximum(top, TINY)) * STEPS)
        v = jnp.round(v * (jnp.exp2(code * (-1.0 / STEPS)) * LEVELS)).astype(jnp.int32)
        o_ref[pl.ds(t * BS, BS), :] = v.astype(jnp.int16)
        codes.append(code)
    codes = jnp.concatenate(codes * (PAD // len(codes)), axis=0)
    o_ref[pl.ds(len(tiles) * BS, PAD), :] = codes.astype(jnp.int32).astype(jnp.int16)


def scales(v_ref, tiles):
    codes = v_ref[pl.ds(tiles * BS, PAD), :].astype(jnp.int32).astype(jnp.float32)
    return jnp.exp2(codes * (1.0 / STEPS)) * (1.0 / LEVELS)


def values(v_ref, at):
    return v_ref[at, :].astype(jnp.int32).astype(jnp.float32)


def product(chunks, pos_ref, owner_ref, a_refs, b_refs, a_s):
    y, c, p, x, layer = pos_ref[0], pos_ref[1], pos_ref[2], pos_ref[4], pos_ref[5]
    for ref, group in zip(a_refs, PANEL):
        for n, (batch, rel, i) in enumerate(group):
            col = (2 * ((p + batch) % 2) + (c + i) % 2) * 4 + (x + rel) % 4
            for u in range(2):
                block = owner_ref[2 * col + u]
                row = block // 4
                at = ((row + c) % 2) * 16 + ((row // 2 + 4 - y) % 4) * 4 + block % 4
                at = pl.ds(pl.multiple_of(at * BS, BS), BS)
                for k, chunk in enumerate(chunks):
                    rows = pl.ds(pl.multiple_of(((layer + chunk) % 4) * BS, BS), BS)
                    a_s[pl.ds(k * BS, BS), at] = ref[n, rows, pl.ds(u * BS, BS)]
    for g in range(2):
        total = None
        for array, first, blocks, half, core, rel, i in SLAB:
            if half != g:
                continue
            at = pl.ds((core * 16 + rel * 4 + i) * BS, blocks * BS)
            b = b_refs[array][pl.ds(first, blocks)].reshape(blocks * BS, 4 * BS)
            part = jnp.dot(a_s[:, at], b, preferred_element_type=jnp.float32)
            total = part if total is None else total + part
        yield g, total


def far_kernel(pos_ref, owner_ref, *refs):
    a_refs, b_refs, (o_ref, a_s) = refs[:NA], refs[NA:NA + NB], refs[NA + NB:]
    tiles = []
    for g, total in product((2,), pos_ref, owner_ref, a_refs, b_refs, a_s):
        tiles += [total[:, n * BS:(n + 1) * BS] for n in range(4)]
    quantize(tiles, o_ref)


def rest_kernel(pos_ref, owner_ref, *refs):
    a_refs, b_refs, (*o_refs, a_s) = refs[:NA], refs[NA:NA + NB], refs[NA + NB:]
    for g, total in product((0, 1, 3), pos_ref, owner_ref, a_refs, b_refs, a_s):
        for k, o_ref in enumerate(o_refs):
            o_ref[g] = total[k * BS:(k + 1) * BS]


def matmul(kernel, name, chunks, out_shape, pos, owner, a, b):
    depth = 32 * BS
    return pl.pallas_call(
        kernel,
        out_shape=out_shape,
        in_specs=[pl.BlockSpec(memory_space=pltpu.SMEM)] * 2 + [pl.BlockSpec(memory_space=pltpu.VMEM)] * (NA + NB),
        out_specs=[pl.BlockSpec(memory_space=pltpu.VMEM)] * len(out_shape),
        scratch_shapes=[pltpu.VMEM((chunks * BS, depth), jnp.bfloat16)],
        compiler_params=pltpu.CompilerParams(vmem_limit_bytes=32 << 20),
        cost_estimate=pl.CostEstimate(flops=2 * chunks * BS * 8 * BS * depth, bytes_accessed=1 << 20, transcendentals=0),
        name=name,
    )(pos, owner, *a, *b)


def add_kernel(pos_ref, own1_ref, own3_ref, got_ref, o1_ref, o3_ref):
    scale = scales(got_ref, 8)
    for core, own_ref, o_ref in ((0, own1_ref, o1_ref), (1, own3_ref, o3_ref)):
        mine = pos_ref[1] == core
        tiles = []
        for t in range(8):
            got = values(got_ref, pl.ds(t * BS, BS)) * scale[t:t + 1, :]
            tiles.append(own_ref[t // 4, :, pl.ds((t % 4) * BS, BS)] + jnp.where(mine, got, 0.0))
        quantize(tiles, o_ref)


def add(pos, own1, own3, got):
    return pl.pallas_call(
        add_kernel,
        out_shape=[jax.ShapeDtypeStruct((8 * BS + PAD, BS), jnp.int16)] * 2,
        in_specs=[pl.BlockSpec(memory_space=pltpu.SMEM)] + [pl.BlockSpec(memory_space=pltpu.VMEM)] * 3,
        out_specs=[pl.BlockSpec(memory_space=pltpu.VMEM)] * 2,
        name="add",
    )(pos, own1, own3, got)


def total_kernel(pos_ref, own_ref, *refs):
    v_refs, o_refs = refs[:2], refs[2:]
    other = (pos_ref[1] + pos_ref[3]) % 2
    found = [scales(v_ref, 8) for v_ref in v_refs]
    for g, o_ref in zip((other, 1 - other), o_refs):
        for n in range(4):
            at = pl.ds(pl.multiple_of((g * 4 + n) * BS, BS), BS)
            total = own_ref[g, :, pl.ds(n * BS, BS)]
            for v_ref, scale in zip(v_refs, found):
                total = total + values(v_ref, at) * jnp.where(g == 0, scale[n:n + 1, :], scale[4 + n:5 + n, :])
            o_ref[:, pl.ds(n * BS, BS)] = total.astype(jnp.bfloat16)


def total(pos, own, v):
    return pl.pallas_call(
        total_kernel,
        out_shape=[jax.ShapeDtypeStruct((BS, 4 * BS), jnp.bfloat16)] * 2,
        in_specs=[pl.BlockSpec(memory_space=pltpu.SMEM)] + [pl.BlockSpec(memory_space=pltpu.VMEM)] * 3,
        out_specs=[pl.BlockSpec(memory_space=pltpu.VMEM)] * 2,
        name="total",
    )(pos, own, *v)


def place_kernel(pos_ref, pat_ref, first_ref, second_ref, o_ref):
    q = pos_ref[3]
    for b, ref in ((q, first_ref), (1 - q, second_ref)):
        for n in range(4):
            keep = pat_ref[b, n].astype(jnp.float32).astype(jnp.bfloat16)
            cols = pl.ds(n * BS, BS)
            o_ref[pl.ds(pl.multiple_of(b * BS, BS), BS), cols] = ref[:, cols] * keep


def place(pos, pattern, first, second):
    return pl.pallas_call(
        place_kernel,
        out_shape=jax.ShapeDtypeStruct((2 * BS, 4 * BS), jnp.bfloat16),
        in_specs=[pl.BlockSpec(memory_space=pltpu.SMEM)] * 2 + [pl.BlockSpec(memory_space=pltpu.VMEM)] * 2,
        out_specs=pl.BlockSpec(memory_space=pltpu.VMEM),
        name="place",
    )(pos, pattern, first, second)


def shards(panel, in_pattern, slab, owner, out_pattern):
    row, col = lax.axis_index("row"), lax.axis_index("col")
    zl = col // 4
    pos = jnp.stack([row // 2, row % 2, zl // 2, zl % 2, col % 4, lax.axis_index("layer")])
    cat = lambda *v: jnp.concatenate(v, axis=0)
    own = slab[0]
    with jax.named_scope("round0"):
        pair = send(own, lambda y, c, zl, x, zh: (y, c, zl ^ 1, x, zh))
        first, second = mask(pos, panel[:, 0, :], in_pattern[:, 0, :].T)
        first = send(first, lambda y, c, zl, x, zh: (y, zl % 2, zl - zl % 2 + c, x, zh))
        second = send(second, lambda y, c, zl, x, zh: (y, 1 - zl % 2, zl - zl % 2 + c, x, zh))
        first, second, pair, late = lax.optimization_barrier((first, second, pair, own))
        near = jnp.stack([first, second])
    with jax.named_scope("round1"):
        far = send(near, lambda y, c, zl, x, zh: (y, c, zl ^ 2, x, zh))
        a1p, a1m = to_x(near, 1), to_x(near, -1)
        b1p, b1m = to_y(late, 1), to_y(late, -1)
        far, a1p, a1m, b1p, b1m = lax.optimization_barrier((far, a1p, a1m, b1p, b1m))
    with jax.named_scope("round2"):
        a2p, a2m = to_x(cat(a1p[:1], far), 1), to_x(cat(a1m[1:], far), -1)
        b2p, b2m = to_y(cat(b1p[:2], pair), 1), to_y(cat(b1m[2:], pair), -1)
        a2p, a2m, b2p, b2m = lax.optimization_barrier((a2p, a2m, b2p, b2m))
    with jax.named_scope("round3"):
        even = row % 2 == 0
        hand_a, hand_b = jnp.where(even, a2p[1:], a2m[1:]), jnp.where(even, b2p[2:], b2m[2:])
        a3 = send(hand_a, lambda y, c, zl, x, zh: (y, c, zl, (x + 1 - 2 * c) % 4, zh))
        b3 = send(hand_b, lambda y, c, zl, x, zh: ((y + 1 - 2 * c) % 4, c, zl, x, zh))
        b3x = send(hand_b, lambda y, c, zl, x, zh: ((y + 1 - 2 * c) % 4, 1 - c, zl, x, zh))
        swap = to_core(cat(late, pair, b1p, b1m, b2p, b2m))
    a = (near, a1p, a1m, far, a2p, a2m, a3)
    b = (late, pair, b1p, b1m, b2p, b2m, b3, swap, b3x)
    far_shape = [jax.ShapeDtypeStruct((8 * BS + PAD, BS), jnp.int16)]
    rest_shape = [jax.ShapeDtypeStruct((2, BS, 4 * BS), jnp.float32)] * 3
    got, = matmul(far_kernel, "matmul_far", 1, far_shape, pos, owner[0], a, b)
    with jax.named_scope("layer_far"):
        got = send(got, lambda y, c, zl, x, zh: (y, c, zl, x, (zh + 1 - 2 * c) % 4))
    own_part, part1, part3 = matmul(rest_kernel, "matmul_rest", 3, rest_shape, pos, owner[0], a, b)
    part1, part3 = add(pos, part1, part3, got)
    with jax.named_scope("layer_sums"):
        got1, got3 = to_layer(part1, 1), to_layer(part3, -1)
    first, second = total(pos, own_part, (got1, got3))
    with jax.named_scope("product_pair"):
        first = send(first, lambda y, c, zl, x, zh: (y, zl % 2, zl - zl % 2 + c, x, zh))
        second = send(second, lambda y, c, zl, x, zh: (y, zl % 2, zl - zl % 2 + 1 - c, x, zh))
    return place(pos, out_pattern, first, second)


def solution(mesh):
    in_specs = (
        P("row", "layer", "col"),
        P("row", "layer", "col"),
        P("layer", "row", None, "col"),
        P("layer", None),
        P(("row", "layer"), "col"),
    )
    out_specs = P(("row", "layer"), "col")
    return jax.shard_map(shards, mesh=mesh, in_specs=in_specs, out_specs=out_specs, check_vma=False)
```

```python
import itertools

import jax
import jax.numpy as jnp
from jax import lax
from jax.experimental import pallas as pl
from jax.experimental.pallas import tpu as pltpu
from jax.sharding import PartitionSpec as P

AXES = ("row", "col", "layer")
BS = 128
LEVELS = 32700.0
TINY = 1e-33
STEPS = 8.0
PAD = 16


def moves(f):
    pairs = []
    for y, c, zl, x, zh in itertools.product(range(4), range(2), range(4), range(4), range(4)):
        y2, c2, zl2, x2, zh2 = f(y, c, zl, x, zh)
        pairs.append((((y * 2 + c) * 16 + zl * 4 + x) * 4 + zh, ((y2 * 2 + c2) * 16 + zl2 * 4 + x2) * 4 + zh2))
    return pairs


def send(v, f):
    return lax.ppermute(v, AXES, moves(f))


def to_x(v, d):
    return send(v, lambda y, c, zl, x, zh: (y, c, zl, (x + d) % 4, zh))


def to_y(v, d):
    return send(v, lambda y, c, zl, x, zh: ((y + d) % 4, c, zl, x, zh))


def to_layer(v, d):
    return send(v, lambda y, c, zl, x, zh: (y, c, zl, x, (zh + d) % 4))


def to_core(v):
    return send(v, lambda y, c, zl, x, zh: (y, 1 - c, zl, x, zh))


def mask_kernel(pos_ref, pat_ref, x_ref, first_ref, second_ref):
    q = pos_ref[3]
    for h, o_ref in ((q, first_ref), (1 - q, second_ref)):
        for b in range(o_ref.shape[0] // BS):
            for j in range(x_ref.shape[1] // BS):
                block = 2 * b + h
                keep = pat_ref[j, block].astype(jnp.float32).astype(jnp.bfloat16)
                cols = pl.ds(j * BS, BS)
                o_ref[pl.ds(b * BS, BS), cols] = x_ref[pl.ds(pl.multiple_of(block * BS, BS), BS), cols] * keep


def mask(pos, panel, pattern):
    rows, width = panel.shape
    return pl.pallas_call(
        mask_kernel,
        out_shape=[jax.ShapeDtypeStruct((rows // 2, width), panel.dtype)] * 2,
        in_specs=[pl.BlockSpec(memory_space=pltpu.SMEM)] * 2 + [pl.BlockSpec(memory_space=pltpu.VMEM)],
        out_specs=[pl.BlockSpec(memory_space=pltpu.VMEM)] * 2,
        compiler_params=pltpu.CompilerParams(vmem_limit_bytes=4 << 20),
        name="mask",
    )(pos, pattern, panel)


PANEL = (
    ((0, 0, 0), (0, 0, 1)),
    ((0, 3, 0), (0, 3, 1)),
    ((0, 1, 0), (0, 1, 1)),
    ((1, 0, 0), (1, 0, 1)),
    ((0, 2, 0), (1, 3, 0), (1, 3, 1)),
    ((0, 2, 1), (1, 1, 0), (1, 1, 1)),
    ((1, 2, 0), (1, 2, 1)),
)
SLAB = (
    (0, 0, 4, 0, 0, 0, 0),
    (1, 0, 4, 1, 0, 0, 0),
    (2, 0, 4, 0, 0, 3, 0),
    (3, 0, 4, 0, 0, 1, 0),
    (4, 0, 2, 0, 0, 2, 0),
    (4, 2, 4, 1, 0, 3, 0),
    (5, 0, 2, 0, 0, 2, 2),
    (5, 2, 4, 1, 0, 1, 0),
    (6, 0, 4, 1, 0, 2, 0),
    (7, 0, 4, 0, 1, 0, 0),
    (7, 4, 4, 1, 1, 0, 0),
    (7, 8, 4, 0, 1, 3, 0),
    (7, 12, 4, 0, 1, 1, 0),
    (7, 16, 2, 0, 1, 2, 0),
    (7, 18, 4, 1, 1, 3, 0),
    (7, 22, 2, 0, 1, 2, 2),
    (7, 24, 4, 1, 1, 1, 0),
    (8, 0, 4, 1, 1, 2, 0),
)
NA, NB = 7, 9


def quantize(tiles, o_ref):
    codes = []
    for t, v in enumerate(tiles):
        top = jnp.max(jnp.abs(v), axis=0, keepdims=True)
        code = jnp.ceil(jnp.log2(jnp.maximum(top, TINY)) * STEPS)
        v = jnp.round(v * (jnp.exp2(code * (-1.0 / STEPS)) * LEVELS)).astype(jnp.int32)
        o_ref[pl.ds(t * BS, BS), :] = v.astype(jnp.int16)
        codes.append(code)
    codes = jnp.concatenate(codes * (PAD // len(codes)), axis=0)
    o_ref[pl.ds(len(tiles) * BS, PAD), :] = codes.astype(jnp.int32).astype(jnp.int16)


def scales(v_ref, tiles):
    codes = v_ref[pl.ds(tiles * BS, PAD), :].astype(jnp.int32).astype(jnp.float32)
    return jnp.exp2(codes * (1.0 / STEPS)) * (1.0 / LEVELS)


def values(v_ref, at):
    return v_ref[at, :].astype(jnp.int32).astype(jnp.float32)


def product(chunks, pos_ref, owner_ref, a_refs, b_refs, a_s):
    y, c, p, x, layer = pos_ref[0], pos_ref[1], pos_ref[2], pos_ref[4], pos_ref[5]
    for ref, group in zip(a_refs, PANEL):
        for n, (batch, rel, i) in enumerate(group):
            col = (2 * ((p + batch) % 2) + (c + i) % 2) * 4 + (x + rel) % 4
            for u in range(2):
                block = owner_ref[2 * col + u]
                row = block // 4
                at = ((row + c) % 2) * 16 + ((row // 2 + 4 - y) % 4) * 4 + block % 4
                at = pl.ds(pl.multiple_of(at * BS, BS), BS)
                for k, chunk in enumerate(chunks):
                    rows = pl.ds(pl.multiple_of(((layer + chunk) % 4) * BS, BS), BS)
                    a_s[pl.ds(k * BS, BS), at] = ref[n, rows, pl.ds(u * BS, BS)]
    for g in range(2):
        total = None
        for array, first, blocks, half, core, rel, i in SLAB:
            if half != g:
                continue
            at = pl.ds((core * 16 + rel * 4 + i) * BS, blocks * BS)
            b = b_refs[array][pl.ds(first, blocks)].reshape(blocks * BS, 4 * BS)
            part = jnp.dot(a_s[:, at], b, preferred_element_type=jnp.float32)
            total = part if total is None else total + part
        yield g, total


def far_kernel(pos_ref, owner_ref, *refs):
    a_refs, b_refs, (o_ref, a_s) = refs[:NA], refs[NA:NA + NB], refs[NA + NB:]
    tiles = []
    for g, total in product((2,), pos_ref, owner_ref, a_refs, b_refs, a_s):
        tiles += [total[:, n * BS:(n + 1) * BS] for n in range(4)]
    quantize(tiles, o_ref)


def rest_kernel(pos_ref, owner_ref, *refs):
    a_refs, b_refs, (*o_refs, a_s) = refs[:NA], refs[NA:NA + NB], refs[NA + NB:]
    for g, total in product((0, 1, 3), pos_ref, owner_ref, a_refs, b_refs, a_s):
        for k, o_ref in enumerate(o_refs):
            o_ref[g] = total[k * BS:(k + 1) * BS]


def matmul(kernel, name, chunks, out_shape, pos, owner, a, b):
    depth = 32 * BS
    return pl.pallas_call(
        kernel,
        out_shape=out_shape,
        in_specs=[pl.BlockSpec(memory_space=pltpu.SMEM)] * 2 + [pl.BlockSpec(memory_space=pltpu.VMEM)] * (NA + NB),
        out_specs=[pl.BlockSpec(memory_space=pltpu.VMEM)] * len(out_shape),
        scratch_shapes=[pltpu.VMEM((chunks * BS, depth), jnp.bfloat16)],
        compiler_params=pltpu.CompilerParams(vmem_limit_bytes=24 << 20),
        cost_estimate=pl.CostEstimate(flops=2 * chunks * BS * 8 * BS * depth, bytes_accessed=1 << 20, transcendentals=0),
        name=name,
    )(pos, owner, *a, *b)


def add_kernel(pos_ref, own1_ref, own3_ref, got_ref, o1_ref, o3_ref):
    scale = scales(got_ref, 8)
    for core, own_ref, o_ref in ((0, own1_ref, o1_ref), (1, own3_ref, o3_ref)):
        mine = pos_ref[1] == core
        tiles = []
        for t in range(8):
            got = values(got_ref, pl.ds(t * BS, BS)) * scale[t:t + 1, :]
            tiles.append(own_ref[t // 4, :, pl.ds((t % 4) * BS, BS)] + jnp.where(mine, got, 0.0))
        quantize(tiles, o_ref)


def add(pos, own1, own3, got):
    return pl.pallas_call(
        add_kernel,
        out_shape=[jax.ShapeDtypeStruct((8 * BS + PAD, BS), jnp.int16)] * 2,
        in_specs=[pl.BlockSpec(memory_space=pltpu.SMEM)] + [pl.BlockSpec(memory_space=pltpu.VMEM)] * 3,
        out_specs=[pl.BlockSpec(memory_space=pltpu.VMEM)] * 2,
        compiler_params=pltpu.CompilerParams(vmem_limit_bytes=8 << 20),
        name="add",
    )(pos, own1, own3, got)


def total_kernel(pos_ref, own_ref, *refs):
    v_refs, o_refs = refs[:2], refs[2:]
    other = (pos_ref[1] + pos_ref[3]) % 2
    found = [scales(v_ref, 8) for v_ref in v_refs]
    for g, o_ref in zip((other, 1 - other), o_refs):
        for n in range(4):
            at = pl.ds(pl.multiple_of((g * 4 + n) * BS, BS), BS)
            total = own_ref[g, :, pl.ds(n * BS, BS)]
            for v_ref, scale in zip(v_refs, found):
                total = total + values(v_ref, at) * jnp.where(g == 0, scale[n:n + 1, :], scale[4 + n:5 + n, :])
            o_ref[:, pl.ds(n * BS, BS)] = total.astype(jnp.bfloat16)


def total(pos, own, v):
    return pl.pallas_call(
        total_kernel,
        out_shape=[jax.ShapeDtypeStruct((BS, 4 * BS), jnp.bfloat16)] * 2,
        in_specs=[pl.BlockSpec(memory_space=pltpu.SMEM)] + [pl.BlockSpec(memory_space=pltpu.VMEM)] * 3,
        out_specs=[pl.BlockSpec(memory_space=pltpu.VMEM)] * 2,
        compiler_params=pltpu.CompilerParams(vmem_limit_bytes=4 << 20),
        name="total",
    )(pos, own, *v)


def place_kernel(pos_ref, pat_ref, first_ref, second_ref, o_ref):
    q = pos_ref[3]
    for b, ref in ((q, first_ref), (1 - q, second_ref)):
        for n in range(4):
            keep = pat_ref[b, n].astype(jnp.float32).astype(jnp.bfloat16)
            cols = pl.ds(n * BS, BS)
            o_ref[pl.ds(pl.multiple_of(b * BS, BS), BS), cols] = ref[:, cols] * keep


def place(pos, pattern, first, second):
    return pl.pallas_call(
        place_kernel,
        out_shape=jax.ShapeDtypeStruct((2 * BS, 4 * BS), jnp.bfloat16),
        in_specs=[pl.BlockSpec(memory_space=pltpu.SMEM)] * 2 + [pl.BlockSpec(memory_space=pltpu.VMEM)] * 2,
        out_specs=pl.BlockSpec(memory_space=pltpu.VMEM),
        compiler_params=pltpu.CompilerParams(vmem_limit_bytes=4 << 20),
        name="place",
    )(pos, pattern, first, second)


def shards(panel, in_pattern, slab, owner, out_pattern):
    row, col = lax.axis_index("row"), lax.axis_index("col")
    zl = col // 4
    pos = jnp.stack([row // 2, row % 2, zl // 2, zl % 2, col % 4, lax.axis_index("layer")])
    cat = lambda *v: jnp.concatenate(v, axis=0)
    own = slab[0]
    with jax.named_scope("round0"):
        pair = send(own, lambda y, c, zl, x, zh: (y, c, zl ^ 1, x, zh))
        first, second = mask(pos, panel[:, 0, :], in_pattern[:, 0, :].T)
        first = send(first, lambda y, c, zl, x, zh: (y, zl % 2, zl - zl % 2 + c, x, zh))
        second = send(second, lambda y, c, zl, x, zh: (y, 1 - zl % 2, zl - zl % 2 + c, x, zh))
        first, second, pair, late = lax.optimization_barrier((first, second, pair, own))
        near = jnp.stack([first, second])
    with jax.named_scope("round1"):
        far = send(near, lambda y, c, zl, x, zh: (y, c, zl ^ 2, x, zh))
        a1p, a1m = to_x(near, 1), to_x(near, -1)
        b1p, b1m = to_y(late, 1), to_y(late, -1)
        far, a1p, a1m, b1p, b1m = lax.optimization_barrier((far, a1p, a1m, b1p, b1m))
    with jax.named_scope("round2"):
        a2p, a2m = to_x(cat(a1p[:1], far), 1), to_x(cat(a1m[1:], far), -1)
        b2p, b2m = to_y(cat(b1p[:2], pair), 1), to_y(cat(b1m[2:], pair), -1)
        a2p, a2m, b2p, b2m = lax.optimization_barrier((a2p, a2m, b2p, b2m))
    with jax.named_scope("round3"):
        even = row % 2 == 0
        hand_a, hand_b = jnp.where(even, a2p[1:], a2m[1:]), jnp.where(even, b2p[2:], b2m[2:])
        a3 = send(hand_a, lambda y, c, zl, x, zh: (y, c, zl, (x + 1 - 2 * c) % 4, zh))
        b3 = send(hand_b, lambda y, c, zl, x, zh: ((y + 1 - 2 * c) % 4, c, zl, x, zh))
        b3x = send(hand_b, lambda y, c, zl, x, zh: ((y + 1 - 2 * c) % 4, 1 - c, zl, x, zh))
        swap = to_core(cat(late, pair, b1p, b1m, b2p, b2m))
    a = (near, a1p, a1m, far, a2p, a2m, a3)
    b = (late, pair, b1p, b1m, b2p, b2m, b3, swap, b3x)
    far_shape = [jax.ShapeDtypeStruct((8 * BS + PAD, BS), jnp.int16)]
    rest_shape = [jax.ShapeDtypeStruct((2, BS, 4 * BS), jnp.float32)] * 3
    got, = matmul(far_kernel, "matmul_far", 1, far_shape, pos, owner[0], a, b)
    with jax.named_scope("layer_far"):
        got = send(got, lambda y, c, zl, x, zh: (y, c, zl, x, (zh + 1 - 2 * c) % 4))
    own_part, part1, part3 = matmul(rest_kernel, "matmul_rest", 3, rest_shape, pos, owner[0], a, b)
    part1, part3 = add(pos, part1, part3, got)
    with jax.named_scope("layer_sums"):
        got1, got3 = to_layer(part1, 1), to_layer(part3, -1)
    first, second = total(pos, own_part, (got1, got3))
    with jax.named_scope("product_pair"):
        first = send(first, lambda y, c, zl, x, zh: (y, zl % 2, zl - zl % 2 + c, x, zh))
        second = send(second, lambda y, c, zl, x, zh: (y, zl % 2, zl - zl % 2 + 1 - c, x, zh))
    return place(pos, out_pattern, first, second)


def solution(mesh):
    in_specs = (
        P("row", "layer", "col"),
        P("row", "layer", "col"),
        P("layer", "row", None, "col"),
        P("layer", None),
        P(("row", "layer"), "col"),
    )
    out_specs = P(("row", "layer"), "col")
    return jax.shard_map(shards, mesh=mesh, in_specs=in_specs, out_specs=out_specs, check_vma=False)
```

```python
import itertools

import jax
import jax.numpy as jnp
from jax import lax
from jax.experimental import pallas as pl
from jax.experimental.pallas import tpu as pltpu
from jax.sharding import PartitionSpec as P

AXES = ("row", "col", "layer")
BS = 128
LEVELS = 32700.0
TINY = 1e-33
STEPS = 8.0
PAD = 16


def moves(f):
    pairs = []
    for y, c, zl, x, zh in itertools.product(range(4), range(2), range(4), range(4), range(4)):
        y2, c2, zl2, x2, zh2 = f(y, c, zl, x, zh)
        pairs.append((((y * 2 + c) * 16 + zl * 4 + x) * 4 + zh, ((y2 * 2 + c2) * 16 + zl2 * 4 + x2) * 4 + zh2))
    return pairs


def send(v, f):
    return lax.ppermute(v, AXES, moves(f))


def to_x(v, d):
    return send(v, lambda y, c, zl, x, zh: (y, c, zl, (x + d) % 4, zh))


def to_y(v, d):
    return send(v, lambda y, c, zl, x, zh: ((y + d) % 4, c, zl, x, zh))


def to_layer(v, d):
    return send(v, lambda y, c, zl, x, zh: (y, c, zl, x, (zh + d) % 4))


def to_core(v):
    return send(v, lambda y, c, zl, x, zh: (y, 1 - c, zl, x, zh))


def mask_kernel(pos_ref, pat_ref, x_ref, first_ref, second_ref):
    q = pos_ref[3]
    for h, o_ref in ((q, first_ref), (1 - q, second_ref)):
        for b in range(o_ref.shape[0] // BS):
            for j in range(x_ref.shape[1] // BS):
                block = 2 * b + h
                keep = pat_ref[j, block].astype(jnp.float32).astype(jnp.bfloat16)
                cols = pl.ds(j * BS, BS)
                o_ref[pl.ds(b * BS, BS), cols] = x_ref[pl.ds(pl.multiple_of(block * BS, BS), BS), cols] * keep


def mask(pos, panel, pattern):
    rows, width = panel.shape
    return pl.pallas_call(
        mask_kernel,
        out_shape=[jax.ShapeDtypeStruct((rows // 2, width), panel.dtype)] * 2,
        in_specs=[pl.BlockSpec(memory_space=pltpu.SMEM)] * 2 + [pl.BlockSpec(memory_space=pltpu.VMEM)],
        out_specs=[pl.BlockSpec(memory_space=pltpu.VMEM)] * 2,
        compiler_params=pltpu.CompilerParams(vmem_limit_bytes=4 << 20),
        name="mask",
    )(pos, pattern, panel)


PANEL = (
    ((0, 0, 0), (0, 0, 1)),
    ((0, 3, 0), (0, 3, 1)),
    ((0, 1, 0), (0, 1, 1)),
    ((1, 0, 0), (1, 0, 1)),
    ((0, 2, 0), (1, 3, 0), (1, 3, 1)),
    ((0, 2, 1), (1, 1, 0), (1, 1, 1)),
    ((1, 2, 0), (1, 2, 1)),
)
SLAB = (
    (0, 0, 4, 0, 0, 0, 0),
    (1, 0, 4, 1, 0, 0, 0),
    (2, 0, 4, 0, 0, 3, 0),
    (3, 0, 4, 0, 0, 1, 0),
    (4, 0, 2, 0, 0, 2, 0),
    (4, 2, 4, 1, 0, 3, 0),
    (5, 0, 2, 0, 0, 2, 2),
    (5, 2, 4, 1, 0, 1, 0),
    (6, 0, 4, 1, 0, 2, 0),
    (7, 0, 4, 0, 1, 0, 0),
    (7, 4, 4, 1, 1, 0, 0),
    (7, 8, 4, 0, 1, 3, 0),
    (7, 12, 4, 0, 1, 1, 0),
    (8, 0, 2, 0, 1, 2, 0),
    (8, 2, 4, 1, 1, 3, 0),
    (8, 6, 2, 0, 1, 2, 2),
    (8, 8, 4, 1, 1, 1, 0),
    (9, 0, 4, 1, 1, 2, 0),
)
NA, NB = 7, 10


def quantize(tiles, o_ref):
    codes = []
    for t, v in enumerate(tiles):
        top = jnp.max(jnp.abs(v), axis=0, keepdims=True)
        code = jnp.ceil(jnp.log2(jnp.maximum(top, TINY)) * STEPS)
        v = jnp.round(v * (jnp.exp2(code * (-1.0 / STEPS)) * LEVELS)).astype(jnp.int32)
        o_ref[pl.ds(t * BS, BS), :] = v.astype(jnp.int16)
        codes.append(code)
    codes = jnp.concatenate(codes * (PAD // len(codes)), axis=0)
    o_ref[pl.ds(len(tiles) * BS, PAD), :] = codes.astype(jnp.int32).astype(jnp.int16)


def scales(v_ref, tiles):
    codes = v_ref[pl.ds(tiles * BS, PAD), :].astype(jnp.int32).astype(jnp.float32)
    return jnp.exp2(codes * (1.0 / STEPS)) * (1.0 / LEVELS)


def values(v_ref, at):
    return v_ref[at, :].astype(jnp.int32).astype(jnp.float32)


def product(chunks, pos_ref, owner_ref, a_refs, b_refs, a_s):
    y, c, p, x, layer = pos_ref[0], pos_ref[1], pos_ref[2], pos_ref[4], pos_ref[5]
    for ref, group in zip(a_refs, PANEL):
        for n, (batch, rel, i) in enumerate(group):
            col = (2 * ((p + batch) % 2) + (c + i) % 2) * 4 + (x + rel) % 4
            for u in range(2):
                block = owner_ref[2 * col + u]
                row = block // 4
                at = ((row + c) % 2) * 16 + ((row // 2 + 4 - y) % 4) * 4 + block % 4
                at = pl.ds(pl.multiple_of(at * BS, BS), BS)
                for k, chunk in enumerate(chunks):
                    rows = pl.ds(pl.multiple_of(((layer + chunk) % 4) * BS, BS), BS)
                    a_s[pl.ds(k * BS, BS), at] = ref[n, rows, pl.ds(u * BS, BS)]
    for g in range(2):
        total = None
        for array, first, blocks, half, core, rel, i in SLAB:
            if half != g:
                continue
            at = pl.ds((core * 16 + rel * 4 + i) * BS, blocks * BS)
            b = b_refs[array][pl.ds(first, blocks)].reshape(blocks * BS, 4 * BS)
            part = jnp.dot(a_s[:, at], b, preferred_element_type=jnp.float32)
            total = part if total is None else total + part
        yield g, total


def far_kernel(pos_ref, owner_ref, *refs):
    a_refs, b_refs, (o_ref, a_s) = refs[:NA], refs[NA:NA + NB], refs[NA + NB:]
    tiles = []
    for g, total in product((2,), pos_ref, owner_ref, a_refs, b_refs, a_s):
        tiles += [total[:, n * BS:(n + 1) * BS] for n in range(4)]
    quantize(tiles, o_ref)


def rest_kernel(pos_ref, owner_ref, *refs):
    a_refs, b_refs, (*o_refs, a_s) = refs[:NA], refs[NA:NA + NB], refs[NA + NB:]
    for g, total in product((0, 1, 3), pos_ref, owner_ref, a_refs, b_refs, a_s):
        for k, o_ref in enumerate(o_refs):
            o_ref[g] = total[k * BS:(k + 1) * BS]


def matmul(kernel, name, chunks, out_shape, pos, owner, a, b):
    depth = 32 * BS
    return pl.pallas_call(
        kernel,
        out_shape=out_shape,
        in_specs=[pl.BlockSpec(memory_space=pltpu.SMEM)] * 2 + [pl.BlockSpec(memory_space=pltpu.VMEM)] * (NA + NB),
        out_specs=[pl.BlockSpec(memory_space=pltpu.VMEM)] * len(out_shape),
        scratch_shapes=[pltpu.VMEM((chunks * BS, depth), jnp.bfloat16)],
        compiler_params=pltpu.CompilerParams(vmem_limit_bytes=24 << 20),
        cost_estimate=pl.CostEstimate(flops=2 * chunks * BS * 8 * BS * depth, bytes_accessed=1 << 20, transcendentals=0),
        name=name,
    )(pos, owner, *a, *b)


def add_kernel(pos_ref, own1_ref, own3_ref, got_ref, o1_ref, o3_ref):
    scale = scales(got_ref, 8)
    for core, own_ref, o_ref in ((0, own1_ref, o1_ref), (1, own3_ref, o3_ref)):
        mine = pos_ref[1] == core
        tiles = []
        for t in range(8):
            got = values(got_ref, pl.ds(t * BS, BS)) * scale[t:t + 1, :]
            tiles.append(own_ref[t // 4, :, pl.ds((t % 4) * BS, BS)] + jnp.where(mine, got, 0.0))
        quantize(tiles, o_ref)


def add(pos, own1, own3, got):
    return pl.pallas_call(
        add_kernel,
        out_shape=[jax.ShapeDtypeStruct((8 * BS + PAD, BS), jnp.int16)] * 2,
        in_specs=[pl.BlockSpec(memory_space=pltpu.SMEM)] + [pl.BlockSpec(memory_space=pltpu.VMEM)] * 3,
        out_specs=[pl.BlockSpec(memory_space=pltpu.VMEM)] * 2,
        compiler_params=pltpu.CompilerParams(vmem_limit_bytes=8 << 20),
        name="add",
    )(pos, own1, own3, got)


def total_kernel(pos_ref, own_ref, *refs):
    v_refs, o_refs = refs[:2], refs[2:]
    other = (pos_ref[1] + pos_ref[3]) % 2
    found = [scales(v_ref, 8) for v_ref in v_refs]
    for g, o_ref in zip((other, 1 - other), o_refs):
        for n in range(4):
            at = pl.ds(pl.multiple_of((g * 4 + n) * BS, BS), BS)
            total = own_ref[g, :, pl.ds(n * BS, BS)]
            for v_ref, scale in zip(v_refs, found):
                total = total + values(v_ref, at) * jnp.where(g == 0, scale[n:n + 1, :], scale[4 + n:5 + n, :])
            o_ref[:, pl.ds(n * BS, BS)] = total.astype(jnp.bfloat16)


def total(pos, own, v):
    return pl.pallas_call(
        total_kernel,
        out_shape=[jax.ShapeDtypeStruct((BS, 4 * BS), jnp.bfloat16)] * 2,
        in_specs=[pl.BlockSpec(memory_space=pltpu.SMEM)] + [pl.BlockSpec(memory_space=pltpu.VMEM)] * 3,
        out_specs=[pl.BlockSpec(memory_space=pltpu.VMEM)] * 2,
        compiler_params=pltpu.CompilerParams(vmem_limit_bytes=4 << 20),
        name="total",
    )(pos, own, *v)


def place_kernel(pos_ref, pat_ref, first_ref, second_ref, o_ref):
    q = pos_ref[3]
    for b, ref in ((q, first_ref), (1 - q, second_ref)):
        for n in range(4):
            keep = pat_ref[b, n].astype(jnp.float32).astype(jnp.bfloat16)
            cols = pl.ds(n * BS, BS)
            o_ref[pl.ds(pl.multiple_of(b * BS, BS), BS), cols] = ref[:, cols] * keep


def place(pos, pattern, first, second):
    return pl.pallas_call(
        place_kernel,
        out_shape=jax.ShapeDtypeStruct((2 * BS, 4 * BS), jnp.bfloat16),
        in_specs=[pl.BlockSpec(memory_space=pltpu.SMEM)] * 2 + [pl.BlockSpec(memory_space=pltpu.VMEM)] * 2,
        out_specs=pl.BlockSpec(memory_space=pltpu.VMEM),
        compiler_params=pltpu.CompilerParams(vmem_limit_bytes=4 << 20),
        name="place",
    )(pos, pattern, first, second)


def shards(panel, in_pattern, slab, owner, out_pattern):
    row, col = lax.axis_index("row"), lax.axis_index("col")
    zl = col // 4
    pos = jnp.stack([row // 2, row % 2, zl // 2, zl % 2, col % 4, lax.axis_index("layer")])
    cat = lambda *v: jnp.concatenate(v, axis=0)
    own = slab[0]
    with jax.named_scope("round0"):
        pair = send(own, lambda y, c, zl, x, zh: (y, c, zl ^ 1, x, zh))
        first, second = mask(pos, panel[:, 0, :], in_pattern[:, 0, :].T)
        first = send(first, lambda y, c, zl, x, zh: (y, zl % 2, zl - zl % 2 + c, x, zh))
        second = send(second, lambda y, c, zl, x, zh: (y, 1 - zl % 2, zl - zl % 2 + c, x, zh))
        first, second, pair, late = lax.optimization_barrier((first, second, pair, own))
        near = jnp.stack([first, second])
    with jax.named_scope("round1"):
        far = send(near, lambda y, c, zl, x, zh: (y, c, zl ^ 2, x, zh))
        a1p, a1m = to_x(near, 1), to_x(near, -1)
        b1p, b1m = to_y(late, 1), to_y(late, -1)
        far, a1p, a1m, b1p, b1m = lax.optimization_barrier((far, a1p, a1m, b1p, b1m))
    with jax.named_scope("round2"):
        a2p, a2m = to_x(cat(a1p[:1], far), 1), to_x(cat(a1m[1:], far), -1)
        b2p, b2m = to_y(cat(b1p[:2], pair), 1), to_y(cat(b1m[2:], pair), -1)
        swap1 = to_core(cat(late, pair, b1p, b1m))
        a2p, a2m, b2p, b2m, swap1 = lax.optimization_barrier((a2p, a2m, b2p, b2m, swap1))
    with jax.named_scope("round3"):
        even = row % 2 == 0
        hand_a, hand_b = jnp.where(even, a2p[1:], a2m[1:]), jnp.where(even, b2p[2:], b2m[2:])
        a3 = send(hand_a, lambda y, c, zl, x, zh: (y, c, zl, (x + 1 - 2 * c) % 4, zh))
        b3 = send(hand_b, lambda y, c, zl, x, zh: ((y + 1 - 2 * c) % 4, c, zl, x, zh))
        b3x = send(hand_b, lambda y, c, zl, x, zh: ((y + 1 - 2 * c) % 4, 1 - c, zl, x, zh))
        swap2 = to_core(cat(b2p, b2m))
    a = (near, a1p, a1m, far, a2p, a2m, a3)
    b = (late, pair, b1p, b1m, b2p, b2m, b3, swap1, swap2, b3x)
    far_shape = [jax.ShapeDtypeStruct((8 * BS + PAD, BS), jnp.int16)]
    rest_shape = [jax.ShapeDtypeStruct((2, BS, 4 * BS), jnp.float32)] * 3
    got, = matmul(far_kernel, "matmul_far", 1, far_shape, pos, owner[0], a, b)
    with jax.named_scope("layer_far"):
        got = send(got, lambda y, c, zl, x, zh: (y, c, zl, x, (zh + 1 - 2 * c) % 4))
    own_part, part1, part3 = matmul(rest_kernel, "matmul_rest", 3, rest_shape, pos, owner[0], a, b)
    part1, part3 = add(pos, part1, part3, got)
    with jax.named_scope("layer_sums"):
        got1, got3 = to_layer(part1, 1), to_layer(part3, -1)
    first, second = total(pos, own_part, (got1, got3))
    with jax.named_scope("product_pair"):
        first = send(first, lambda y, c, zl, x, zh: (y, zl % 2, zl - zl % 2 + c, x, zh))
        second = send(second, lambda y, c, zl, x, zh: (y, zl % 2, zl - zl % 2 + 1 - c, x, zh))
    return place(pos, out_pattern, first, second)


def solution(mesh):
    in_specs = (
        P("row", "layer", "col"),
        P("row", "layer", "col"),
        P("layer", "row", None, "col"),
        P("layer", None),
        P(("row", "layer"), "col"),
    )
    out_specs = P(("row", "layer"), "col")
    return jax.shard_map(shards, mesh=mesh, in_specs=in_specs, out_specs=out_specs, check_vma=False)
```

```python
import itertools

import jax
import jax.numpy as jnp
from jax import lax
from jax.experimental import pallas as pl
from jax.experimental.pallas import tpu as pltpu
from jax.sharding import PartitionSpec as P

AXES = ("row", "col", "layer")
BS = 128
LEVELS = 32700.0
TINY = 1e-33
STEPS = 8.0
PAD = 16


def moves(f):
    pairs = []
    for y, c, zl, x, zh in itertools.product(range(4), range(2), range(4), range(4), range(4)):
        y2, c2, zl2, x2, zh2 = f(y, c, zl, x, zh)
        pairs.append((((y * 2 + c) * 16 + zl * 4 + x) * 4 + zh, ((y2 * 2 + c2) * 16 + zl2 * 4 + x2) * 4 + zh2))
    return pairs


def send(v, f):
    return lax.ppermute(v, AXES, moves(f))


def to_x(v, d):
    return send(v, lambda y, c, zl, x, zh: (y, c, zl, (x + d) % 4, zh))


def to_y(v, d):
    return send(v, lambda y, c, zl, x, zh: ((y + d) % 4, c, zl, x, zh))


def to_layer(v, d):
    return send(v, lambda y, c, zl, x, zh: (y, c, zl, x, (zh + d) % 4))


def to_core(v):
    return send(v, lambda y, c, zl, x, zh: (y, 1 - c, zl, x, zh))


def mask_kernel(pos_ref, pat_ref, x_ref, first_ref, second_ref):
    q = pos_ref[3]
    for h, o_ref in ((q, first_ref), (1 - q, second_ref)):
        for b in range(o_ref.shape[0] // BS):
            for j in range(x_ref.shape[1] // BS):
                block = 2 * b + h
                keep = pat_ref[j, block].astype(jnp.float32).astype(jnp.bfloat16)
                cols = pl.ds(j * BS, BS)
                o_ref[pl.ds(b * BS, BS), cols] = x_ref[pl.ds(pl.multiple_of(block * BS, BS), BS), cols] * keep


def mask(pos, panel, pattern):
    rows, width = panel.shape
    return pl.pallas_call(
        mask_kernel,
        out_shape=[jax.ShapeDtypeStruct((rows // 2, width), panel.dtype)] * 2,
        in_specs=[pl.BlockSpec(memory_space=pltpu.SMEM)] * 2 + [pl.BlockSpec(memory_space=pltpu.VMEM)],
        out_specs=[pl.BlockSpec(memory_space=pltpu.VMEM)] * 2,
        compiler_params=pltpu.CompilerParams(vmem_limit_bytes=4 << 20),
        name="mask",
    )(pos, pattern, panel)


PANEL = (
    ((0, 0, 0), (0, 0, 1)),
    ((0, 3, 0), (0, 3, 1)),
    ((0, 1, 0), (0, 1, 1)),
    ((1, 0, 0), (1, 0, 1)),
    ((0, 2, 0), (1, 3, 0), (1, 3, 1)),
    ((0, 2, 1), (1, 1, 0), (1, 1, 1)),
    ((1, 2, 0),),
    ((1, 2, 1),),
)
SLAB = (
    (0, 0, 4, 0, 0, 0, 0),
    (1, 0, 4, 1, 0, 0, 0),
    (2, 0, 4, 0, 0, 3, 0),
    (3, 0, 4, 0, 0, 1, 0),
    (4, 0, 2, 0, 0, 2, 0),
    (4, 2, 4, 1, 0, 3, 0),
    (5, 0, 2, 0, 0, 2, 2),
    (5, 2, 4, 1, 0, 1, 0),
    (6, 0, 2, 1, 0, 2, 0),
    (7, 0, 2, 1, 0, 2, 2),
    (8, 0, 4, 0, 1, 0, 0),
    (8, 4, 4, 1, 1, 0, 0),
    (9, 0, 4, 0, 1, 3, 0),
    (9, 4, 4, 0, 1, 1, 0),
    (9, 8, 2, 0, 1, 2, 0),
    (9, 10, 4, 1, 1, 3, 0),
    (9, 14, 2, 0, 1, 2, 2),
    (9, 16, 4, 1, 1, 1, 0),
    (10, 0, 2, 1, 1, 2, 0),
    (10, 2, 2, 1, 1, 2, 2),
)
NA, NB = 8, 11


def quantize(tiles, o_ref):
    codes = []
    for t, v in enumerate(tiles):
        top = jnp.max(jnp.abs(v), axis=0, keepdims=True)
        code = jnp.ceil(jnp.log2(jnp.maximum(top, TINY)) * STEPS)
        v = jnp.round(v * (jnp.exp2(code * (-1.0 / STEPS)) * LEVELS)).astype(jnp.int32)
        o_ref[pl.ds(t * BS, BS), :] = v.astype(jnp.int16)
        codes.append(code)
    codes = jnp.concatenate(codes * (PAD // len(codes)), axis=0)
    o_ref[pl.ds(len(tiles) * BS, PAD), :] = codes.astype(jnp.int32).astype(jnp.int16)


def scales(v_ref, tiles):
    codes = v_ref[pl.ds(tiles * BS, PAD), :].astype(jnp.int32).astype(jnp.float32)
    return jnp.exp2(codes * (1.0 / STEPS)) * (1.0 / LEVELS)


def values(v_ref, at):
    return v_ref[at, :].astype(jnp.int32).astype(jnp.float32)


def product(chunks, pos_ref, owner_ref, a_refs, b_refs, a_s):
    y, c, p, x, layer = pos_ref[0], pos_ref[1], pos_ref[2], pos_ref[4], pos_ref[5]
    for ref, group in zip(a_refs, PANEL):
        for n, (batch, rel, i) in enumerate(group):
            col = (2 * ((p + batch) % 2) + (c + i) % 2) * 4 + (x + rel) % 4
            for u in range(2):
                block = owner_ref[2 * col + u]
                row = block // 4
                at = ((row + c) % 2) * 16 + ((row // 2 + 4 - y) % 4) * 4 + block % 4
                at = pl.ds(pl.multiple_of(at * BS, BS), BS)
                for k, chunk in enumerate(chunks):
                    rows = pl.ds(pl.multiple_of(((layer + chunk) % 4) * BS, BS), BS)
                    a_s[pl.ds(k * BS, BS), at] = ref[n, rows, pl.ds(u * BS, BS)]
    for g in range(2):
        total = None
        for array, first, blocks, half, core, rel, i in SLAB:
            if half != g:
                continue
            at = pl.ds((core * 16 + rel * 4 + i) * BS, blocks * BS)
            b = b_refs[array][pl.ds(first, blocks)].reshape(blocks * BS, 4 * BS)
            part = jnp.dot(a_s[:, at], b, preferred_element_type=jnp.float32)
            total = part if total is None else total + part
        yield g, total


def far_kernel(pos_ref, owner_ref, *refs):
    a_refs, b_refs, (o_ref, a_s) = refs[:NA], refs[NA:NA + NB], refs[NA + NB:]
    tiles = []
    for g, total in product((2,), pos_ref, owner_ref, a_refs, b_refs, a_s):
        tiles += [total[:, n * BS:(n + 1) * BS] for n in range(4)]
    quantize(tiles, o_ref)


def rest_kernel(pos_ref, owner_ref, *refs):
    a_refs, b_refs, (*o_refs, a_s) = refs[:NA], refs[NA:NA + NB], refs[NA + NB:]
    for g, total in product((0, 1, 3), pos_ref, owner_ref, a_refs, b_refs, a_s):
        for k, o_ref in enumerate(o_refs):
            o_ref[g] = total[k * BS:(k + 1) * BS]


def matmul(kernel, name, chunks, out_shape, pos, owner, a, b):
    depth = 32 * BS
    return pl.pallas_call(
        kernel,
        out_shape=out_shape,
        in_specs=[pl.BlockSpec(memory_space=pltpu.SMEM)] * 2 + [pl.BlockSpec(memory_space=pltpu.VMEM)] * (NA + NB),
        out_specs=[pl.BlockSpec(memory_space=pltpu.VMEM)] * len(out_shape),
        scratch_shapes=[pltpu.VMEM((chunks * BS, depth), jnp.bfloat16)],
        compiler_params=pltpu.CompilerParams(vmem_limit_bytes=24 << 20),
        cost_estimate=pl.CostEstimate(flops=2 * chunks * BS * 8 * BS * depth, bytes_accessed=1 << 20, transcendentals=0),
        name=name,
    )(pos, owner, *a, *b)


def add_kernel(pos_ref, own1_ref, own3_ref, got_ref, o1_ref, o3_ref):
    scale = scales(got_ref, 8)
    for core, own_ref, o_ref in ((0, own1_ref, o1_ref), (1, own3_ref, o3_ref)):
        mine = pos_ref[1] == core
        tiles = []
        for t in range(8):
            got = values(got_ref, pl.ds(t * BS, BS)) * scale[t:t + 1, :]
            tiles.append(own_ref[t // 4, :, pl.ds((t % 4) * BS, BS)] + jnp.where(mine, got, 0.0))
        quantize(tiles, o_ref)


def add(pos, own1, own3, got):
    return pl.pallas_call(
        add_kernel,
        out_shape=[jax.ShapeDtypeStruct((8 * BS + PAD, BS), jnp.int16)] * 2,
        in_specs=[pl.BlockSpec(memory_space=pltpu.SMEM)] + [pl.BlockSpec(memory_space=pltpu.VMEM)] * 3,
        out_specs=[pl.BlockSpec(memory_space=pltpu.VMEM)] * 2,
        compiler_params=pltpu.CompilerParams(vmem_limit_bytes=8 << 20),
        name="add",
    )(pos, own1, own3, got)


def total_kernel(pos_ref, own_ref, *refs):
    v_refs, o_refs = refs[:2], refs[2:]
    other = (pos_ref[1] + pos_ref[3]) % 2
    found = [scales(v_ref, 8) for v_ref in v_refs]
    for g, o_ref in zip((other, 1 - other), o_refs):
        for n in range(4):
            at = pl.ds(pl.multiple_of((g * 4 + n) * BS, BS), BS)
            total = own_ref[g, :, pl.ds(n * BS, BS)]
            for v_ref, scale in zip(v_refs, found):
                total = total + values(v_ref, at) * jnp.where(g == 0, scale[n:n + 1, :], scale[4 + n:5 + n, :])
            o_ref[:, pl.ds(n * BS, BS)] = total.astype(jnp.bfloat16)


def total(pos, own, v):
    return pl.pallas_call(
        total_kernel,
        out_shape=[jax.ShapeDtypeStruct((BS, 4 * BS), jnp.bfloat16)] * 2,
        in_specs=[pl.BlockSpec(memory_space=pltpu.SMEM)] + [pl.BlockSpec(memory_space=pltpu.VMEM)] * 3,
        out_specs=[pl.BlockSpec(memory_space=pltpu.VMEM)] * 2,
        compiler_params=pltpu.CompilerParams(vmem_limit_bytes=4 << 20),
        name="total",
    )(pos, own, *v)


def place_kernel(pos_ref, pat_ref, first_ref, second_ref, o_ref):
    q = pos_ref[3]
    for b, ref in ((q, first_ref), (1 - q, second_ref)):
        for n in range(4):
            keep = pat_ref[b, n].astype(jnp.float32).astype(jnp.bfloat16)
            cols = pl.ds(n * BS, BS)
            o_ref[pl.ds(pl.multiple_of(b * BS, BS), BS), cols] = ref[:, cols] * keep


def place(pos, pattern, first, second):
    return pl.pallas_call(
        place_kernel,
        out_shape=jax.ShapeDtypeStruct((2 * BS, 4 * BS), jnp.bfloat16),
        in_specs=[pl.BlockSpec(memory_space=pltpu.SMEM)] * 2 + [pl.BlockSpec(memory_space=pltpu.VMEM)] * 2,
        out_specs=pl.BlockSpec(memory_space=pltpu.VMEM),
        compiler_params=pltpu.CompilerParams(vmem_limit_bytes=4 << 20),
        name="place",
    )(pos, pattern, first, second)


def shards(panel, in_pattern, slab, owner, out_pattern):
    row, col = lax.axis_index("row"), lax.axis_index("col")
    zl = col // 4
    pos = jnp.stack([row // 2, row % 2, zl // 2, zl % 2, col % 4, lax.axis_index("layer")])
    cat = lambda *v: jnp.concatenate(v, axis=0)
    own = slab[0]
    first, second = mask(pos, panel[:, 0, :], in_pattern[:, 0, :].T)
    with jax.named_scope("round0"):
        first = send(first, lambda y, c, zl, x, zh: (y, zl % 2, zl - zl % 2 + c, x, zh))
        second = send(second, lambda y, c, zl, x, zh: (y, 1 - zl % 2, zl - zl % 2 + c, x, zh))
        pair = send(own, lambda y, c, zl, x, zh: (y, c, zl ^ 1, x, zh))
        b1p, b1m = to_y(own, 1), to_y(own, -1)
        first, second, pair, b1p, b1m = lax.optimization_barrier((first, second, pair, b1p, b1m))
        near = jnp.stack([first, second])
    with jax.named_scope("round1"):
        far = send(near, lambda y, c, zl, x, zh: (y, c, zl ^ 2, x, zh))
        a1p, a1m = to_x(near, 1), to_x(near, -1)
        b2p, b2m = to_y(cat(b1p[:2], pair), 1), to_y(cat(b1m[2:], pair), -1)
        far, a1p, a1m, b2p, b2m = lax.optimization_barrier((far, a1p, a1m, b2p, b2m))
    with jax.named_scope("round2"):
        a2p, a2m = to_x(cat(a1p[:1], far), 1), to_x(cat(a1m[1:], far), -1)
        b3p, b3m = to_y(b2p[2:4], 1), to_y(b2m[4:], -1)
        c12 = to_core(cat(b1p, b1m, b2p, b2m))
        a2p, a2m, b3p, b3m, c12, late = lax.optimization_barrier((a2p, a2m, b3p, b3m, c12, pair))
    with jax.named_scope("round3"):
        a3p, a3m = to_x(a2p[1:2], 1), to_x(a2m[2:], -1)
        c3, c0 = to_core(cat(b3p, b3m)), to_core(cat(own, late))
    a = (near, a1p, a1m, far, a2p, a2m, a3p, a3m)
    b = (own, pair, b1p, b1m, b2p, b2m, b3p, b3m, c0, c12, c3)
    far_shape = [jax.ShapeDtypeStruct((8 * BS + PAD, BS), jnp.int16)]
    rest_shape = [jax.ShapeDtypeStruct((2, BS, 4 * BS), jnp.float32)] * 3
    got, = matmul(far_kernel, "matmul_far", 1, far_shape, pos, owner[0], a, b)
    with jax.named_scope("layer_far"):
        got = send(got, lambda y, c, zl, x, zh: (y, c, zl, x, (zh + 1 - 2 * c) % 4))
    own_part, part1, part3 = matmul(rest_kernel, "matmul_rest", 3, rest_shape, pos, owner[0], a, b)
    part1, part3 = add(pos, part1, part3, got)
    with jax.named_scope("layer_sums"):
        got1, got3 = to_layer(part1, 1), to_layer(part3, -1)
    first, second = total(pos, own_part, (got1, got3))
    with jax.named_scope("product_pair"):
        first = send(first, lambda y, c, zl, x, zh: (y, zl % 2, zl - zl % 2 + c, x, zh))
        second = send(second, lambda y, c, zl, x, zh: (y, zl % 2, zl - zl % 2 + 1 - c, x, zh))
    return place(pos, out_pattern, first, second)


def solution(mesh):
    in_specs = (
        P("row", "layer", "col"),
        P("row", "layer", "col"),
        P("layer", "row", None, "col"),
        P("layer", None),
        P(("row", "layer"), "col"),
    )
    out_specs = P(("row", "layer"), "col")
    return jax.shard_map(shards, mesh=mesh, in_specs=in_specs, out_specs=out_specs, check_vma=False)
```

```python
import itertools

import jax
import jax.numpy as jnp
from jax import lax
from jax.experimental import pallas as pl
from jax.experimental.pallas import tpu as pltpu
from jax.sharding import PartitionSpec as P

AXES = ("row", "col", "layer")
BS = 128
LEVELS = 32700.0
TINY = 1e-33
STEPS = 8.0
PAD = 16


def moves(f):
    pairs = []
    for y, c, zl, x, zh in itertools.product(range(4), range(2), range(4), range(4), range(4)):
        y2, c2, zl2, x2, zh2 = f(y, c, zl, x, zh)
        pairs.append((((y * 2 + c) * 16 + zl * 4 + x) * 4 + zh, ((y2 * 2 + c2) * 16 + zl2 * 4 + x2) * 4 + zh2))
    return pairs


def send(v, f):
    return lax.ppermute(v, AXES, moves(f))


def to_x(v, d):
    return send(v, lambda y, c, zl, x, zh: (y, c, zl, (x + d) % 4, zh))


def to_y(v, d):
    return send(v, lambda y, c, zl, x, zh: ((y + d) % 4, c, zl, x, zh))


def to_layer(v, d):
    return send(v, lambda y, c, zl, x, zh: (y, c, zl, x, (zh + d) % 4))


def to_core(v):
    return send(v, lambda y, c, zl, x, zh: (y, 1 - c, zl, x, zh))


def mask_kernel(pos_ref, pat_ref, x_ref, first_ref, second_ref):
    q = pos_ref[3]
    for h, o_ref in ((q, first_ref), (1 - q, second_ref)):
        for b in range(o_ref.shape[0] // BS):
            for j in range(x_ref.shape[1] // BS):
                block = 2 * b + h
                keep = pat_ref[j, block].astype(jnp.float32).astype(jnp.bfloat16)
                cols = pl.ds(j * BS, BS)
                o_ref[pl.ds(b * BS, BS), cols] = x_ref[pl.ds(pl.multiple_of(block * BS, BS), BS), cols] * keep


def mask(pos, panel, pattern):
    rows, width = panel.shape
    return pl.pallas_call(
        mask_kernel,
        out_shape=[jax.ShapeDtypeStruct((rows // 2, width), panel.dtype)] * 2,
        in_specs=[pl.BlockSpec(memory_space=pltpu.SMEM)] * 2 + [pl.BlockSpec(memory_space=pltpu.VMEM)],
        out_specs=[pl.BlockSpec(memory_space=pltpu.VMEM)] * 2,
        compiler_params=pltpu.CompilerParams(vmem_limit_bytes=4 << 20),
        name="mask",
    )(pos, pattern, panel)


PANEL = (
    ((0, 0, 0), (0, 0, 1)),
    ((0, 3, 0), (0, 3, 1)),
    ((0, 1, 0), (0, 1, 1)),
    ((1, 0, 0), (1, 0, 1)),
    ((0, 2, 0), (1, 3, 0), (1, 3, 1)),
    ((0, 2, 1), (1, 1, 0), (1, 1, 1)),
    ((1, 2, 0),),
    ((1, 2, 1),),
)
SLAB = (
    (0, 0, 4, 0, 0, 0, 0),
    (1, 0, 4, 1, 0, 0, 0),
    (2, 0, 4, 0, 0, 3, 0),
    (3, 0, 4, 0, 0, 1, 0),
    (4, 0, 4, 1, 0, 3, 0),
    (5, 0, 4, 1, 0, 1, 0),
    (6, 0, 2, 0, 0, 2, 0),
    (6, 2, 2, 1, 0, 2, 0),
    (7, 0, 2, 0, 0, 2, 2),
    (7, 2, 2, 1, 0, 2, 2),
    (8, 0, 4, 0, 1, 3, 0),
    (8, 4, 4, 0, 1, 1, 0),
    (8, 8, 4, 1, 1, 3, 0),
    (8, 12, 4, 1, 1, 1, 0),
    (9, 0, 4, 0, 1, 0, 0),
    (9, 4, 4, 1, 1, 0, 0),
    (9, 8, 2, 0, 1, 2, 0),
    (9, 10, 2, 1, 1, 2, 0),
    (9, 12, 2, 0, 1, 2, 2),
    (9, 14, 2, 1, 1, 2, 2),
)
NA, NB = 8, 10


def quantize(tiles, o_ref):
    codes = []
    for t, v in enumerate(tiles):
        top = jnp.max(jnp.abs(v), axis=0, keepdims=True)
        code = jnp.ceil(jnp.log2(jnp.maximum(top, TINY)) * STEPS)
        v = jnp.round(v * (jnp.exp2(code * (-1.0 / STEPS)) * LEVELS)).astype(jnp.int32)
        o_ref[pl.ds(t * BS, BS), :] = v.astype(jnp.int16)
        codes.append(code)
    codes = jnp.concatenate(codes * (PAD // len(codes)), axis=0)
    o_ref[pl.ds(len(tiles) * BS, PAD), :] = codes.astype(jnp.int32).astype(jnp.int16)


def scales(v_ref, tiles):
    codes = v_ref[pl.ds(tiles * BS, PAD), :].astype(jnp.int32).astype(jnp.float32)
    return jnp.exp2(codes * (1.0 / STEPS)) * (1.0 / LEVELS)


def values(v_ref, at):
    return v_ref[at, :].astype(jnp.int32).astype(jnp.float32)


def product(chunks, pos_ref, owner_ref, a_refs, b_refs, a_s):
    y, c, p, x, layer = pos_ref[0], pos_ref[1], pos_ref[2], pos_ref[4], pos_ref[5]
    for ref, group in zip(a_refs, PANEL):
        for n, (batch, rel, i) in enumerate(group):
            col = (2 * ((p + batch) % 2) + (c + i) % 2) * 4 + (x + rel) % 4
            for u in range(2):
                block = owner_ref[2 * col + u]
                row = block // 4
                at = ((row + c) % 2) * 16 + ((row // 2 + 4 - y) % 4) * 4 + block % 4
                at = pl.ds(pl.multiple_of(at * BS, BS), BS)
                for k, chunk in enumerate(chunks):
                    rows = pl.ds(pl.multiple_of(((layer + chunk) % 4) * BS, BS), BS)
                    a_s[pl.ds(k * BS, BS), at] = ref[n, rows, pl.ds(u * BS, BS)]
    for g in range(2):
        total = None
        for array, first, blocks, half, core, rel, i in SLAB:
            if half != g:
                continue
            at = pl.ds((core * 16 + rel * 4 + i) * BS, blocks * BS)
            b = b_refs[array][pl.ds(first, blocks)].reshape(blocks * BS, 4 * BS)
            part = jnp.dot(a_s[:, at], b, preferred_element_type=jnp.float32)
            total = part if total is None else total + part
        yield g, total


def far_kernel(pos_ref, owner_ref, *refs):
    a_refs, b_refs, (o_ref, a_s) = refs[:NA], refs[NA:NA + NB], refs[NA + NB:]
    tiles = []
    for g, total in product((2,), pos_ref, owner_ref, a_refs, b_refs, a_s):
        tiles += [total[:, n * BS:(n + 1) * BS] for n in range(4)]
    quantize(tiles, o_ref)


def rest_kernel(pos_ref, owner_ref, *refs):
    a_refs, b_refs, (*o_refs, a_s) = refs[:NA], refs[NA:NA + NB], refs[NA + NB:]
    for g, total in product((0, 1, 3), pos_ref, owner_ref, a_refs, b_refs, a_s):
        for k, o_ref in enumerate(o_refs):
            o_ref[g] = total[k * BS:(k + 1) * BS]


def matmul(kernel, name, chunks, out_shape, pos, owner, a, b):
    depth = 32 * BS
    return pl.pallas_call(
        kernel,
        out_shape=out_shape,
        in_specs=[pl.BlockSpec(memory_space=pltpu.SMEM)] * 2 + [pl.BlockSpec(memory_space=pltpu.VMEM)] * (NA + NB),
        out_specs=[pl.BlockSpec(memory_space=pltpu.VMEM)] * len(out_shape),
        scratch_shapes=[pltpu.VMEM((chunks * BS, depth), jnp.bfloat16)],
        compiler_params=pltpu.CompilerParams(vmem_limit_bytes=24 << 20),
        cost_estimate=pl.CostEstimate(flops=2 * chunks * BS * 8 * BS * depth, bytes_accessed=1 << 20, transcendentals=0),
        name=name,
    )(pos, owner, *a, *b)


def add_kernel(pos_ref, own1_ref, own3_ref, got_ref, o1_ref, o3_ref):
    scale = scales(got_ref, 8)
    for core, own_ref, o_ref in ((0, own1_ref, o1_ref), (1, own3_ref, o3_ref)):
        mine = pos_ref[1] == core
        tiles = []
        for t in range(8):
            got = values(got_ref, pl.ds(t * BS, BS)) * scale[t:t + 1, :]
            tiles.append(own_ref[t // 4, :, pl.ds((t % 4) * BS, BS)] + jnp.where(mine, got, 0.0))
        quantize(tiles, o_ref)


def add(pos, own1, own3, got):
    return pl.pallas_call(
        add_kernel,
        out_shape=[jax.ShapeDtypeStruct((8 * BS + PAD, BS), jnp.int16)] * 2,
        in_specs=[pl.BlockSpec(memory_space=pltpu.SMEM)] + [pl.BlockSpec(memory_space=pltpu.VMEM)] * 3,
        out_specs=[pl.BlockSpec(memory_space=pltpu.VMEM)] * 2,
        compiler_params=pltpu.CompilerParams(vmem_limit_bytes=8 << 20),
        name="add",
    )(pos, own1, own3, got)


def total_kernel(pos_ref, own_ref, *refs):
    v_refs, o_refs = refs[:2], refs[2:]
    other = (pos_ref[1] + pos_ref[3]) % 2
    found = [scales(v_ref, 8) for v_ref in v_refs]
    for g, o_ref in zip((other, 1 - other), o_refs):
        for n in range(4):
            at = pl.ds(pl.multiple_of((g * 4 + n) * BS, BS), BS)
            total = own_ref[g, :, pl.ds(n * BS, BS)]
            for v_ref, scale in zip(v_refs, found):
                total = total + values(v_ref, at) * jnp.where(g == 0, scale[n:n + 1, :], scale[4 + n:5 + n, :])
            o_ref[:, pl.ds(n * BS, BS)] = total.astype(jnp.bfloat16)


def total(pos, own, v):
    return pl.pallas_call(
        total_kernel,
        out_shape=[jax.ShapeDtypeStruct((BS, 4 * BS), jnp.bfloat16)] * 2,
        in_specs=[pl.BlockSpec(memory_space=pltpu.SMEM)] + [pl.BlockSpec(memory_space=pltpu.VMEM)] * 3,
        out_specs=[pl.BlockSpec(memory_space=pltpu.VMEM)] * 2,
        compiler_params=pltpu.CompilerParams(vmem_limit_bytes=4 << 20),
        name="total",
    )(pos, own, *v)


def place_kernel(pos_ref, pat_ref, first_ref, second_ref, o_ref):
    q = pos_ref[3]
    for b, ref in ((q, first_ref), (1 - q, second_ref)):
        for n in range(4):
            keep = pat_ref[b, n].astype(jnp.float32).astype(jnp.bfloat16)
            cols = pl.ds(n * BS, BS)
            o_ref[pl.ds(pl.multiple_of(b * BS, BS), BS), cols] = ref[:, cols] * keep


def place(pos, pattern, first, second):
    return pl.pallas_call(
        place_kernel,
        out_shape=jax.ShapeDtypeStruct((2 * BS, 4 * BS), jnp.bfloat16),
        in_specs=[pl.BlockSpec(memory_space=pltpu.SMEM)] * 2 + [pl.BlockSpec(memory_space=pltpu.VMEM)] * 2,
        out_specs=pl.BlockSpec(memory_space=pltpu.VMEM),
        compiler_params=pltpu.CompilerParams(vmem_limit_bytes=4 << 20),
        name="place",
    )(pos, pattern, first, second)


def shards(panel, in_pattern, slab, owner, out_pattern):
    row, col = lax.axis_index("row"), lax.axis_index("col")
    zl = col // 4
    pos = jnp.stack([row // 2, row % 2, zl // 2, zl % 2, col % 4, lax.axis_index("layer")])
    cat = lambda *v: jnp.concatenate(v, axis=0)
    own = slab[0]
    first, second = mask(pos, panel[:, 0, :], in_pattern[:, 0, :].T)
    with jax.named_scope("round0"):
        first = send(first, lambda y, c, zl, x, zh: (y, zl % 2, zl - zl % 2 + c, x, zh))
        second = send(second, lambda y, c, zl, x, zh: (y, 1 - zl % 2, zl - zl % 2 + c, x, zh))
        pair = send(own, lambda y, c, zl, x, zh: (y, c, zl ^ 1, x, zh))
        b1p, b1m = to_y(own, 1), to_y(own, -1)
        first, second, pair, b1p, b1m = lax.optimization_barrier((first, second, pair, b1p, b1m))
        near = jnp.stack([first, second])
    with jax.named_scope("round1"):
        far = send(near, lambda y, c, zl, x, zh: (y, c, zl ^ 2, x, zh))
        a1p, a1m = to_x(near, 1), to_x(near, -1)
        b2p, b2m = to_y(pair, 1), to_y(pair, -1)
        far, a1p, a1m, b2p, b2m = lax.optimization_barrier((far, a1p, a1m, b2p, b2m))
    with jax.named_scope("round2"):
        a2p, a2m = to_x(cat(a1p[:1], far), 1), to_x(cat(a1m[1:], far), -1)
        b3p, b3m = to_y(cat(b1p[:2], b2p[:2]), 1), to_y(cat(b1m[2:], b2m[2:]), -1)
        c12 = to_core(cat(b1p, b1m, b2p, b2m))
        a2p, a2m, b3p, b3m, c12, late = lax.optimization_barrier((a2p, a2m, b3p, b3m, c12, pair))
    with jax.named_scope("round3"):
        a3p, a3m = to_x(a2p[1:2], 1), to_x(a2m[2:], -1)
        c03 = to_core(cat(own, late, b3p, b3m))
    a = (near, a1p, a1m, far, a2p, a2m, a3p, a3m)
    b = (own, pair, b1p, b1m, b2p, b2m, b3p, b3m, c12, c03)
    far_shape = [jax.ShapeDtypeStruct((8 * BS + PAD, BS), jnp.int16)]
    rest_shape = [jax.ShapeDtypeStruct((2, BS, 4 * BS), jnp.float32)] * 3
    got, = matmul(far_kernel, "matmul_far", 1, far_shape, pos, owner[0], a, b)
    with jax.named_scope("layer_far"):
        got = send(got, lambda y, c, zl, x, zh: (y, c, zl, x, (zh + 1 - 2 * c) % 4))
    own_part, part1, part3 = matmul(rest_kernel, "matmul_rest", 3, rest_shape, pos, owner[0], a, b)
    part1, part3 = add(pos, part1, part3, got)
    with jax.named_scope("layer_sums"):
        got1, got3 = to_layer(part1, 1), to_layer(part3, -1)
    first, second = total(pos, own_part, (got1, got3))
    with jax.named_scope("product_pair"):
        first = send(first, lambda y, c, zl, x, zh: (y, zl % 2, zl - zl % 2 + c, x, zh))
        second = send(second, lambda y, c, zl, x, zh: (y, zl % 2, zl - zl % 2 + 1 - c, x, zh))
    return place(pos, out_pattern, first, second)


def solution(mesh):
    in_specs = (
        P("row", "layer", "col"),
        P("row", "layer", "col"),
        P("layer", "row", None, "col"),
        P("layer", None),
        P(("row", "layer"), "col"),
    )
    out_specs = P(("row", "layer"), "col")
    return jax.shard_map(shards, mesh=mesh, in_specs=in_specs, out_specs=out_specs, check_vma=False)
```

```python
import itertools

import jax
import jax.numpy as jnp
from jax import lax
from jax.experimental import pallas as pl
from jax.experimental.pallas import tpu as pltpu
from jax.sharding import PartitionSpec as P

AXES = ("row", "col", "layer")
BS = 128
LEVELS = 32700.0
TINY = 1e-33
STEPS = 8.0
PAD = 16


def moves(f):
    pairs = []
    for y, c, zl, x, zh in itertools.product(range(4), range(2), range(4), range(4), range(4)):
        y2, c2, zl2, x2, zh2 = f(y, c, zl, x, zh)
        pairs.append((((y * 2 + c) * 16 + zl * 4 + x) * 4 + zh, ((y2 * 2 + c2) * 16 + zl2 * 4 + x2) * 4 + zh2))
    return pairs


def send(v, f):
    return lax.ppermute(v, AXES, moves(f))


def to_x(v, d):
    return send(v, lambda y, c, zl, x, zh: (y, c, zl, (x + d) % 4, zh))


def to_y(v, d):
    return send(v, lambda y, c, zl, x, zh: ((y + d) % 4, c, zl, x, zh))


def to_layer(v, d):
    return send(v, lambda y, c, zl, x, zh: (y, c, zl, x, (zh + d) % 4))


def to_core(v):
    return send(v, lambda y, c, zl, x, zh: (y, 1 - c, zl, x, zh))


def mask_kernel(pos_ref, pat_ref, x_ref, first_ref, second_ref):
    q = pos_ref[3]
    for h, o_ref in ((q, first_ref), (1 - q, second_ref)):
        for b in range(o_ref.shape[0] // BS):
            for j in range(x_ref.shape[1] // BS):
                block = 2 * b + h
                keep = pat_ref[j, block].astype(jnp.float32).astype(jnp.bfloat16)
                cols = pl.ds(j * BS, BS)
                o_ref[pl.ds(b * BS, BS), cols] = x_ref[pl.ds(pl.multiple_of(block * BS, BS), BS), cols] * keep


def mask(pos, panel, pattern):
    rows, width = panel.shape
    return pl.pallas_call(
        mask_kernel,
        out_shape=[jax.ShapeDtypeStruct((rows // 2, width), panel.dtype)] * 2,
        in_specs=[pl.BlockSpec(memory_space=pltpu.SMEM)] * 2 + [pl.BlockSpec(memory_space=pltpu.VMEM)],
        out_specs=[pl.BlockSpec(memory_space=pltpu.VMEM)] * 2,
        compiler_params=pltpu.CompilerParams(vmem_limit_bytes=4 << 20),
        name="mask",
    )(pos, pattern, panel)


PANEL = (
    ((0, 0, 0), (0, 0, 1)),
    ((0, 3, 0), (0, 3, 1)),
    ((0, 1, 0), (0, 1, 1)),
    ((1, 0, 0), (1, 0, 1)),
    ((0, 2, 0), (1, 3, 0), (1, 3, 1)),
    ((0, 2, 1), (1, 1, 0), (1, 1, 1)),
    ((1, 2, 0), (1, 2, 1)),
)
SLAB = (
    (0, 0, 4, 0, 0, 0, 0),
    (1, 0, 4, 1, 0, 0, 0),
    (2, 0, 4, 0, 0, 3, 0),
    (3, 0, 4, 0, 0, 1, 0),
    (4, 0, 4, 1, 0, 3, 0),
    (5, 0, 4, 1, 0, 1, 0),
    (6, 0, 4, 0, 0, 2, 0),
    (6, 4, 4, 1, 0, 2, 0),
    (7, 0, 4, 0, 1, 3, 0),
    (7, 4, 4, 0, 1, 1, 0),
    (7, 8, 4, 1, 1, 3, 0),
    (7, 12, 4, 1, 1, 1, 0),
    (8, 0, 4, 0, 1, 0, 0),
    (8, 4, 4, 1, 1, 0, 0),
    (8, 8, 4, 0, 1, 2, 0),
    (8, 12, 4, 1, 1, 2, 0),
)
NA, NB = 7, 9


def quantize(tiles, o_ref):
    codes = []
    for t, v in enumerate(tiles):
        top = jnp.max(jnp.abs(v), axis=0, keepdims=True)
        code = jnp.ceil(jnp.log2(jnp.maximum(top, TINY)) * STEPS)
        v = jnp.round(v * (jnp.exp2(code * (-1.0 / STEPS)) * LEVELS)).astype(jnp.int32)
        o_ref[pl.ds(t * BS, BS), :] = v.astype(jnp.int16)
        codes.append(code)
    codes = jnp.concatenate(codes * (PAD // len(codes)), axis=0)
    o_ref[pl.ds(len(tiles) * BS, PAD), :] = codes.astype(jnp.int32).astype(jnp.int16)


def scales(v_ref, tiles):
    codes = v_ref[pl.ds(tiles * BS, PAD), :].astype(jnp.int32).astype(jnp.float32)
    return jnp.exp2(codes * (1.0 / STEPS)) * (1.0 / LEVELS)


def values(v_ref, at):
    return v_ref[at, :].astype(jnp.int32).astype(jnp.float32)


def product(chunks, pos_ref, owner_ref, a_refs, b_refs, a_s):
    y, c, p, x, layer = pos_ref[0], pos_ref[1], pos_ref[2], pos_ref[4], pos_ref[5]
    for ref, group in zip(a_refs, PANEL):
        for n, (batch, rel, i) in enumerate(group):
            col = (2 * ((p + batch) % 2) + (c + i) % 2) * 4 + (x + rel) % 4
            for u in range(2):
                block = owner_ref[2 * col + u]
                row = block // 4
                at = ((row + c) % 2) * 16 + ((row // 2 + 4 - y) % 4) * 4 + block % 4
                at = pl.ds(pl.multiple_of(at * BS, BS), BS)
                for k, chunk in enumerate(chunks):
                    rows = pl.ds(pl.multiple_of(((layer + chunk) % 4) * BS, BS), BS)
                    a_s[pl.ds(k * BS, BS), at] = ref[n, rows, pl.ds(u * BS, BS)]
    for g in range(2):
        total = None
        for array, first, blocks, half, core, rel, i in SLAB:
            if half != g:
                continue
            at = pl.ds((core * 16 + rel * 4 + i) * BS, blocks * BS)
            b = b_refs[array][pl.ds(first, blocks)].reshape(blocks * BS, 4 * BS)
            part = jnp.dot(a_s[:, at], b, preferred_element_type=jnp.float32)
            total = part if total is None else total + part
        yield g, total


def far_kernel(pos_ref, owner_ref, *refs):
    a_refs, b_refs, (o_ref, a_s) = refs[:NA], refs[NA:NA + NB], refs[NA + NB:]
    tiles = []
    for g, total in product((2,), pos_ref, owner_ref, a_refs, b_refs, a_s):
        tiles += [total[:, n * BS:(n + 1) * BS] for n in range(4)]
    quantize(tiles, o_ref)


def rest_kernel(pos_ref, owner_ref, *refs):
    a_refs, b_refs, (*o_refs, a_s) = refs[:NA], refs[NA:NA + NB], refs[NA + NB:]
    for g, total in product((0, 1, 3), pos_ref, owner_ref, a_refs, b_refs, a_s):
        for k, o_ref in enumerate(o_refs):
            o_ref[g] = total[k * BS:(k + 1) * BS]


def matmul(kernel, name, chunks, out_shape, pos, owner, a, b):
    depth = 32 * BS
    return pl.pallas_call(
        kernel,
        out_shape=out_shape,
        in_specs=[pl.BlockSpec(memory_space=pltpu.SMEM)] * 2 + [pl.BlockSpec(memory_space=pltpu.VMEM)] * (NA + NB),
        out_specs=[pl.BlockSpec(memory_space=pltpu.VMEM)] * len(out_shape),
        scratch_shapes=[pltpu.VMEM((chunks * BS, depth), jnp.bfloat16)],
        compiler_params=pltpu.CompilerParams(vmem_limit_bytes=24 << 20),
        cost_estimate=pl.CostEstimate(flops=2 * chunks * BS * 8 * BS * depth, bytes_accessed=1 << 20, transcendentals=0),
        name=name,
    )(pos, owner, *a, *b)


def add_kernel(pos_ref, own1_ref, own3_ref, got_ref, o1_ref, o3_ref):
    scale = scales(got_ref, 8)
    for core, own_ref, o_ref in ((0, own1_ref, o1_ref), (1, own3_ref, o3_ref)):
        mine = pos_ref[1] == core
        tiles = []
        for t in range(8):
            got = values(got_ref, pl.ds(t * BS, BS)) * scale[t:t + 1, :]
            tiles.append(own_ref[t // 4, :, pl.ds((t % 4) * BS, BS)] + jnp.where(mine, got, 0.0))
        quantize(tiles, o_ref)


def add(pos, own1, own3, got):
    return pl.pallas_call(
        add_kernel,
        out_shape=[jax.ShapeDtypeStruct((8 * BS + PAD, BS), jnp.int16)] * 2,
        in_specs=[pl.BlockSpec(memory_space=pltpu.SMEM)] + [pl.BlockSpec(memory_space=pltpu.VMEM)] * 3,
        out_specs=[pl.BlockSpec(memory_space=pltpu.VMEM)] * 2,
        compiler_params=pltpu.CompilerParams(vmem_limit_bytes=8 << 20),
        name="add",
    )(pos, own1, own3, got)


def total_kernel(pos_ref, own_ref, *refs):
    v_refs, o_refs = refs[:2], refs[2:]
    other = (pos_ref[1] + pos_ref[3]) % 2
    found = [scales(v_ref, 8) for v_ref in v_refs]
    for g, o_ref in zip((other, 1 - other), o_refs):
        for n in range(4):
            at = pl.ds(pl.multiple_of((g * 4 + n) * BS, BS), BS)
            total = own_ref[g, :, pl.ds(n * BS, BS)]
            for v_ref, scale in zip(v_refs, found):
                total = total + values(v_ref, at) * jnp.where(g == 0, scale[n:n + 1, :], scale[4 + n:5 + n, :])
            o_ref[:, pl.ds(n * BS, BS)] = total.astype(jnp.bfloat16)


def total(pos, own, v):
    return pl.pallas_call(
        total_kernel,
        out_shape=[jax.ShapeDtypeStruct((BS, 4 * BS), jnp.bfloat16)] * 2,
        in_specs=[pl.BlockSpec(memory_space=pltpu.SMEM)] + [pl.BlockSpec(memory_space=pltpu.VMEM)] * 3,
        out_specs=[pl.BlockSpec(memory_space=pltpu.VMEM)] * 2,
        compiler_params=pltpu.CompilerParams(vmem_limit_bytes=4 << 20),
        name="total",
    )(pos, own, *v)


def place_kernel(pos_ref, pat_ref, first_ref, second_ref, o_ref):
    q = pos_ref[3]
    for b, ref in ((q, first_ref), (1 - q, second_ref)):
        for n in range(4):
            keep = pat_ref[b, n].astype(jnp.float32).astype(jnp.bfloat16)
            cols = pl.ds(n * BS, BS)
            o_ref[pl.ds(pl.multiple_of(b * BS, BS), BS), cols] = ref[:, cols] * keep


def place(pos, pattern, first, second):
    return pl.pallas_call(
        place_kernel,
        out_shape=jax.ShapeDtypeStruct((2 * BS, 4 * BS), jnp.bfloat16),
        in_specs=[pl.BlockSpec(memory_space=pltpu.SMEM)] * 2 + [pl.BlockSpec(memory_space=pltpu.VMEM)] * 2,
        out_specs=pl.BlockSpec(memory_space=pltpu.VMEM),
        compiler_params=pltpu.CompilerParams(vmem_limit_bytes=4 << 20),
        name="place",
    )(pos, pattern, first, second)


def shards(panel, in_pattern, slab, owner, out_pattern):
    row, col = lax.axis_index("row"), lax.axis_index("col")
    zl = col // 4
    pos = jnp.stack([row // 2, row % 2, zl // 2, zl % 2, col % 4, lax.axis_index("layer")])
    cat = lambda *v: jnp.concatenate(v, axis=0)
    own = slab[0]
    first, second = mask(pos, panel[:, 0, :], in_pattern[:, 0, :].T)
    with jax.named_scope("round0"):
        first = send(first, lambda y, c, zl, x, zh: (y, zl % 2, zl - zl % 2 + c, x, zh))
        second = send(second, lambda y, c, zl, x, zh: (y, 1 - zl % 2, zl - zl % 2 + c, x, zh))
        pair = send(own, lambda y, c, zl, x, zh: (y, c, zl ^ 1, x, zh))
        b1p, b1m = to_y(own, 1), to_y(own, -1)
        first, second, pair, b1p, b1m = lax.optimization_barrier((first, second, pair, b1p, b1m))
        near = jnp.stack([first, second])
    with jax.named_scope("round1"):
        far = send(near, lambda y, c, zl, x, zh: (y, c, zl ^ 2, x, zh))
        a1p, a1m = to_x(near, 1), to_x(near, -1)
        b2p, b2m = to_y(pair, 1), to_y(pair, -1)
        far, a1p, a1m, b2p, b2m = lax.optimization_barrier((far, a1p, a1m, b2p, b2m))
    even = row % 2 == 0
    with jax.named_scope("round2"):
        a2p, a2m = to_x(cat(a1p[:1], far), 1), to_x(cat(a1m[1:], far), -1)
        b3 = send(jnp.where(even, cat(b1p, b2p), cat(b1m, b2m)), lambda y, c, zl, x, zh: ((y + 1 - 2 * c) % 4, c, zl, x, zh))
        c12 = to_core(cat(b1p, b1m, b2p, b2m))
        a2p, a2m, b3, c12, late = lax.optimization_barrier((a2p, a2m, b3, c12, pair))
    with jax.named_scope("round3"):
        a3 = send(jnp.where(even, a2p[1:], a2m[1:]), lambda y, c, zl, x, zh: (y, c, zl, (x + 1 - 2 * c) % 4, zh))
        c03 = to_core(cat(own, late, b3))
    a = (near, a1p, a1m, far, a2p, a2m, a3)
    b = (own, pair, b1p, b1m, b2p, b2m, b3, c12, c03)
    far_shape = [jax.ShapeDtypeStruct((8 * BS + PAD, BS), jnp.int16)]
    rest_shape = [jax.ShapeDtypeStruct((2, BS, 4 * BS), jnp.float32)] * 3
    got, = matmul(far_kernel, "matmul_far", 1, far_shape, pos, owner[0], a, b)
    with jax.named_scope("layer_far"):
        got = send(got, lambda y, c, zl, x, zh: (y, c, zl, x, (zh + 1 - 2 * c) % 4))
    own_part, part1, part3 = matmul(rest_kernel, "matmul_rest", 3, rest_shape, pos, owner[0], a, b)
    part1, part3 = add(pos, part1, part3, got)
    with jax.named_scope("layer_sums"):
        got1, got3 = to_layer(part1, 1), to_layer(part3, -1)
    first, second = total(pos, own_part, (got1, got3))
    with jax.named_scope("product_pair"):
        first = send(first, lambda y, c, zl, x, zh: (y, zl % 2, zl - zl % 2 + c, x, zh))
        second = send(second, lambda y, c, zl, x, zh: (y, zl % 2, zl - zl % 2 + 1 - c, x, zh))
    return place(pos, out_pattern, first, second)


def solution(mesh):
    in_specs = (
        P("row", "layer", "col"),
        P("row", "layer", "col"),
        P("layer", "row", None, "col"),
        P("layer", None),
        P(("row", "layer"), "col"),
    )
    out_specs = P(("row", "layer"), "col")
    return jax.shard_map(shards, mesh=mesh, in_specs=in_specs, out_specs=out_specs, check_vma=False)
```

```python
import itertools

import jax
import jax.numpy as jnp
from jax import lax
from jax.experimental import pallas as pl
from jax.experimental.pallas import tpu as pltpu
from jax.sharding import PartitionSpec as P

AXES = ("row", "col", "layer")
BS = 128
LEVELS = 32700.0
TINY = 1e-33
STEPS = 8.0
PAD = 16


def moves(f):
    pairs = []
    for y, c, zl, x, zh in itertools.product(range(4), range(2), range(4), range(4), range(4)):
        y2, c2, zl2, x2, zh2 = f(y, c, zl, x, zh)
        pairs.append((((y * 2 + c) * 16 + zl * 4 + x) * 4 + zh, ((y2 * 2 + c2) * 16 + zl2 * 4 + x2) * 4 + zh2))
    return pairs


def send(v, f):
    return lax.ppermute(v, AXES, moves(f))


def to_x(v, d):
    return send(v, lambda y, c, zl, x, zh: (y, c, zl, (x + d) % 4, zh))


def to_y(v, d):
    return send(v, lambda y, c, zl, x, zh: ((y + d) % 4, c, zl, x, zh))


def to_layer(v, d):
    return send(v, lambda y, c, zl, x, zh: (y, c, zl, x, (zh + d) % 4))


def to_core(v):
    return send(v, lambda y, c, zl, x, zh: (y, 1 - c, zl, x, zh))


def mask_kernel(pos_ref, pat_ref, x_ref, first_ref, second_ref):
    q = pos_ref[3]
    for h, o_ref in ((q, first_ref), (1 - q, second_ref)):
        for b in range(o_ref.shape[0] // BS):
            for j in range(x_ref.shape[1] // BS):
                block = 2 * b + h
                keep = pat_ref[j, block].astype(jnp.float32).astype(jnp.bfloat16)
                cols = pl.ds(j * BS, BS)
                o_ref[pl.ds(b * BS, BS), cols] = x_ref[pl.ds(pl.multiple_of(block * BS, BS), BS), cols] * keep


def mask(pos, panel, pattern):
    rows, width = panel.shape
    return pl.pallas_call(
        mask_kernel,
        out_shape=[jax.ShapeDtypeStruct((rows // 2, width), panel.dtype)] * 2,
        in_specs=[pl.BlockSpec(memory_space=pltpu.SMEM)] * 2 + [pl.BlockSpec(memory_space=pltpu.VMEM)],
        out_specs=[pl.BlockSpec(memory_space=pltpu.VMEM)] * 2,
        compiler_params=pltpu.CompilerParams(vmem_limit_bytes=4 << 20),
        name="mask",
    )(pos, pattern, panel)


PANEL = (
    ((0, 0, 0), (0, 0, 1)),
    ((0, 3, 0), (0, 3, 1)),
    ((0, 1, 0), (0, 1, 1)),
    ((1, 0, 0), (1, 0, 1)),
    ((0, 2, 0), (1, 3, 0), (1, 3, 1)),
    ((0, 2, 1), (1, 1, 0), (1, 1, 1)),
    ((1, 2, 0), (1, 2, 1)),
)
SLAB = (
    (0, 0, 4, 0, 0, 0, 0),
    (1, 0, 4, 1, 0, 0, 0),
    (2, 0, 4, 0, 0, 3, 0),
    (3, 0, 4, 0, 0, 1, 0),
    (4, 0, 4, 1, 0, 3, 0),
    (5, 0, 4, 1, 0, 1, 0),
    (6, 0, 4, 0, 0, 2, 0),
    (6, 4, 4, 1, 0, 2, 0),
    (7, 0, 4, 0, 1, 3, 0),
    (7, 4, 4, 0, 1, 1, 0),
    (7, 8, 4, 1, 1, 3, 0),
    (7, 12, 4, 1, 1, 1, 0),
    (8, 0, 4, 0, 1, 0, 0),
    (8, 4, 4, 1, 1, 0, 0),
    (8, 8, 4, 0, 1, 2, 0),
    (8, 12, 4, 1, 1, 2, 0),
)
NA, NB = 7, 9


def quantize(tiles, o_ref):
    codes = []
    for t, v in enumerate(tiles):
        top = jnp.max(jnp.abs(v), axis=0, keepdims=True)
        code = jnp.ceil(jnp.log2(jnp.maximum(top, TINY)) * STEPS)
        v = jnp.round(v * (jnp.exp2(code * (-1.0 / STEPS)) * LEVELS)).astype(jnp.int32)
        o_ref[pl.ds(t * BS, BS), :] = v.astype(jnp.int16)
        codes.append(code)
    codes = jnp.concatenate(codes * (PAD // len(codes)), axis=0)
    o_ref[pl.ds(len(tiles) * BS, PAD), :] = codes.astype(jnp.int32).astype(jnp.int16)


def scales(v_ref, tiles):
    codes = v_ref[pl.ds(tiles * BS, PAD), :].astype(jnp.int32).astype(jnp.float32)
    return jnp.exp2(codes * (1.0 / STEPS)) * (1.0 / LEVELS)


def values(v_ref, at):
    return v_ref[at, :].astype(jnp.int32).astype(jnp.float32)


def product(chunks, pos_ref, owner_ref, a_refs, b_refs, a_s):
    y, c, p, x, layer = pos_ref[0], pos_ref[1], pos_ref[2], pos_ref[4], pos_ref[5]
    for ref, group in zip(a_refs, PANEL):
        for n, (batch, rel, i) in enumerate(group):
            col = (2 * ((p + batch) % 2) + (c + i) % 2) * 4 + (x + rel) % 4
            for u in range(2):
                block = owner_ref[2 * col + u]
                row = block // 4
                at = ((row + c) % 2) * 16 + ((row // 2 + 4 - y) % 4) * 4 + block % 4
                at = pl.ds(pl.multiple_of(at * BS, BS), BS)
                for k, chunk in enumerate(chunks):
                    rows = pl.ds(pl.multiple_of(((layer + chunk) % 4) * BS, BS), BS)
                    a_s[pl.ds(k * BS, BS), at] = ref[n, rows, pl.ds(u * BS, BS)]
    for g in range(2):
        total = None
        for array, first, blocks, half, core, rel, i in SLAB:
            if half != g:
                continue
            at = pl.ds((core * 16 + rel * 4 + i) * BS, blocks * BS)
            b = b_refs[array][pl.ds(first, blocks)].reshape(blocks * BS, 4 * BS)
            part = jnp.dot(a_s[:, at], b, preferred_element_type=jnp.float32)
            total = part if total is None else total + part
        yield g, total


def far_kernel(pos_ref, owner_ref, *refs):
    a_refs, b_refs, (o_ref, a_s) = refs[:NA], refs[NA:NA + NB], refs[NA + NB:]
    tiles = []
    for g, total in product((2,), pos_ref, owner_ref, a_refs, b_refs, a_s):
        tiles += [total[:, n * BS:(n + 1) * BS] for n in range(4)]
    quantize(tiles, o_ref)


def rest_kernel(pos_ref, owner_ref, *refs):
    a_refs, b_refs, (*o_refs, a_s) = refs[:NA], refs[NA:NA + NB], refs[NA + NB:]
    for g, total in product((0, 1, 3), pos_ref, owner_ref, a_refs, b_refs, a_s):
        for k, o_ref in enumerate(o_refs):
            o_ref[g] = total[k * BS:(k + 1) * BS]


def matmul(kernel, name, chunks, out_shape, pos, owner, a, b):
    depth = 32 * BS
    return pl.pallas_call(
        kernel,
        out_shape=out_shape,
        in_specs=[pl.BlockSpec(memory_space=pltpu.SMEM)] * 2 + [pl.BlockSpec(memory_space=pltpu.VMEM)] * (NA + NB),
        out_specs=[pl.BlockSpec(memory_space=pltpu.VMEM)] * len(out_shape),
        scratch_shapes=[pltpu.VMEM((chunks * BS, depth), jnp.bfloat16)],
        compiler_params=pltpu.CompilerParams(vmem_limit_bytes=24 << 20),
        cost_estimate=pl.CostEstimate(flops=2 * chunks * BS * 8 * BS * depth, bytes_accessed=1 << 20, transcendentals=0),
        name=name,
    )(pos, owner, *a, *b)


def add_kernel(pos_ref, own1_ref, own3_ref, got_ref, o1_ref, o3_ref):
    scale = scales(got_ref, 8)
    for core, own_ref, o_ref in ((0, own1_ref, o1_ref), (1, own3_ref, o3_ref)):
        mine = pos_ref[1] == core
        tiles = []
        for t in range(8):
            got = values(got_ref, pl.ds(t * BS, BS)) * scale[t:t + 1, :]
            tiles.append(own_ref[t // 4, :, pl.ds((t % 4) * BS, BS)] + jnp.where(mine, got, 0.0))
        quantize(tiles, o_ref)


def add(pos, own1, own3, got):
    return pl.pallas_call(
        add_kernel,
        out_shape=[jax.ShapeDtypeStruct((8 * BS + PAD, BS), jnp.int16)] * 2,
        in_specs=[pl.BlockSpec(memory_space=pltpu.SMEM)] + [pl.BlockSpec(memory_space=pltpu.VMEM)] * 3,
        out_specs=[pl.BlockSpec(memory_space=pltpu.VMEM)] * 2,
        compiler_params=pltpu.CompilerParams(vmem_limit_bytes=8 << 20),
        name="add",
    )(pos, own1, own3, got)


def total_kernel(pos_ref, own_ref, *refs):
    v_refs, o_refs = refs[:2], refs[2:]
    other = (pos_ref[1] + pos_ref[3]) % 2
    found = [scales(v_ref, 8) for v_ref in v_refs]
    for g, o_ref in zip((other, 1 - other), o_refs):
        for n in range(4):
            at = pl.ds(pl.multiple_of((g * 4 + n) * BS, BS), BS)
            total = own_ref[g, :, pl.ds(n * BS, BS)]
            for v_ref, scale in zip(v_refs, found):
                total = total + values(v_ref, at) * jnp.where(g == 0, scale[n:n + 1, :], scale[4 + n:5 + n, :])
            o_ref[:, pl.ds(n * BS, BS)] = total.astype(jnp.bfloat16)


def total(pos, own, v):
    return pl.pallas_call(
        total_kernel,
        out_shape=[jax.ShapeDtypeStruct((BS, 4 * BS), jnp.bfloat16)] * 2,
        in_specs=[pl.BlockSpec(memory_space=pltpu.SMEM)] + [pl.BlockSpec(memory_space=pltpu.VMEM)] * 3,
        out_specs=[pl.BlockSpec(memory_space=pltpu.VMEM)] * 2,
        compiler_params=pltpu.CompilerParams(vmem_limit_bytes=4 << 20),
        name="total",
    )(pos, own, *v)


def place_kernel(pos_ref, pat_ref, first_ref, second_ref, o_ref):
    q = pos_ref[3]
    for b, ref in ((q, first_ref), (1 - q, second_ref)):
        for n in range(4):
            keep = pat_ref[b, n].astype(jnp.float32).astype(jnp.bfloat16)
            cols = pl.ds(n * BS, BS)
            o_ref[pl.ds(pl.multiple_of(b * BS, BS), BS), cols] = ref[:, cols] * keep


def place(pos, pattern, first, second):
    return pl.pallas_call(
        place_kernel,
        out_shape=jax.ShapeDtypeStruct((2 * BS, 4 * BS), jnp.bfloat16),
        in_specs=[pl.BlockSpec(memory_space=pltpu.SMEM)] * 2 + [pl.BlockSpec(memory_space=pltpu.VMEM)] * 2,
        out_specs=pl.BlockSpec(memory_space=pltpu.VMEM),
        compiler_params=pltpu.CompilerParams(vmem_limit_bytes=4 << 20),
        name="place",
    )(pos, pattern, first, second)


def pick_kernel(pos_ref, *refs):
    *in_refs, o_ref = refs
    half = len(in_refs) // 2
    for core, group in ((0, in_refs[:half]), (1, in_refs[half:])):

        @pl.when(pos_ref[1] == core)
        def _():
            done = 0
            for ref in group:
                count = min(ref.shape[0], o_ref.shape[0])
                o_ref[pl.ds(done, count)] = ref[pl.ds(ref.shape[0] - count, count)]
                done += count


def pick(pos, count, *v):
    return pl.pallas_call(
        pick_kernel,
        out_shape=jax.ShapeDtypeStruct((count,) + v[0].shape[1:], v[0].dtype),
        in_specs=[pl.BlockSpec(memory_space=pltpu.SMEM)] + [pl.BlockSpec(memory_space=pltpu.VMEM)] * len(v),
        out_specs=pl.BlockSpec(memory_space=pltpu.VMEM),
        compiler_params=pltpu.CompilerParams(vmem_limit_bytes=8 << 20),
        name="pick",
    )(pos, *v)


def shards(panel, in_pattern, slab, owner, out_pattern):
    row, col = lax.axis_index("row"), lax.axis_index("col")
    zl = col // 4
    pos = jnp.stack([row // 2, row % 2, zl // 2, zl % 2, col % 4, lax.axis_index("layer")])
    cat = lambda *v: jnp.concatenate(v, axis=0)
    own = slab[0]
    first, second = mask(pos, panel[:, 0, :], in_pattern[:, 0, :].T)
    with jax.named_scope("round0"):
        first = send(first, lambda y, c, zl, x, zh: (y, zl % 2, zl - zl % 2 + c, x, zh))
        second = send(second, lambda y, c, zl, x, zh: (y, 1 - zl % 2, zl - zl % 2 + c, x, zh))
        pair = send(own, lambda y, c, zl, x, zh: (y, c, zl ^ 1, x, zh))
        b1p, b1m = to_y(own, 1), to_y(own, -1)
        first, second, pair, b1p, b1m = lax.optimization_barrier((first, second, pair, b1p, b1m))
        near = jnp.stack([first, second])
    with jax.named_scope("round1"):
        far = send(near, lambda y, c, zl, x, zh: (y, c, zl ^ 2, x, zh))
        a1p, a1m = to_x(near, 1), to_x(near, -1)
        b2p, b2m = to_y(pair, 1), to_y(pair, -1)
        far, a1p, a1m, b2p, b2m = lax.optimization_barrier((far, a1p, a1m, b2p, b2m))
    with jax.named_scope("round2"):
        a2p, a2m = to_x(cat(a1p[:1], far), 1), to_x(cat(a1m[1:], far), -1)
        b3 = send(pick(pos, 8, b1p, b2p, b1m, b2m), lambda y, c, zl, x, zh: ((y + 1 - 2 * c) % 4, c, zl, x, zh))
        c12 = to_core(cat(b1p, b1m, b2p, b2m))
        a2p, a2m, b3, c12, late = lax.optimization_barrier((a2p, a2m, b3, c12, pair))
    with jax.named_scope("round3"):
        a3 = send(pick(pos, 2, a2p, a2m), lambda y, c, zl, x, zh: (y, c, zl, (x + 1 - 2 * c) % 4, zh))
        c03 = to_core(cat(own, late, b3))
    a = (near, a1p, a1m, far, a2p, a2m, a3)
    b = (own, pair, b1p, b1m, b2p, b2m, b3, c12, c03)
    far_shape = [jax.ShapeDtypeStruct((8 * BS + PAD, BS), jnp.int16)]
    rest_shape = [jax.ShapeDtypeStruct((2, BS, 4 * BS), jnp.float32)] * 3
    got, = matmul(far_kernel, "matmul_far", 1, far_shape, pos, owner[0], a, b)
    with jax.named_scope("layer_far"):
        got = send(got, lambda y, c, zl, x, zh: (y, c, zl, x, (zh + 1 - 2 * c) % 4))
    own_part, part1, part3 = matmul(rest_kernel, "matmul_rest", 3, rest_shape, pos, owner[0], a, b)
    part1, part3 = add(pos, part1, part3, got)
    with jax.named_scope("layer_sums"):
        got1, got3 = to_layer(part1, 1), to_layer(part3, -1)
    first, second = total(pos, own_part, (got1, got3))
    with jax.named_scope("product_pair"):
        first = send(first, lambda y, c, zl, x, zh: (y, zl % 2, zl - zl % 2 + c, x, zh))
        second = send(second, lambda y, c, zl, x, zh: (y, zl % 2, zl - zl % 2 + 1 - c, x, zh))
    return place(pos, out_pattern, first, second)


def solution(mesh):
    in_specs = (
        P("row", "layer", "col"),
        P("row", "layer", "col"),
        P("layer", "row", None, "col"),
        P("layer", None),
        P(("row", "layer"), "col"),
    )
    out_specs = P(("row", "layer"), "col")
    return jax.shard_map(shards, mesh=mesh, in_specs=in_specs, out_specs=out_specs, check_vma=False)
```

```python
import itertools

import jax
import jax.numpy as jnp
from jax import lax
from jax.experimental import pallas as pl
from jax.experimental.pallas import tpu as pltpu
from jax.sharding import PartitionSpec as P

AXES = ("row", "col", "layer")
BS = 128
LEVELS = 32700.0
TINY = 1e-33
STEPS = 8.0
PAD = 16


def moves(f):
    pairs = []
    for y, c, zl, x, zh in itertools.product(range(4), range(2), range(4), range(4), range(4)):
        y2, c2, zl2, x2, zh2 = f(y, c, zl, x, zh)
        pairs.append((((y * 2 + c) * 16 + zl * 4 + x) * 4 + zh, ((y2 * 2 + c2) * 16 + zl2 * 4 + x2) * 4 + zh2))
    return pairs


def send(v, f):
    return lax.ppermute(v, AXES, moves(f))


def to_x(v, d):
    return send(v, lambda y, c, zl, x, zh: (y, c, zl, (x + d) % 4, zh))


def to_y(v, d):
    return send(v, lambda y, c, zl, x, zh: ((y + d) % 4, c, zl, x, zh))


def to_layer(v, d):
    return send(v, lambda y, c, zl, x, zh: (y, c, zl, x, (zh + d) % 4))


def to_core(v):
    return send(v, lambda y, c, zl, x, zh: (y, 1 - c, zl, x, zh))


def mask_kernel(pos_ref, pat_ref, x_ref, first_ref, second_ref):
    q = pos_ref[3]
    for h, o_ref in ((q, first_ref), (1 - q, second_ref)):
        for b in range(o_ref.shape[0] // BS):
            for j in range(x_ref.shape[1] // BS):
                block = 2 * b + h
                keep = pat_ref[j, block].astype(jnp.float32).astype(jnp.bfloat16)
                cols = pl.ds(j * BS, BS)
                o_ref[pl.ds(b * BS, BS), cols] = x_ref[pl.ds(pl.multiple_of(block * BS, BS), BS), cols] * keep


def mask(pos, panel, pattern):
    rows, width = panel.shape
    return pl.pallas_call(
        mask_kernel,
        out_shape=[jax.ShapeDtypeStruct((rows // 2, width), panel.dtype)] * 2,
        in_specs=[pl.BlockSpec(memory_space=pltpu.SMEM)] * 2 + [pl.BlockSpec(memory_space=pltpu.VMEM)],
        out_specs=[pl.BlockSpec(memory_space=pltpu.VMEM)] * 2,
        compiler_params=pltpu.CompilerParams(vmem_limit_bytes=4 << 20),
        name="mask",
    )(pos, pattern, panel)


PANEL = (
    ((0, 0, 0), (0, 0, 1)),
    ((0, 3, 0), (0, 3, 1)),
    ((0, 1, 0), (0, 1, 1)),
    ((0, 2, 0), (0, 2, 1)),
    ((1, 0, 0), (1, 0, 1)),
    ((1, 3, 0), (1, 3, 1)),
    ((1, 1, 0), (1, 1, 1)),
    ((1, 2, 0), (1, 2, 1)),
)
SLAB = (
    (0, 0, 4, 0, 0, 0, 0),
    (1, 0, 4, 1, 0, 0, 0),
    (2, 0, 4, 0, 0, 3, 0),
    (3, 0, 4, 0, 0, 1, 0),
    (4, 0, 4, 1, 0, 3, 0),
    (5, 0, 4, 1, 0, 1, 0),
    (6, 0, 4, 0, 0, 2, 0),
    (6, 4, 4, 1, 0, 2, 0),
    (7, 0, 4, 0, 1, 3, 0),
    (7, 4, 4, 0, 1, 1, 0),
    (7, 8, 4, 1, 1, 3, 0),
    (7, 12, 4, 1, 1, 1, 0),
    (8, 0, 4, 0, 1, 0, 0),
    (8, 4, 4, 1, 1, 0, 0),
    (8, 8, 4, 0, 1, 2, 0),
    (8, 12, 4, 1, 1, 2, 0),
)
NA, NB = 8, 9


def quantize(tiles, o_ref):
    codes = []
    for t, v in enumerate(tiles):
        top = jnp.max(jnp.abs(v), axis=0, keepdims=True)
        code = jnp.ceil(jnp.log2(jnp.maximum(top, TINY)) * STEPS)
        v = jnp.round(v * (jnp.exp2(code * (-1.0 / STEPS)) * LEVELS)).astype(jnp.int32)
        o_ref[pl.ds(t * BS, BS), :] = v.astype(jnp.int16)
        codes.append(code)
    codes = jnp.concatenate(codes * (PAD // len(codes)), axis=0)
    o_ref[pl.ds(len(tiles) * BS, PAD), :] = codes.astype(jnp.int32).astype(jnp.int16)


def scales(v_ref, tiles):
    codes = v_ref[pl.ds(tiles * BS, PAD), :].astype(jnp.int32).astype(jnp.float32)
    return jnp.exp2(codes * (1.0 / STEPS)) * (1.0 / LEVELS)


def values(v_ref, at):
    return v_ref[at, :].astype(jnp.int32).astype(jnp.float32)


def product(chunks, pos_ref, owner_ref, a_refs, b_refs, a_s):
    y, c, p, x, layer = pos_ref[0], pos_ref[1], pos_ref[2], pos_ref[4], pos_ref[5]
    for ref, group in zip(a_refs, PANEL):
        for n, (batch, rel, i) in enumerate(group):
            col = (2 * ((p + batch) % 2) + (c + i) % 2) * 4 + (x + rel) % 4
            for u in range(2):
                block = owner_ref[2 * col + u]
                row = block // 4
                at = ((row + c) % 2) * 16 + ((row // 2 + 4 - y) % 4) * 4 + block % 4
                at = pl.ds(pl.multiple_of(at * BS, BS), BS)
                for k, chunk in enumerate(chunks):
                    rows = pl.ds(pl.multiple_of(((layer + chunk) % 4) * BS, BS), BS)
                    a_s[pl.ds(k * BS, BS), at] = ref[n, rows, pl.ds(u * BS, BS)]
    for g in range(2):
        total = None
        for array, first, blocks, half, core, rel, i in SLAB:
            if half != g:
                continue
            at = pl.ds((core * 16 + rel * 4 + i) * BS, blocks * BS)
            b = b_refs[array][pl.ds(first, blocks)].reshape(blocks * BS, 4 * BS)
            part = jnp.dot(a_s[:, at], b, preferred_element_type=jnp.float32)
            total = part if total is None else total + part
        yield g, total


def far_kernel(pos_ref, owner_ref, *refs):
    a_refs, b_refs, (o_ref, a_s) = refs[:NA], refs[NA:NA + NB], refs[NA + NB:]
    tiles = []
    for g, total in product((2,), pos_ref, owner_ref, a_refs, b_refs, a_s):
        tiles += [total[:, n * BS:(n + 1) * BS] for n in range(4)]
    quantize(tiles, o_ref)


def rest_kernel(pos_ref, owner_ref, *refs):
    a_refs, b_refs, (*o_refs, a_s) = refs[:NA], refs[NA:NA + NB], refs[NA + NB:]
    for g, total in product((0, 1, 3), pos_ref, owner_ref, a_refs, b_refs, a_s):
        for k, o_ref in enumerate(o_refs):
            o_ref[g] = total[k * BS:(k + 1) * BS]


def matmul(kernel, name, chunks, out_shape, pos, owner, a, b):
    depth = 32 * BS
    return pl.pallas_call(
        kernel,
        out_shape=out_shape,
        in_specs=[pl.BlockSpec(memory_space=pltpu.SMEM)] * 2 + [pl.BlockSpec(memory_space=pltpu.VMEM)] * (NA + NB),
        out_specs=[pl.BlockSpec(memory_space=pltpu.VMEM)] * len(out_shape),
        scratch_shapes=[pltpu.VMEM((chunks * BS, depth), jnp.bfloat16)],
        compiler_params=pltpu.CompilerParams(vmem_limit_bytes=24 << 20),
        cost_estimate=pl.CostEstimate(flops=2 * chunks * BS * 8 * BS * depth, bytes_accessed=1 << 20, transcendentals=0),
        name=name,
    )(pos, owner, *a, *b)


def add_kernel(pos_ref, own1_ref, own3_ref, got_ref, o1_ref, o3_ref):
    scale = scales(got_ref, 8)
    for core, own_ref, o_ref in ((0, own1_ref, o1_ref), (1, own3_ref, o3_ref)):
        mine = pos_ref[1] == core
        tiles = []
        for t in range(8):
            got = values(got_ref, pl.ds(t * BS, BS)) * scale[t:t + 1, :]
            tiles.append(own_ref[t // 4, :, pl.ds((t % 4) * BS, BS)] + jnp.where(mine, got, 0.0))
        quantize(tiles, o_ref)


def add(pos, own1, own3, got):
    return pl.pallas_call(
        add_kernel,
        out_shape=[jax.ShapeDtypeStruct((8 * BS + PAD, BS), jnp.int16)] * 2,
        in_specs=[pl.BlockSpec(memory_space=pltpu.SMEM)] + [pl.BlockSpec(memory_space=pltpu.VMEM)] * 3,
        out_specs=[pl.BlockSpec(memory_space=pltpu.VMEM)] * 2,
        compiler_params=pltpu.CompilerParams(vmem_limit_bytes=8 << 20),
        name="add",
    )(pos, own1, own3, got)


def total_kernel(pos_ref, own_ref, *refs):
    v_refs, o_refs = refs[:2], refs[2:]
    other = (pos_ref[1] + pos_ref[3]) % 2
    found = [scales(v_ref, 8) for v_ref in v_refs]
    for g, o_ref in zip((other, 1 - other), o_refs):
        for n in range(4):
            at = pl.ds(pl.multiple_of((g * 4 + n) * BS, BS), BS)
            total = own_ref[g, :, pl.ds(n * BS, BS)]
            for v_ref, scale in zip(v_refs, found):
                total = total + values(v_ref, at) * jnp.where(g == 0, scale[n:n + 1, :], scale[4 + n:5 + n, :])
            o_ref[:, pl.ds(n * BS, BS)] = total.astype(jnp.bfloat16)


def total(pos, own, v):
    return pl.pallas_call(
        total_kernel,
        out_shape=[jax.ShapeDtypeStruct((BS, 4 * BS), jnp.bfloat16)] * 2,
        in_specs=[pl.BlockSpec(memory_space=pltpu.SMEM)] + [pl.BlockSpec(memory_space=pltpu.VMEM)] * 3,
        out_specs=[pl.BlockSpec(memory_space=pltpu.VMEM)] * 2,
        compiler_params=pltpu.CompilerParams(vmem_limit_bytes=4 << 20),
        name="total",
    )(pos, own, *v)


def place_kernel(pos_ref, pat_ref, first_ref, second_ref, o_ref):
    q = pos_ref[3]
    for b, ref in ((q, first_ref), (1 - q, second_ref)):
        for n in range(4):
            keep = pat_ref[b, n].astype(jnp.float32).astype(jnp.bfloat16)
            cols = pl.ds(n * BS, BS)
            o_ref[pl.ds(pl.multiple_of(b * BS, BS), BS), cols] = ref[:, cols] * keep


def place(pos, pattern, first, second):
    return pl.pallas_call(
        place_kernel,
        out_shape=jax.ShapeDtypeStruct((2 * BS, 4 * BS), jnp.bfloat16),
        in_specs=[pl.BlockSpec(memory_space=pltpu.SMEM)] * 2 + [pl.BlockSpec(memory_space=pltpu.VMEM)] * 2,
        out_specs=pl.BlockSpec(memory_space=pltpu.VMEM),
        compiler_params=pltpu.CompilerParams(vmem_limit_bytes=4 << 20),
        name="place",
    )(pos, pattern, first, second)


def pick_kernel(pos_ref, *refs):
    *in_refs, o_ref = refs
    half = len(in_refs) // 2
    for core, group in ((0, in_refs[:half]), (1, in_refs[half:])):

        @pl.when(pos_ref[1] == core)
        def _():
            done = 0
            for ref in group:
                count = min(ref.shape[0], o_ref.shape[0])
                o_ref[pl.ds(done, count)] = ref[pl.ds(ref.shape[0] - count, count)]
                done += count


def pick(pos, count, *v):
    return pl.pallas_call(
        pick_kernel,
        out_shape=jax.ShapeDtypeStruct((count,) + v[0].shape[1:], v[0].dtype),
        in_specs=[pl.BlockSpec(memory_space=pltpu.SMEM)] + [pl.BlockSpec(memory_space=pltpu.VMEM)] * len(v),
        out_specs=pl.BlockSpec(memory_space=pltpu.VMEM),
        compiler_params=pltpu.CompilerParams(vmem_limit_bytes=8 << 20),
        name="pick",
    )(pos, *v)


def shards(panel, in_pattern, slab, owner, out_pattern):
    row, col = lax.axis_index("row"), lax.axis_index("col")
    zl = col // 4
    pos = jnp.stack([row // 2, row % 2, zl // 2, zl % 2, col % 4, lax.axis_index("layer")])
    cat = lambda *v: jnp.concatenate(v, axis=0)
    own = slab[0]
    first, second = mask(pos, panel[:, 0, :], in_pattern[:, 0, :].T)
    with jax.named_scope("round0"):
        first = send(first, lambda y, c, zl, x, zh: (y, zl % 2, zl - zl % 2 + c, x, zh))
        second = send(second, lambda y, c, zl, x, zh: (y, 1 - zl % 2, zl - zl % 2 + c, x, zh))
        pair = send(own, lambda y, c, zl, x, zh: (y, c, zl ^ 1, x, zh))
        b1p, b1m = to_y(own, 1), to_y(own, -1)
        first, second, pair, b1p, b1m = lax.optimization_barrier((first, second, pair, b1p, b1m))
        near = jnp.stack([first, second])
    with jax.named_scope("round1"):
        far = send(near, lambda y, c, zl, x, zh: (y, c, zl ^ 2, x, zh))
        a1p, a1m = to_x(near, 1), to_x(near, -1)
        b2p, b2m = to_y(pair, 1), to_y(pair, -1)
        a1h = send(pick(pos, 2, a1p, a1m), lambda y, c, zl, x, zh: (y, c, zl, (x + 1 - 2 * c) % 4, zh))
        far, a1p, a1m, a1h, b2p, b2m = lax.optimization_barrier((far, a1p, a1m, a1h, b2p, b2m))
    with jax.named_scope("round2"):
        a2p, a2m = to_x(far, 1), to_x(far, -1)
        b3 = send(pick(pos, 8, b1p, b2p, b1m, b2m), lambda y, c, zl, x, zh: ((y + 1 - 2 * c) % 4, c, zl, x, zh))
        c12 = to_core(cat(b1p, b1m, b2p, b2m))
        a2p, a2m, b3, c12, late = lax.optimization_barrier((a2p, a2m, b3, c12, pair))
    with jax.named_scope("round3"):
        a3 = send(pick(pos, 2, a2p, a2m), lambda y, c, zl, x, zh: (y, c, zl, (x + 1 - 2 * c) % 4, zh))
        c03 = to_core(cat(own, late, b3))
    a = (near, a1p, a1m, a1h, far, a2p, a2m, a3)
    b = (own, pair, b1p, b1m, b2p, b2m, b3, c12, c03)
    far_shape = [jax.ShapeDtypeStruct((8 * BS + PAD, BS), jnp.int16)]
    rest_shape = [jax.ShapeDtypeStruct((2, BS, 4 * BS), jnp.float32)] * 3
    got, = matmul(far_kernel, "matmul_far", 1, far_shape, pos, owner[0], a, b)
    with jax.named_scope("layer_far"):
        got = send(got, lambda y, c, zl, x, zh: (y, c, zl, x, (zh + 1 - 2 * c) % 4))
    own_part, part1, part3 = matmul(rest_kernel, "matmul_rest", 3, rest_shape, pos, owner[0], a, b)
    part1, part3 = add(pos, part1, part3, got)
    with jax.named_scope("layer_sums"):
        got1, got3 = to_layer(part1, 1), to_layer(part3, -1)
    first, second = total(pos, own_part, (got1, got3))
    with jax.named_scope("product_pair"):
        first = send(first, lambda y, c, zl, x, zh: (y, zl % 2, zl - zl % 2 + c, x, zh))
        second = send(second, lambda y, c, zl, x, zh: (y, zl % 2, zl - zl % 2 + 1 - c, x, zh))
    return place(pos, out_pattern, first, second)


def solution(mesh):
    in_specs = (
        P("row", "layer", "col"),
        P("row", "layer", "col"),
        P("layer", "row", None, "col"),
        P("layer", None),
        P(("row", "layer"), "col"),
    )
    out_specs = P(("row", "layer"), "col")
    return jax.shard_map(shards, mesh=mesh, in_specs=in_specs, out_specs=out_specs, check_vma=False)
```

```python
import itertools

import jax
import jax.numpy as jnp
from jax import lax
from jax.experimental import pallas as pl
from jax.experimental.pallas import tpu as pltpu
from jax.sharding import PartitionSpec as P

AXES = ("row", "col", "layer")
BS = 128
LEVELS = 32700.0
TINY = 1e-33
STEPS = 8.0
PAD = 16


def moves(f):
    pairs = []
    for y, c, zl, x, zh in itertools.product(range(4), range(2), range(4), range(4), range(4)):
        y2, c2, zl2, x2, zh2 = f(y, c, zl, x, zh)
        pairs.append((((y * 2 + c) * 16 + zl * 4 + x) * 4 + zh, ((y2 * 2 + c2) * 16 + zl2 * 4 + x2) * 4 + zh2))
    return pairs


def send(v, f):
    return lax.ppermute(v, AXES, moves(f))


def to_x(v, d):
    return send(v, lambda y, c, zl, x, zh: (y, c, zl, (x + d) % 4, zh))


def to_y(v, d):
    return send(v, lambda y, c, zl, x, zh: ((y + d) % 4, c, zl, x, zh))


def to_layer(v, d):
    return send(v, lambda y, c, zl, x, zh: (y, c, zl, x, (zh + d) % 4))


def to_core(v):
    return send(v, lambda y, c, zl, x, zh: (y, 1 - c, zl, x, zh))


def mask_kernel(pos_ref, pat_ref, x_ref, first_ref, second_ref):
    q = pos_ref[3]
    for h, o_ref in ((q, first_ref), (1 - q, second_ref)):
        for b in range(o_ref.shape[0] // BS):
            for j in range(x_ref.shape[1] // BS):
                block = 2 * b + h
                keep = pat_ref[j, block].astype(jnp.float32).astype(jnp.bfloat16)
                cols = pl.ds(j * BS, BS)
                o_ref[pl.ds(b * BS, BS), cols] = x_ref[pl.ds(pl.multiple_of(block * BS, BS), BS), cols] * keep


def mask(pos, panel, pattern):
    rows, width = panel.shape
    return pl.pallas_call(
        mask_kernel,
        out_shape=[jax.ShapeDtypeStruct((rows // 2, width), panel.dtype)] * 2,
        in_specs=[pl.BlockSpec(memory_space=pltpu.SMEM)] * 2 + [pl.BlockSpec(memory_space=pltpu.VMEM)],
        out_specs=[pl.BlockSpec(memory_space=pltpu.VMEM)] * 2,
        compiler_params=pltpu.CompilerParams(vmem_limit_bytes=4 << 20),
        name="mask",
    )(pos, pattern, panel)


PANEL = (
    ((0, 0, 0), (0, 0, 1)),
    ((0, 3, 0), (0, 3, 1)),
    ((0, 1, 0), (0, 1, 1)),
    ((0, 2, 0), (0, 2, 1)),
    ((1, 0, 0), (1, 0, 1)),
    ((1, 3, 0), (1, 3, 1)),
    ((1, 1, 0), (1, 1, 1)),
    ((1, 2, 0), (1, 2, 1)),
)
SLAB = (
    (0, 0, 4, 0, 0, 0, 0),
    (1, 0, 4, 1, 0, 0, 0),
    (2, 0, 4, 0, 0, 3, 0),
    (3, 0, 4, 0, 0, 1, 0),
    (4, 0, 4, 1, 0, 3, 0),
    (5, 0, 4, 1, 0, 1, 0),
    (6, 0, 4, 0, 0, 2, 0),
    (6, 4, 4, 1, 0, 2, 0),
    (7, 0, 4, 0, 1, 0, 0),
    (7, 4, 4, 1, 1, 0, 0),
    (7, 8, 4, 0, 1, 3, 0),
    (7, 12, 4, 0, 1, 1, 0),
    (8, 0, 4, 1, 1, 3, 0),
    (8, 4, 4, 1, 1, 1, 0),
    (8, 8, 4, 0, 1, 2, 0),
    (8, 12, 4, 1, 1, 2, 0),
)
NA, NB = 8, 9


def quantize(tiles, o_ref):
    codes = []
    for t, v in enumerate(tiles):
        top = jnp.max(jnp.abs(v), axis=0, keepdims=True)
        code = jnp.ceil(jnp.log2(jnp.maximum(top, TINY)) * STEPS)
        v = jnp.round(v * (jnp.exp2(code * (-1.0 / STEPS)) * LEVELS)).astype(jnp.int32)
        o_ref[pl.ds(t * BS, BS), :] = v.astype(jnp.int16)
        codes.append(code)
    codes = jnp.concatenate(codes * (PAD // len(codes)), axis=0)
    o_ref[pl.ds(len(tiles) * BS, PAD), :] = codes.astype(jnp.int32).astype(jnp.int16)


def scales(v_ref, tiles):
    codes = v_ref[pl.ds(tiles * BS, PAD), :].astype(jnp.int32).astype(jnp.float32)
    return jnp.exp2(codes * (1.0 / STEPS)) * (1.0 / LEVELS)


def values(v_ref, at):
    return v_ref[at, :].astype(jnp.int32).astype(jnp.float32)


def product(chunks, pos_ref, owner_ref, a_refs, b_refs, a_s):
    y, c, p, x, layer = pos_ref[0], pos_ref[1], pos_ref[2], pos_ref[4], pos_ref[5]
    for ref, group in zip(a_refs, PANEL):
        for n, (batch, rel, i) in enumerate(group):
            col = (2 * ((p + batch) % 2) + (c + i) % 2) * 4 + (x + rel) % 4
            for u in range(2):
                block = owner_ref[2 * col + u]
                row = block // 4
                at = ((row + c) % 2) * 16 + ((row // 2 + 4 - y) % 4) * 4 + block % 4
                at = pl.ds(pl.multiple_of(at * BS, BS), BS)
                for k, chunk in enumerate(chunks):
                    rows = pl.ds(pl.multiple_of(((layer + chunk) % 4) * BS, BS), BS)
                    a_s[pl.ds(k * BS, BS), at] = ref[n, rows, pl.ds(u * BS, BS)]
    for g in range(2):
        total = None
        for array, first, blocks, half, core, rel, i in SLAB:
            if half != g:
                continue
            at = pl.ds((core * 16 + rel * 4 + i) * BS, blocks * BS)
            b = b_refs[array][pl.ds(first, blocks)].reshape(blocks * BS, 4 * BS)
            part = jnp.dot(a_s[:, at], b, preferred_element_type=jnp.float32)
            total = part if total is None else total + part
        yield g, total


def far_kernel(pos_ref, owner_ref, *refs):
    a_refs, b_refs, (o_ref, a_s) = refs[:NA], refs[NA:NA + NB], refs[NA + NB:]
    tiles = []
    for g, total in product((2,), pos_ref, owner_ref, a_refs, b_refs, a_s):
        tiles += [total[:, n * BS:(n + 1) * BS] for n in range(4)]
    quantize(tiles, o_ref)


def rest_kernel(pos_ref, owner_ref, *refs):
    a_refs, b_refs, (*o_refs, a_s) = refs[:NA], refs[NA:NA + NB], refs[NA + NB:]
    for g, total in product((0, 1, 3), pos_ref, owner_ref, a_refs, b_refs, a_s):
        for k, o_ref in enumerate(o_refs):
            o_ref[g] = total[k * BS:(k + 1) * BS]


def matmul(kernel, name, chunks, out_shape, pos, owner, a, b):
    depth = 32 * BS
    return pl.pallas_call(
        kernel,
        out_shape=out_shape,
        in_specs=[pl.BlockSpec(memory_space=pltpu.SMEM)] * 2 + [pl.BlockSpec(memory_space=pltpu.VMEM)] * (NA + NB),
        out_specs=[pl.BlockSpec(memory_space=pltpu.VMEM)] * len(out_shape),
        scratch_shapes=[pltpu.VMEM((chunks * BS, depth), jnp.bfloat16)],
        compiler_params=pltpu.CompilerParams(vmem_limit_bytes=24 << 20),
        cost_estimate=pl.CostEstimate(flops=2 * chunks * BS * 8 * BS * depth, bytes_accessed=1 << 20, transcendentals=0),
        name=name,
    )(pos, owner, *a, *b)


def add_kernel(pos_ref, own1_ref, own3_ref, got_ref, o1_ref, o3_ref):
    scale = scales(got_ref, 8)
    for core, own_ref, o_ref in ((0, own1_ref, o1_ref), (1, own3_ref, o3_ref)):
        mine = pos_ref[1] == core
        tiles = []
        for t in range(8):
            got = values(got_ref, pl.ds(t * BS, BS)) * scale[t:t + 1, :]
            tiles.append(own_ref[t // 4, :, pl.ds((t % 4) * BS, BS)] + jnp.where(mine, got, 0.0))
        quantize(tiles, o_ref)


def add(pos, own1, own3, got):
    return pl.pallas_call(
        add_kernel,
        out_shape=[jax.ShapeDtypeStruct((8 * BS + PAD, BS), jnp.int16)] * 2,
        in_specs=[pl.BlockSpec(memory_space=pltpu.SMEM)] + [pl.BlockSpec(memory_space=pltpu.VMEM)] * 3,
        out_specs=[pl.BlockSpec(memory_space=pltpu.VMEM)] * 2,
        compiler_params=pltpu.CompilerParams(vmem_limit_bytes=8 << 20),
        name="add",
    )(pos, own1, own3, got)


def total_kernel(pos_ref, own_ref, *refs):
    v_refs, o_refs = refs[:2], refs[2:]
    other = (pos_ref[1] + pos_ref[3]) % 2
    found = [scales(v_ref, 8) for v_ref in v_refs]
    for g, o_ref in zip((other, 1 - other), o_refs):
        for n in range(4):
            at = pl.ds(pl.multiple_of((g * 4 + n) * BS, BS), BS)
            total = own_ref[g, :, pl.ds(n * BS, BS)]
            for v_ref, scale in zip(v_refs, found):
                total = total + values(v_ref, at) * jnp.where(g == 0, scale[n:n + 1, :], scale[4 + n:5 + n, :])
            o_ref[:, pl.ds(n * BS, BS)] = total.astype(jnp.bfloat16)


def total(pos, own, v):
    return pl.pallas_call(
        total_kernel,
        out_shape=[jax.ShapeDtypeStruct((BS, 4 * BS), jnp.bfloat16)] * 2,
        in_specs=[pl.BlockSpec(memory_space=pltpu.SMEM)] + [pl.BlockSpec(memory_space=pltpu.VMEM)] * 3,
        out_specs=[pl.BlockSpec(memory_space=pltpu.VMEM)] * 2,
        compiler_params=pltpu.CompilerParams(vmem_limit_bytes=4 << 20),
        name="total",
    )(pos, own, *v)


def place_kernel(pos_ref, pat_ref, first_ref, second_ref, o_ref):
    q = pos_ref[3]
    for b, ref in ((q, first_ref), (1 - q, second_ref)):
        for n in range(4):
            keep = pat_ref[b, n].astype(jnp.float32).astype(jnp.bfloat16)
            cols = pl.ds(n * BS, BS)
            o_ref[pl.ds(pl.multiple_of(b * BS, BS), BS), cols] = ref[:, cols] * keep


def place(pos, pattern, first, second):
    return pl.pallas_call(
        place_kernel,
        out_shape=jax.ShapeDtypeStruct((2 * BS, 4 * BS), jnp.bfloat16),
        in_specs=[pl.BlockSpec(memory_space=pltpu.SMEM)] * 2 + [pl.BlockSpec(memory_space=pltpu.VMEM)] * 2,
        out_specs=pl.BlockSpec(memory_space=pltpu.VMEM),
        compiler_params=pltpu.CompilerParams(vmem_limit_bytes=4 << 20),
        name="place",
    )(pos, pattern, first, second)


def pick_kernel(pos_ref, *refs):
    *in_refs, o_ref = refs
    half = len(in_refs) // 2
    for core, group in ((0, in_refs[:half]), (1, in_refs[half:])):

        @pl.when(pos_ref[1] == core)
        def _():
            done = 0
            for ref in group:
                count = min(ref.shape[0], o_ref.shape[0])
                o_ref[pl.ds(done, count)] = ref[pl.ds(ref.shape[0] - count, count)]
                done += count


def pick(pos, count, *v):
    return pl.pallas_call(
        pick_kernel,
        out_shape=jax.ShapeDtypeStruct((count,) + v[0].shape[1:], v[0].dtype),
        in_specs=[pl.BlockSpec(memory_space=pltpu.SMEM)] + [pl.BlockSpec(memory_space=pltpu.VMEM)] * len(v),
        out_specs=pl.BlockSpec(memory_space=pltpu.VMEM),
        compiler_params=pltpu.CompilerParams(vmem_limit_bytes=8 << 20),
        name="pick",
    )(pos, *v)


def shards(panel, in_pattern, slab, owner, out_pattern):
    row, col = lax.axis_index("row"), lax.axis_index("col")
    zl = col // 4
    pos = jnp.stack([row // 2, row % 2, zl // 2, zl % 2, col % 4, lax.axis_index("layer")])
    cat = lambda *v: jnp.concatenate(v, axis=0)
    own = slab[0]
    first, second = mask(pos, panel[:, 0, :], in_pattern[:, 0, :].T)
    with jax.named_scope("round0"):
        first = send(first, lambda y, c, zl, x, zh: (y, zl % 2, zl - zl % 2 + c, x, zh))
        second = send(second, lambda y, c, zl, x, zh: (y, 1 - zl % 2, zl - zl % 2 + c, x, zh))
        pair = send(own, lambda y, c, zl, x, zh: (y, c, zl ^ 1, x, zh))
        b1p, b1m = to_y(own, 1), to_y(own, -1)
        first, second, pair, b1p, b1m = lax.optimization_barrier((first, second, pair, b1p, b1m))
        near = jnp.stack([first, second])
    with jax.named_scope("round1"):
        far = send(near, lambda y, c, zl, x, zh: (y, c, zl ^ 2, x, zh))
        a1p, a1m = to_x(near, 1), to_x(near, -1)
        b2p, b2m = to_y(pair, 1), to_y(pair, -1)
        a1h = send(pick(pos, 2, a1p, a1m), lambda y, c, zl, x, zh: (y, c, zl, (x + 1 - 2 * c) % 4, zh))
        a1p, late = lax.optimization_barrier((a1p, pair))
        c01 = to_core(cat(own, late, b1p, b1m))
        far, a1p, a1m, a1h, c01, b2p, b2m = lax.optimization_barrier((far, a1p, a1m, a1h, c01, b2p, b2m))
    with jax.named_scope("round2"):
        a2p, a2m = to_x(far, 1), to_x(far, -1)
        b3 = send(pick(pos, 8, b1p, b2p, b1m, b2m), lambda y, c, zl, x, zh: ((y + 1 - 2 * c) % 4, c, zl, x, zh))
        a2p, a2m, b3 = lax.optimization_barrier((a2p, a2m, b3))
    with jax.named_scope("round3"):
        a3 = send(pick(pos, 2, a2p, a2m), lambda y, c, zl, x, zh: (y, c, zl, (x + 1 - 2 * c) % 4, zh))
        c23 = to_core(cat(b2p, b2m, b3))
    a = (near, a1p, a1m, a1h, far, a2p, a2m, a3)
    b = (own, pair, b1p, b1m, b2p, b2m, b3, c01, c23)
    far_shape = [jax.ShapeDtypeStruct((8 * BS + PAD, BS), jnp.int16)]
    rest_shape = [jax.ShapeDtypeStruct((2, BS, 4 * BS), jnp.float32)] * 3
    got, = matmul(far_kernel, "matmul_far", 1, far_shape, pos, owner[0], a, b)
    with jax.named_scope("layer_far"):
        got = send(got, lambda y, c, zl, x, zh: (y, c, zl, x, (zh + 1 - 2 * c) % 4))
    own_part, part1, part3 = matmul(rest_kernel, "matmul_rest", 3, rest_shape, pos, owner[0], a, b)
    part1, part3 = add(pos, part1, part3, got)
    with jax.named_scope("layer_sums"):
        got1, got3 = to_layer(part1, 1), to_layer(part3, -1)
    first, second = total(pos, own_part, (got1, got3))
    with jax.named_scope("product_pair"):
        first = send(first, lambda y, c, zl, x, zh: (y, zl % 2, zl - zl % 2 + c, x, zh))
        second = send(second, lambda y, c, zl, x, zh: (y, zl % 2, zl - zl % 2 + 1 - c, x, zh))
    return place(pos, out_pattern, first, second)


def solution(mesh):
    in_specs = (
        P("row", "layer", "col"),
        P("row", "layer", "col"),
        P("layer", "row", None, "col"),
        P("layer", None),
        P(("row", "layer"), "col"),
    )
    out_specs = P(("row", "layer"), "col")
    return jax.shard_map(shards, mesh=mesh, in_specs=in_specs, out_specs=out_specs, check_vma=False)
```
